128 devices in a mesh: dp: 4 (over x), ctx: 32 (over y, z, core).
Axes of the slice: x: 4, y: 4, z: 4, core: 2. Of those that a mesh axis runs over, the one named last changes fastest.
Arguments:
- queries: bfloat16 [8192, 1024], P('ctx'), may hold values from -12 to 12
- keys: bfloat16 [8192, 128], P('ctx'), may hold values from -5 to 5
- values: bfloat16 [8192, 128], P('ctx'), may hold values from -5 to 5
- out_grad: bfloat16 [8192, 1024], P('ctx'), may hold values from -5 to 5
- segment_ids: int32 [8192], replicated, may hold values from 0 to 3, never falling along the last dimension, each value on 1 to 7168 neighbouring positions
Outputs:
- attn_out: bfloat16 [8192, 1024], P('ctx', 'dp')
- grad_q: bfloat16 [8192, 1024], P('ctx', 'dp')
- grad_k: bfloat16 [8192, 128], P(('dp', 'ctx'))
- grad_v: bfloat16 [8192, 128], P(('dp', 'ctx'))
The draws below stay inside these ranges and needn't reach their ends.
Inputs may be any that keep to these rules, and one draw needn't show every extreme that they name: `segment_ids`: document numbers never fall along the tokens; each document is a run of positions, the longest exactly 7168.
All inputs are finite; a program needn't handle non-finite values.
Results may differ from the reference program's by a relative error of at most 0.04.
Values may be sent and summed in bfloat16 or wider, within the bound.
A program may use at most 64 MiB of HBM per device.

```python
import math
import jax
import jax.numpy as jnp
import numpy as np
from jax import lax

HEAD = 128
GROUP_HEADS = 8
DOCS = 4
SEQ_TOKENS = 8192


def draw_queries(key, part):
    key = jax.random.fold_in(key, 11)
    drawn = jnp.clip(2.5 * jax.random.normal(key, (SEQ_TOKENS, GROUP_HEADS * HEAD), jnp.float32), -12.0, 12.0)
    return drawn.astype(jnp.bfloat16)


def draw_keys(key, part):
    key = jax.random.fold_in(key, 23)
    drawn = jnp.clip(jax.random.normal(key, (SEQ_TOKENS, HEAD), jnp.float32), -5.0, 5.0)
    return drawn.astype(jnp.bfloat16)


def shard_levels(stream_key, extent, pieces, smallest, largest):
    def one(dim, parts):
        draws = jax.random.uniform(jax.random.fold_in(jax.random.fold_in(stream_key, 6), dim), (parts,), jnp.float32, smallest / len(pieces), largest / len(pieces))
        return jnp.repeat(jnp.exp(draws), extent[dim] // parts).reshape((-1,) + (1,) * (len(extent) - dim - 1))

    level = one(*pieces[0])
    for cut in pieces[1:]:
        level = level * one(*cut)
    return level


def length_profile(amount, total, most, skew):
    portions = [(1 << 20) // math.isqrt(standing ** skew) + 1 for standing in range(2, amount + 1)]
    surplus, counts = total - most - (amount - 1), [1] * (amount - 1)
    while surplus > 0:
        movable = [i for i in range(amount - 1) if counts[i] < most]
        mass, left = sum([portions[i] for i in movable]), surplus
        for i in movable:
            extra = min(most - counts[i], max(1, left * portions[i] // mass), surplus)
            counts[i] = counts[i] + extra
            surplus = surplus - extra
    return np.array([most] + counts)


def ragged_sizes(rng, number_of, total, reach, skew):
    if number_of == 2:
        one = jax.random.randint(rng, (), max(1, total - reach), min(reach, total - 1) + 1)
        return jnp.stack([one, total - one])
    sizes = jnp.asarray(length_profile(number_of, total, reach, skew), jnp.int32)
    pairs = (number_of - 1) // 2
    giver, receiver = sizes[1:1 + 2 * pairs:2], sizes[2:2 + 2 * pairs:2]
    slack = jnp.minimum(giver - 1, reach - receiver)
    shifted = jax.random.randint(jax.random.fold_in(rng, 1), (pairs,), 0, 1 << 20) % (slack + 1)
    sizes = sizes.at[1:1 + 2 * pairs:2].set(giver - shifted).at[2:2 + 2 * pairs:2].set(receiver + shifted)
    return sizes[jax.random.permutation(jax.random.fold_in(rng, 2), number_of)]


def gaussian(own_key, dims, spread, reach, pieces=(), kind=jnp.bfloat16):
    values = jax.random.normal(own_key, dims, jnp.float32) * spread
    if len(pieces) > 0:
        values = shard_levels(own_key, dims, pieces, -0.22, 0.18) * values
    return jnp.clip(values, min=-reach, max=reach).astype(kind)


def setup_inputs(seed: int = 0) -> dict:
    streams_of = jax.random.split(jax.random.key(seed), 6)
    queries = draw_queries(jax.random.fold_in(streams_of[5], 71), 0)
    keys = draw_keys(jax.random.fold_in(streams_of[5], 71), 0)
    values = gaussian(streams_of[2], (SEQ_TOKENS, HEAD), 1.0, 5.0, ((0, 32),))
    out_grad = gaussian(streams_of[3], (SEQ_TOKENS, GROUP_HEADS * HEAD), 1.0, 5.0, ((0, 32),))
    segment_ids = jnp.searchsorted(jnp.cumsum(ragged_sizes(streams_of[4], DOCS, SEQ_TOKENS, 7 * SEQ_TOKENS // 8, 2)), jnp.arange(SEQ_TOKENS), side="right").astype(jnp.int32)
    return dict(queries=queries, keys=keys, values=values, out_grad=out_grad, segment_ids=segment_ids)


def to_half(value):
    return lax.optimization_barrier(value.astype(jnp.bfloat16)).astype(jnp.float32)


def reference(queries, keys, values, out_grad, segment_ids):
    seq = keys.shape[0]
    width = keys.shape[1]
    heads = queries.shape[1] // width
    scale = width ** -0.5
    block = math.gcd(256, seq)
    key_pos = jnp.arange(seq, dtype=jnp.int32)
    key_f = keys.astype(jnp.float32)
    val_f = values.astype(jnp.float32)

    def one_block(carry, index):
        grad_keys, grad_vals = carry
        start = (index * block).astype(jnp.int32)
        query_b = lax.dynamic_slice_in_dim(queries, start, block, 0).astype(jnp.float32)
        query_h = query_b.reshape(block, heads, width).transpose(1, 0, 2)
        grad_b = lax.dynamic_slice_in_dim(out_grad, start, block, 0).astype(jnp.float32)
        grad_h = grad_b.reshape(block, heads, width).transpose(1, 0, 2)
        query_pos = start + jnp.arange(block, dtype=jnp.int32)
        seg_q = lax.dynamic_slice_in_dim(segment_ids, start, block, 0)
        allowed = (seg_q[:, None] == segment_ids[None, :]) & (key_pos[None, :] <= query_pos[:, None])
        scores = jnp.einsum('hqd,kd->hqk', query_h, key_f) * scale
        scores = jnp.where(allowed[None], scores, -jnp.inf)
        rowmax = jnp.max(scores, axis=-1)
        expd = jnp.exp(scores - rowmax[..., None])
        total = jnp.sum(expd, axis=-1)
        weights = to_half(expd)
        output = jnp.einsum('hqk,kd->hqd', weights, val_f) / total[..., None]
        output_bf = output.astype(jnp.bfloat16)
        delta = jnp.sum(grad_h * output_bf.astype(jnp.float32), axis=-1)
        lse = rowmax + jnp.log(total)
        probs = jnp.exp(scores - lse[..., None])
        probs_bf = to_half(probs)
        grad_vals = grad_vals + jnp.einsum('hqk,hqd->kd', probs_bf, grad_h)
        dprobs = jnp.einsum('hqd,kd->hqk', grad_h, val_f)
        dscores = to_half(probs * (dprobs - delta[..., None]))
        grad_query = jnp.einsum('hqk,kd->hqd', dscores, key_f) * scale
        grad_keys = grad_keys + jnp.einsum('hqk,hqd->kd', dscores, query_h) * scale
        out_rows = output_bf.transpose(1, 0, 2).reshape(block, heads * width)
        gq_rows = grad_query.astype(jnp.bfloat16).transpose(1, 0, 2).reshape(block, heads * width)
        return (grad_keys, grad_vals), (out_rows, gq_rows)

    zeros = jnp.zeros((seq, width), jnp.float32)
    (grad_keys, grad_vals), (out_rows, gq_rows) = lax.scan(
        one_block, (zeros, zeros), jnp.arange(seq // block, dtype=jnp.int32))
    attn_out = out_rows.reshape(seq, heads * width)
    grad_q = gq_rows.reshape(seq, heads * width)
    return attn_out, grad_q, grad_keys.astype(jnp.bfloat16), grad_vals.astype(jnp.bfloat16)
```

```python
import math

import jax
import jax.numpy as jnp
from jax import lax
from jax.experimental import pallas as pl
from jax.experimental.pallas import tpu as pltpu
from jax.sharding import PartitionSpec as P

F32 = jnp.float32
BF16 = jnp.bfloat16
MESH = pl.DeviceIdType.MESH

N = 4
ROWS = 256
BLOCKS = 32
WIDTH = 128
SEQ = ROWS * BLOCKS
TILE = 512
TILES = 17
NEG = -1e30
PIECES = (
    (0, 0, 48, "xyz"),
    (1, 0, 48, "yzx"),
    (0, 48, 16, "zxy"),
    (1, 48, 16, "zxy"),
)


def dot(a, b):
    return lax.dot_general(a, b, (((1,), (0,)), ((), ())), preferred_element_type=F32)


def kernel(
    seg_ref, q_hbm, k_ref, v_ref, g_hbm,
    out_ref, dq_ref, dk_ref, dv_ref,
    kall, vall, qbuf, gbuf, s_buf, e_buf,
    qa, gpa, gp, mx, tot, o_t, dq_t, rng, dkv, part, sib, comb,
    r1a, r1b, r1c, r1d, r2a, r2b, r2c, r2d, r3a, r3b, r3c, r3d, d2a, d2b, d2c, d2d, d3a, d3b, d3c, d3d,
    obuf, orecv,
    load_sem, ag_send, ag_recv, pair_send, pair_recv, out_send, out_recv, sib_send, sib_recv, rs_send, rs_recv,
):
    p = lax.axis_index("dp")
    c = lax.axis_index("ctx")
    core = c % 2
    z = (c // 2) % N
    y = c // (2 * N)
    at = dict(x=p, y=y, z=z)

    def index(y_, z_, core_):
        return (y_ * N + z_) * 2 + core_

    def peer(axis, d):
        there = dict(at)
        there[axis] = (at[axis] + d) % N
        return (there["x"], index(there["y"], there["z"], core))

    sibling = (p, index(y, z, 1 - core))
    partner = (p, BLOCKS - 1 - c)
    upper = (c >= BLOCKS // 2).astype(jnp.int32)
    own_unit = 1 - upper
    lo = jnp.minimum(c, BLOCKS - 1 - c)
    hi = BLOCKS - 1 - lo
    n_hi = (hi + 2) // 2

    barrier = pltpu.get_barrier_semaphore()
    friends = [peer(a, d) for a in "xyz" for d in (1, 2, 3)] + [sibling, partner]
    for there in friends:
        pl.semaphore_signal(barrier, inc=1, device_id=there, device_id_type=MESH)
    my_head = 2 * p + upper
    pair_head = 2 * p + 1 - upper

    def head_cols(head):
        return pl.ds(pl.multiple_of(head * WIDTH, WIDTH), WIDTH)

    loads = [
        pltpu.make_async_copy(src.at[:, head_cols(my_head)], buf.at[own_unit], load_sem.at[i])
        for i, (src, buf) in enumerate(((q_hbm, qbuf), (g_hbm, gbuf)))
    ]
    for copy in loads:
        copy.start()
    kall[c] = k_ref[...]
    vall[c] = v_ref[...]
    pl.semaphore_wait(barrier, len(friends))

    def remote(src, dst, send, recv, there):
        return pltpu.make_async_remote_copy(
            src_ref=src, dst_ref=dst, send_sem=send, recv_sem=recv, device_id=there, device_id_type=MESH
        )

    pair_copies = [
        remote(src.at[:, head_cols(pair_head)], buf.at[own_unit], pair_send.at[i], pair_recv.at[i], partner)
        for i, (src, buf) in enumerate(((q_hbm, qbuf), (g_hbm, gbuf)))
    ]

    started = []
    count = [0, 0]

    def push(which, block, there):
        buf = (kall, vall)[which]
        copy = remote(
            buf.at[block], buf.at[block], ag_send.at[which, count[which]], ag_recv.at[which, block], there
        )
        count[which] += 1
        copy.start()
        started.append(copy)

    def arrived(which, block):
        buf = (kall, vall)[which]
        remote(
            buf.at[block], buf.at[block], ag_send.at[which, 0], ag_recv.at[which, block], sibling
        ).wait_recv()

    first, second = ("y", "z"), ("z", "y")
    for d in (1, 3, 2):
        for which in (0, 1):
            push(which, c, peer(first[which], d))
    for which in (0, 1):
        push(which, c, sibling)
    for copy in pair_copies:
        copy.start()
    for d in (1, 3, 2):
        for which in (0, 1):
            push(which, c, peer(second[which], d))
    from_y = lambda d: index((y - d) % N, z, core)
    from_z = lambda d: index(y, (z - d) % N, core)
    for d in (1, 3, 2):
        for which in (0, 1):
            block = from_y(d) if which == 0 else from_z(d)
            arrived(which, block)
            for d2 in (1, 3, 2):
                push(which, block, peer(second[which], d2))
            push(which, block, sibling)
    for d in (1, 3, 2):
        for d2 in (0, 1, 3, 2):
            for which in (0, 1):
                if which == 0:
                    block = index((y - d2) % N, (z - d) % N, core)
                else:
                    block = index((y - d) % N, (z - d2) % N, core)
                arrived(which, block)
                push(which, block, sibling)
    for dy in range(N):
        for dz in range(N):
            for which in (0, 1):
                arrived(which, index((y + dy) % N, (z + dz) % N, 1 - core))
    for copy in loads:
        copy.wait()
    for copy in pair_copies:
        copy.wait_recv()

    scale = WIDTH**-0.5
    seg = seg_ref[...]
    starts = [
        jnp.sum((seg < doc).astype(jnp.int32), axis=(0, 1), keepdims=True) for doc in (1, 2, 3)
    ]
    lane = lax.broadcasted_iota(jnp.int32, (1, WIDTH), 1)
    for unit, block in ((0, hi), (1, lo)):
        for half in range(2):
            ids = seg_ref[pl.ds(2 * block + half, 1), :]
            start = jnp.where(
                ids == 0, 0, jnp.where(ids == 1, starts[0], jnp.where(ids == 2, starts[1], starts[2]))
            )
            rng[unit, 0, :, half * WIDTH : (half + 1) * WIDTH] = start
            rng[unit, 1, :, half * WIDTH : (half + 1) * WIDTH] = block * ROWS + half * WIDTH + lane
        scaled = qbuf[unit].astype(F32).T * (scale * math.log2(math.e))
        high = scaled.astype(BF16)
        qa[unit, :WIDTH] = high
        qa[unit, WIDTH:] = (scaled - high.astype(F32)).astype(BF16)
    mx[...] = jnp.full_like(mx, NEG)
    tot[...] = jnp.zeros_like(tot)
    o_t[...] = jnp.zeros_like(o_t)
    dq_t[...] = jnp.zeros_like(dq_t)

    def zero(i, carry):
        dkv[0, i] = jnp.zeros((ROWS, WIDTH), F32)
        dkv[1, i] = jnp.zeros((ROWS, WIDTH), F32)
        return carry

    lax.fori_loop(0, BLOCKS, zero, 0)

    per = TILE // ROWS
    row = lax.broadcasted_iota(jnp.int32, (TILE, ROWS), 0)

    def place(t):
        unit = (t >= n_hi).astype(jnp.int32)
        return unit, t - unit * n_hi

    def tile_of(buf, kt):
        return buf[pl.ds(kt * per, per)].reshape(TILE, WIDTH)

    def scores_step(t, carry):
        unit, kt = place(t)
        k = tile_of(kall, kt)
        s = dot(jnp.concatenate([k, k], axis=1), qa[unit])
        key = row + kt * TILE
        s = jnp.where((key >= rng[unit, 0]) & (key <= rng[unit, 1]), s, NEG)
        s_buf[t] = s
        mx[unit] = jnp.maximum(mx[unit], jnp.max(s.reshape(TILE // 8, 8, ROWS), axis=0))
        return carry

    lax.fori_loop(0, TILES, scores_step, 0)
    for unit in (0, 1):
        mx[unit] = jnp.broadcast_to(jnp.max(mx[unit], axis=0, keepdims=True), (8, ROWS))

    def weights_step(t, carry):
        unit, kt = place(t)
        e = jnp.exp2(s_buf[t] - mx[unit, 0:1])
        tot[unit] = tot[unit] + jnp.sum(e.reshape(TILE // 8, 8, ROWS), axis=0)
        e = e.astype(BF16)
        e_buf[t] = e
        o_t[unit] = o_t[unit] + dot(tile_of(vall, kt).T, e)
        return carry

    lax.fori_loop(0, TILES, weights_step, 0)
    for unit in (0, 1):
        inv = 1.0 / jnp.sum(tot[unit], axis=0, keepdims=True)
        out_t = o_t[unit] * inv
        obuf[0, unit] = out_t.T.astype(BF16)
        grad = (gbuf[unit].astype(F32).T * inv).astype(BF16)
        grad_f = grad.astype(F32)
        gp[unit] = grad_f.T.astype(BF16)
        delta = -jnp.sum(grad_f * out_t, axis=0, keepdims=True)
        d1 = delta.astype(BF16).astype(F32)
        d2 = (delta - d1).astype(BF16).astype(F32)
        d3 = delta - d1 - d2
        sub = lax.broadcasted_iota(jnp.int32, (WIDTH, ROWS), 0)
        extra = jnp.where(sub == 0, d1, jnp.where(sub == 1, d2, jnp.where(sub == 2, d3, 0.0)))
        gpa[unit, :WIDTH] = grad
        gpa[unit, WIDTH:] = extra.astype(BF16)
    out_copies = [remote(obuf.at[0, 1 - own_unit], orecv.at[0], out_send.at[0], out_recv.at[0], partner)]
    out_copies[0].start()

    ones = jnp.ones((TILE, WIDTH), BF16)

    def grads_step(t, carry):
        unit, kt = place(t)
        e = e_buf[t]
        k = tile_of(kall, kt)
        dp = dot(jnp.concatenate([tile_of(vall, kt), ones], axis=1), gpa[unit])
        ds = (e.astype(F32) * dp).astype(BF16)
        at_ = pl.ds(kt * per, per)
        dkv[1, at_] = dkv[1, at_] + dot(e, gp[unit]).reshape(per, ROWS, WIDTH)
        dkv[0, at_] = dkv[0, at_] + dot(ds, qbuf[unit]).reshape(per, ROWS, WIDTH)
        dq_t[unit] = dq_t[unit] + dot(k.T, ds)
        return carry

    lax.fori_loop(0, TILES, grads_step, 0)
    for unit in (0, 1):
        obuf[1, unit] = (dq_t[unit] * scale).T.astype(BF16)
    out_copies.append(remote(obuf.at[1, 1 - own_unit], orecv.at[1], out_send.at[1], out_recv.at[1], partner))
    out_copies[1].start()

    def to_half(i, carry):
        both = dkv[:, i].reshape(2, 2, 2, 64, WIDTH)
        for which, factor in ((0, scale), (1, 1.0)):
            part[which, pl.ds(2 * i, 2)] = (both[which] * factor).astype(BF16)
        return carry

    lax.fori_loop(0, BLOCKS, to_half, 0)
    sib_copies = [
        remote(part.at[i, :, 1 - core], sib.at[i], sib_send.at[i], sib_recv.at[i], sibling) for i in (0, 1)
    ]
    for copy in sib_copies:
        copy.start()
    for copy in sib_copies:
        copy.wait_recv()

    def add_core(i, carry):
        for which in (0, 1):
            total = part[which, i, core].astype(F32) + sib[which, i].astype(F32)
            comb[which, i // 16, (i // 4) % 4, i % 4] = total.astype(BF16)
        return carry

    lax.fori_loop(0, 64, add_core, 0)

    def cut(ref, axes, axis, i, rows=None):
        return ref.at[tuple(i if a == axis else slice(None) for a in axes) + ((rows, slice(None)) if rows else ())]

    recvs = ((r1a, r2a, r3a), (r1b, r2b, r3b), (r1c, r2c, r3c), (r1d, r2d, r3d))
    sums = ((d2a, d3a), (d2b, d3b), (d2c, d3c), (d2d, d3d))
    rs_copies = {}

    def launch(i, phase, src, axes, rows=None):
        axis = PIECES[i][3][phase]
        for d in (1, 3, 2):
            copy = remote(
                cut(src, axes, axis, (at[axis] + d) % N, rows), recvs[i][phase].at[d - 1],
                rs_send.at[i, phase, d - 1], rs_recv.at[i, phase, d - 1], peer(axis, d),
            )
            copy.start()
            rs_copies[i, phase, d] = copy

    def settle(i, phase):
        for d in (1, 3, 2):
            rs_copies[i, phase, d].wait_recv()

    order = (0, 1, 2, 3)
    for i in order:
        which, first_row, n, axes = PIECES[i]
        launch(i, 0, comb.at[which], "xyz", slice(first_row, first_row + n))
    for i in order:
        which, first_row, n, axes = PIECES[i]
        settle(i, 0)
        left = [a for a in "xyz" if a != axes[0]]

        def add_first(j, carry, i=i, which=which, first_row=first_row, n=n, axes=axes, left=left):
            spot = dict(zip(left, (j // N, j % N)))
            spot[axes[0]] = at[axes[0]]
            total = comb[which, spot["x"], spot["y"], spot["z"], first_row : first_row + n].astype(F32)
            for d in range(N - 1):
                total = total + recvs[i][0][d, j // N, j % N].astype(F32)
            sums[i][0][j // N, j % N] = total.astype(BF16)
            return carry

        lax.fori_loop(0, N * N, add_first, 0)
        launch(i, 1, sums[i][0], left)
    for i in order:
        which, first_row, n, axes = PIECES[i]
        settle(i, 1)
        left = [a for a in "xyz" if a != axes[0]]
        for j in range(N):
            spot = {axes[1]: at[axes[1]], axes[2]: j}
            total = sums[i][0][spot[left[0]], spot[left[1]]].astype(F32)
            for d in range(N - 1):
                total = total + recvs[i][1][d, j].astype(F32)
            sums[i][1][j] = total.astype(BF16)
        launch(i, 2, sums[i][1], axes[2])
    for i in order:
        which, first_row, n, axes = PIECES[i]
        settle(i, 2)
        total = sums[i][1][at[axes[2]]].astype(F32)
        for d in range(N - 1):
            total = total + recvs[i][2][d].astype(F32)
        (dk_ref, dv_ref)[which][first_row : first_row + n] = total.astype(BF16)

    mine = pl.ds(pl.multiple_of(upper * WIDTH, WIDTH), WIDTH)
    other = pl.ds(pl.multiple_of((1 - upper) * WIDTH, WIDTH), WIDTH)
    for i, ref in enumerate((out_ref, dq_ref)):
        ref[:, mine] = obuf[i, own_unit]
        out_copies[i].wait_recv()
        ref[:, other] = orecv[i]
    for copy in started + pair_copies + out_copies + sib_copies + list(rs_copies.values()):
        copy.wait_send()


def on_device(queries, keys, values, out_grad, segment_ids):
    vmem = pl.BlockSpec(memory_space=pltpu.VMEM)
    hbm = pl.BlockSpec(memory_space=pl.ANY)
    dma = pltpu.SemaphoreType.DMA
    sizes = [n for _, _, n, _ in PIECES]
    scratch = [
        pltpu.VMEM((BLOCKS, ROWS, WIDTH), BF16),
        pltpu.VMEM((BLOCKS, ROWS, WIDTH), BF16),
        pltpu.VMEM((2, ROWS, WIDTH), BF16),
        pltpu.VMEM((2, ROWS, WIDTH), BF16),
        pltpu.VMEM((TILES, TILE, ROWS), F32),
        pltpu.VMEM((TILES, TILE, ROWS), BF16),
        pltpu.VMEM((2, 2 * WIDTH, ROWS), BF16),
        pltpu.VMEM((2, 2 * WIDTH, ROWS), BF16),
        pltpu.VMEM((2, ROWS, WIDTH), BF16),
        pltpu.VMEM((2, 8, ROWS), F32),
        pltpu.VMEM((2, 8, ROWS), F32),
        pltpu.VMEM((2, WIDTH, ROWS), F32),
        pltpu.VMEM((2, WIDTH, ROWS), F32),
        pltpu.VMEM((2, 2, 1, ROWS), jnp.int32),
        pltpu.VMEM((2, BLOCKS, ROWS, WIDTH), F32),
        pltpu.VMEM((2, 64, 2, 64, WIDTH), BF16),
        pltpu.VMEM((2, 64, 64, WIDTH), BF16),
        pltpu.VMEM((2, N, N, N, 64, WIDTH), BF16),
    ]
    scratch += [pltpu.VMEM((N - 1, N, N, n, WIDTH), BF16) for n in sizes]
    scratch += [pltpu.VMEM((N - 1, N, n, WIDTH), BF16) for n in sizes]
    scratch += [pltpu.VMEM((N - 1, n, WIDTH), BF16) for n in sizes]
    scratch += [pltpu.VMEM((N, N, n, WIDTH), BF16) for n in sizes]
    scratch += [pltpu.VMEM((N, n, WIDTH), BF16) for n in sizes]
    scratch += [
        pltpu.VMEM((2, 2, ROWS, WIDTH), BF16),
        pltpu.VMEM((2, ROWS, WIDTH), BF16),
        dma((2,)),
        dma((2, BLOCKS)),
        dma((2, BLOCKS)),
        dma((2,)), dma((2,)),
        dma((2,)), dma((2,)),
        dma((2,)), dma((2,)),
        dma((4, 3, 3)), dma((4, 3, 3)),
    ]
    tokens = jax.ShapeDtypeStruct((ROWS, 2 * WIDTH), BF16)
    terms = jax.ShapeDtypeStruct((64, WIDTH), BF16)
    return pl.pallas_call(
        kernel,
        out_shape=(tokens, tokens, terms, terms),
        in_specs=[vmem, hbm, vmem, vmem, hbm],
        out_specs=(vmem, vmem, vmem, vmem),
        scratch_shapes=scratch,
        compiler_params=pltpu.CompilerParams(
            collective_id=0, has_side_effects=True, vmem_limit_bytes=56 * 1024 * 1024
        ),
    )(segment_ids.reshape(SEQ // WIDTH, WIDTH), queries, keys, values, out_grad)


def solution(mesh):
    return jax.shard_map(
        on_device,
        mesh=mesh,
        in_specs=(P("ctx", None), P("ctx", None), P("ctx", None), P("ctx", None), P()),
        out_specs=(P("ctx", "dp"), P("ctx", "dp"), P(("dp", "ctx"), None), P(("dp", "ctx"), None)),
        check_vma=False,
    )
```

```python
import math

import jax
import jax.numpy as jnp
from jax import lax
from jax.experimental import pallas as pl
from jax.experimental.pallas import tpu as pltpu
from jax.sharding import PartitionSpec as P

F32 = jnp.float32
BF16 = jnp.bfloat16
MESH = pl.DeviceIdType.MESH

N = 4
CHIPS = N * N
ROWS = 256
PAIR = 2 * ROWS
WIDTH = 128
SEQ = PAIR * CHIPS
GROUP = 64
TILES = CHIPS + 1
NEG = -1e30


def dot(a, b):
    return lax.dot_general(a, b, (((1,), (0,)), ((), ())), preferred_element_type=F32)


def kernel(
    seg_hbm, q_hbm, k_hbm, v_hbm, g_hbm,
    out_hbm, dq_hbm, dk_hbm, dv_hbm,
    seg_ref, kall, vall, qbuf, gbuf, s_buf, e_buf,
    qa, gt, gpa, gp, mx, tot, o_t, dq_t, o_x, dq_x, st, st_x, rng, dkv,
    part, r1, d2, r2, d3, r3, final, obuf, orecv,
    load_sem, ag_send, ag_recv, q_send, q_recv, st_send, st_recv, mix_send, mix_recv, out_send, out_recv,
    rs_send, rs_recv, store_sem,
):
    p = lax.axis_index("dp")
    c = lax.axis_index("ctx")
    core = c % 2
    z = (c // 2) % N
    y = c // (2 * N)
    chip = c // 2
    at = dict(x=p, y=y, z=z)

    def peer(axis, d):
        there = dict(at)
        there[axis] = (at[axis] + d) % N
        return (there["x"], (there["y"] * N + there["z"]) * 2 + core)

    def chip_at(dy, dz):
        return ((y + N - dy) % N) * N + (z + N - dz) % N

    sibling = (p, 2 * chip + 1 - core)
    partner = (p, 2 * (CHIPS - 1 - chip) + core)
    upper = (chip >= CHIPS // 2).astype(jnp.int32)
    own = 1 - upper
    lo = jnp.minimum(chip, CHIPS - 1 - chip)
    hi = CHIPS - 1 - lo
    my_head = 2 * p + upper
    pair_head = 2 * p + 1 - upper

    def head_cols(head):
        return pl.ds(pl.multiple_of(head * WIDTH, WIDTH), WIDTH)

    barrier = pltpu.get_barrier_semaphore()
    friends = [peer(a, d) for a in "xyz" for d in (1, 2, 3)] + [sibling, partner]
    for there in friends:
        pl.semaphore_signal(barrier, inc=1, device_id=there, device_id_type=MESH)
    loads = [
        pltpu.make_async_copy(src, dst, load_sem.at[i])
        for i, (src, dst) in enumerate(
            (
                (k_hbm.at[:, core], kall.at[chip, core]),
                (v_hbm.at[:, core], vall.at[chip, core]),
                (q_hbm.at[:, head_cols(my_head)], qbuf.at[own, core]),
                (g_hbm.at[:, head_cols(my_head)], gbuf.at[own, core]),
                (seg_hbm, seg_ref),
            )
        )
    ]
    for copy in loads:
        copy.start()

    started = []

    def remote(src, dst, send, recv, there):
        return pltpu.make_async_remote_copy(
            src_ref=src, dst_ref=dst, send_sem=send, recv_sem=recv, device_id=there, device_id_type=MESH
        )

    def go(copy):
        copy.start()
        started.append(copy)
        return copy

    count = [0, 0]
    whole = (kall, vall)

    def next_send(which):
        count[which] += 1
        return ag_send.at[which, count[which] - 1]

    def push(which, block, part_of, there):
        spot = whole[which].at[block, part_of]
        go(remote(spot, spot, next_send(which), ag_recv.at[which, block, part_of], there))

    def arrived(which, block, part_of):
        spot = whole[which].at[block, part_of]
        remote(spot, spot, ag_send.at[which, 0], ag_recv.at[which, block, part_of], sibling).wait_recv()

    def push_mine(which):
        for axis in "yz":
            for d in (1, 3, 2):
                push(which, chip, core, peer(axis, d))

    def push_siblings(which):
        arrived(which, chip, 1 - core)
        for axis in "zy":
            for d in (1, 3, 2):
                push(which, chip, 1 - core, peer(axis, d))

    def relay(which):
        for d in (1, 3, 2):
            block = chip_at(d, 0)
            arrived(which, block, core)
            for d2 in (1, 3, 2):
                push(which, block, core, peer("z", d2))
            block = chip_at(0, d)
            arrived(which, block, 1 - core)
            for d2 in (1, 3, 2):
                push(which, block, 1 - core, peer("y", d2))

    def share_rows(i):
        src, buf = ((q_hbm, qbuf), (g_hbm, gbuf))[i]
        go(remote(src.at[:, head_cols(pair_head)], buf.at[own, core], q_send.at[i, 0], q_recv.at[i, 0], partner))
        mine = buf.at[own, core]
        loads[2 + i].wait()
        go(remote(mine, mine, q_send.at[i, 1], q_recv.at[i, 1], sibling))

    def pass_rows(i):
        buf = (qbuf, gbuf)[i]
        theirs = buf.at[1 - own, core]
        remote(theirs, theirs, q_send.at[i, 0], q_recv.at[i, 0], partner).wait_recv()
        go(remote(theirs, theirs, q_send.at[i, 2], q_recv.at[i, 2], sibling))
        for slot in (1, 2):
            spot = buf.at[own if slot == 1 else 1 - own, 1 - core]
            remote(spot, spot, q_send.at[i, slot], q_recv.at[i, slot], sibling).wait_recv()

    pl.semaphore_wait(barrier, len(friends))
    for which, src in ((0, k_hbm), (1, v_hbm)):
        go(
            remote(
                src.at[:, 1 - core], whole[which].at[chip, core],
                next_send(which), ag_recv.at[which, chip, core], sibling,
            )
        )
    loads[0].wait()
    push_mine(0)
    share_rows(0)
    push_siblings(0)
    share_rows(1)
    relay(0)
    loads[1].wait()
    push_mine(1)
    push_siblings(1)

    scale = WIDTH**-0.5
    loads[4].wait()
    seg = seg_ref[...]
    starts = [jnp.sum((seg < doc).astype(jnp.int32), axis=(0, 1), keepdims=True) for doc in (1, 2, 3)]
    lane = lax.broadcasted_iota(jnp.int32, (1, WIDTH), 1)
    for g, block in ((0, hi), (1, lo)):
        for i in range(PAIR // WIDTH):
            ids = seg_ref[pl.ds(block * (PAIR // WIDTH) + i, 1), :]
            start = jnp.where(
                ids == 0, 0, jnp.where(ids == 1, starts[0], jnp.where(ids == 2, starts[1], starts[2]))
            )
            rng[g, 0, :, i * WIDTH : (i + 1) * WIDTH] = start
            rng[g, 1, :, i * WIDTH : (i + 1) * WIDTH] = block * PAIR + i * WIDTH + lane
    mx[...] = jnp.full_like(mx, NEG)
    tot[...] = jnp.zeros_like(tot)
    o_t[...] = jnp.zeros_like(o_t)
    dq_t[...] = jnp.zeros_like(dq_t)
    pass_rows(0)
    for g in (0, 1):
        for r in (0, 1):
            cols = slice(r * ROWS, (r + 1) * ROWS)
            scaled = qbuf[g, r].astype(F32).T * (scale * math.log2(math.e))
            high = scaled.astype(BF16)
            qa[g, :WIDTH, cols] = high
            qa[g, WIDTH:, cols] = (scaled - high.astype(F32)).astype(BF16)

    row = lax.broadcasted_iota(jnp.int32, (ROWS, PAIR), 0)
    token = row + GROUP * (row // GROUP) + GROUP * core

    def slot_of(g, j):
        return j + g * (hi + 1)

    def rows_of(buf, j):
        return buf[j].reshape(ROWS, WIDTH)

    def fold(op, values):
        return op(values.reshape(ROWS // 8, 8, PAIR), axis=0)

    def scores_step(g, j):
        k = rows_of(kall, j)
        s = dot(jnp.concatenate([k, k], axis=1), qa[g])
        key = token + j * PAIR
        s = jnp.where((key >= rng[g, 0]) & (key <= rng[g, 1]), s, NEG)
        s_buf[slot_of(g, j)] = s
        mx[g] = jnp.maximum(mx[g], fold(jnp.max, s))

    def weights_step(g, j):
        t = slot_of(g, j)
        e = jnp.exp2(s_buf[t] - mx[g, 0:1])
        tot[g] = tot[g] + fold(jnp.sum, e)
        e = e.astype(BF16)
        e_buf[t] = e
        o = dot(rows_of(vall, j).T, e)
        for r in (0, 1):
            o_t[g, r] = o_t[g, r] + o[:, r * ROWS : (r + 1) * ROWS]

    def both_groups(step, j):
        for g, last in ((0, hi), (1, lo)):

            @pl.when(j <= last)
            def _(g=g):
                step(g, j)

    def over_row(which, step):
        both_groups(step, chip)

        def one(dz, carry):
            j = chip_at(0, dz)
            arrived(which, j, core)
            both_groups(step, j)
            return carry

        lax.fori_loop(1, N, one, 0)

    def over_rest(which, step):
        def one_row(dy, carry):
            j = chip_at(dy, 0)
            arrived(which, j, 1 - core)
            both_groups(step, j)

            def one(dz, inner):
                j = chip_at(dy, dz)
                arrived(which, j, core)
                arrived(which, j, 1 - core)
                both_groups(step, j)
                return inner

            lax.fori_loop(1, N, one, 0)
            return carry

        lax.fori_loop(1, N, one_row, 0)

    over_row(0, scores_step)
    relay(1)
    over_rest(0, scores_step)

    for g in (0, 1):
        mx[g] = jnp.broadcast_to(jnp.max(mx[g], axis=0, keepdims=True), (8, PAIR))
    pass_rows(1)
    for g in (0, 1):
        for r in (0, 1):
            gt[g, :, r * ROWS : (r + 1) * ROWS] = gbuf[g, r].astype(F32).T
    over_row(1, weights_step)
    over_rest(1, weights_step)

    for g in (0, 1):
        st[g, 0:1] = mx[g, 0:1]
        st[g, 1:2] = jnp.sum(tot[g], axis=0, keepdims=True)
        o = jnp.concatenate([o_t[g, 0], o_t[g, 1]], axis=1)
        st[g, 2:3] = jnp.sum(gt[g] * o, axis=0, keepdims=True)
        st[g, 3:8] = jnp.zeros((5, PAIR), F32)
    go(remote(st, st_x, st_send, st_recv, sibling)).wait_recv()
    sub = lax.broadcasted_iota(jnp.int32, (WIDTH, PAIR), 0)
    for g in (0, 1):
        top = jnp.maximum(st[g, 0:1], st_x[g, 0:1])
        here, there = jnp.exp2(st[g, 0:1] - top), jnp.exp2(st_x[g, 0:1] - top)
        inv = 1.0 / (here * st[g, 1:2] + there * st_x[g, 1:2])
        factor = here * inv
        delta = -(here * st[g, 2:3] + there * st_x[g, 2:3]) * inv * factor
        for r in (0, 1):
            o_t[g, r] = o_t[g, r] * factor[:, r * ROWS : (r + 1) * ROWS]
        grad = gt[g] * factor
        gpa[g, :WIDTH] = grad.astype(BF16)
        gp[g] = grad.T.astype(BF16)
        d1 = delta.astype(BF16).astype(F32)
        d2_ = (delta - d1).astype(BF16).astype(F32)
        extra = jnp.where(sub == 0, d1, jnp.where(sub == 1, d2_, jnp.where(sub == 2, delta - d1 - d2_, 0.0)))
        gpa[g, WIDTH:] = extra.astype(BF16)
    go(remote(o_t.at[:, 1 - core], o_x, mix_send.at[0], mix_recv.at[0], sibling))

    out_copies, stores = [], []

    def finish_rows(i):
        acc, other = ((o_t, o_x), (dq_t, dq_x))[i]
        remote(acc.at[:, core], other, mix_send.at[i], mix_recv.at[i], sibling).wait_recv()
        for g in (0, 1):
            total = acc[g, core] + other[g]
            if i == 1:
                total = total * scale
            obuf[i, g] = total.T.astype(BF16)
        out_copies.append(go(remote(obuf.at[i, 1 - own], orecv.at[i], out_send.at[i], out_recv.at[i], partner)))
        cols = pl.ds(pl.multiple_of(upper * WIDTH, WIDTH), WIDTH)
        store(obuf.at[i, own], (out_hbm, dq_hbm)[i].at[:, cols], i)

    def store(src, dst, i):
        stores.append(pltpu.make_async_copy(src, dst, store_sem.at[i]))
        stores[-1].start()

    def finish_partner_rows(i):
        out_copies[i].wait_recv()
        cols = pl.ds(pl.multiple_of((1 - upper) * WIDTH, WIDTH), WIDTH)
        store(orecv.at[i], (out_hbm, dq_hbm)[i].at[:, cols], 2 + i)

    ones = jnp.ones((ROWS, WIDTH), BF16)

    def grads_step(g, j):
        e = e_buf[slot_of(g, j)]
        k = rows_of(kall, j)
        dp = dot(jnp.concatenate([rows_of(vall, j), ones], axis=1), gpa[g])
        ds = (e.astype(F32) * dp).astype(BF16)
        terms = (dot(ds, qbuf[g].reshape(PAIR, WIDTH)), dot(e, gp[g]))
        for which in (0, 1):
            dkv[which, j] = terms[which] if g == 0 else dkv[which, j] + terms[which]
        dq = dot(k.T, ds)
        for r in (0, 1):
            dq_t[g, r] = dq_t[g, r] + dq[:, r * ROWS : (r + 1) * ROWS]

    rs_copies = {}

    def launch(phase, which, q, axis, src_of, dst_of):
        for d in (1, 3, 2):
            rs_copies[phase, which, q, d] = go(
                remote(
                    src_of((at[axis] + d) % N), dst_of(d - 1),
                    rs_send.at[phase, which, q, d - 1], rs_recv.at[phase, which, q, d - 1], peer(axis, d),
                )
            )

    def settle(phase, which, q):
        for d in (1, 3, 2):
            rs_copies[phase, which, q, d].wait_recv()

    def total_of(first, ref):
        total = first.astype(F32)
        for d in range(N - 1):
            total = total + ref[d].astype(F32)
        return total

    def first_phase(q):
        launch(0, 0, q, "y", lambda i: part.at[0, q, i], lambda s: r1.at[0, q, s])
        launch(0, 1, q, "z", lambda i: part.at[1, q, :, i], lambda s: r1.at[1, q, s])

    def second_phase(q):
        for which, axis in ((0, "z"), (1, "y")):
            settle(0, which, q)
            mine = part[0, q, y] if which == 0 else part[1, q, :, z]
            d2[which, q] = total_of(mine, r1.at[which, q]).astype(BF16)
            launch(1, which, q, axis, lambda i: d2.at[which, q, i], lambda s: r2.at[which, q, s])

    for q in reversed(range(N)):
        first, end = N * q, N * (q + 1)
        hi_end = jnp.clip(hi + 1, first, end)

        def hi_step(j, carry):
            grads_step(0, j)
            return carry

        def zero(j, carry):
            for which in (0, 1):
                dkv[which, j] = jnp.zeros((ROWS, WIDTH), F32)
            return carry

        def lo_step(j, carry):
            grads_step(1, j)
            return carry

        def round_off(j, carry):
            for which, by in ((0, scale), (1, 1.0)):
                part[which, q, j - first] = (dkv[which, j] * by).astype(BF16).reshape(N, GROUP, WIDTH)
            return carry

        lax.fori_loop(first, hi_end, hi_step, 0)
        lax.fori_loop(hi_end, end, zero, 0)
        if q < 2:
            lax.fori_loop(first, jnp.clip(lo + 1, first, end), lo_step, 0)
        lax.fori_loop(first, end, round_off, 0)
        first_phase(q)
        if q == 3:
            finish_rows(0)
        if q < 2:
            second_phase(q + 2)
    go(remote(dq_t.at[:, 1 - core], dq_x, mix_send.at[1], mix_recv.at[1], sibling))
    second_phase(1)
    finish_rows(1)
    second_phase(0)
    finish_partner_rows(0)
    for q in reversed(range(N)):
        for which, mine in ((0, z), (1, y)):
            settle(1, which, q)
            d3[which, q] = total_of(d2[which, q, mine], r2.at[which, q]).astype(BF16)
    for which in (0, 1):
        launch(2, which, 0, "x", lambda i: d3.at[which, i], lambda s: r3.at[which, s])
    finish_partner_rows(1)
    for which in (0, 1):
        settle(2, which, 0)
        final[which] = total_of(d3[which, p], r3.at[which]).astype(BF16)
        store(final.at[which], (dk_hbm, dv_hbm)[which], 4 + which)
    for copy in started:
        copy.wait_send()
    for copy in stores:
        copy.wait()


def on_device(queries, keys, values, out_grad, segment_ids):
    hbm = pl.BlockSpec(memory_space=pl.ANY)
    dma = pltpu.SemaphoreType.DMA
    vmem = pltpu.VMEM
    scratch = [
        vmem((SEQ // WIDTH, WIDTH), jnp.int32),
        vmem((CHIPS, 2, 2, GROUP, WIDTH), BF16),
        vmem((CHIPS, 2, 2, GROUP, WIDTH), BF16),
        vmem((2, 2, ROWS, WIDTH), BF16),
        vmem((2, 2, ROWS, WIDTH), BF16),
        vmem((TILES, ROWS, PAIR), F32),
        vmem((TILES, ROWS, PAIR), BF16),
        vmem((2, 2 * WIDTH, PAIR), BF16),
        vmem((2, WIDTH, PAIR), F32),
        vmem((2, 2 * WIDTH, PAIR), BF16),
        vmem((2, PAIR, WIDTH), BF16),
        vmem((2, 8, PAIR), F32),
        vmem((2, 8, PAIR), F32),
        vmem((2, 2, WIDTH, ROWS), F32),
        vmem((2, 2, WIDTH, ROWS), F32),
        vmem((2, WIDTH, ROWS), F32),
        vmem((2, WIDTH, ROWS), F32),
        vmem((2, 8, PAIR), F32),
        vmem((2, 8, PAIR), F32),
        vmem((2, 2, 1, PAIR), jnp.int32),
        vmem((2, CHIPS, ROWS, WIDTH), F32),
        vmem((2, N, N, N, GROUP, WIDTH), BF16),
        vmem((2, N, N - 1, N, GROUP, WIDTH), BF16),
        vmem((2, N, N, GROUP, WIDTH), BF16),
        vmem((2, N, N - 1, GROUP, WIDTH), BF16),
        vmem((2, N, GROUP, WIDTH), BF16),
        vmem((2, N - 1, GROUP, WIDTH), BF16),
        vmem((2, GROUP, WIDTH), BF16),
        vmem((2, 2, ROWS, WIDTH), BF16),
        vmem((2, ROWS, WIDTH), BF16),
        dma((5,)),
        dma((2, 32)),
        dma((2, CHIPS, 2)),
        dma((2, 3)),
        dma((2, 3)),
        dma,
        dma,
        dma((2,)),
        dma((2,)),
        dma((2,)),
        dma((2,)),
        dma((3, 2, N, N - 1)),
        dma((3, 2, N, N - 1)),
        dma((6,)),
    ]
    tokens = jax.ShapeDtypeStruct((ROWS, 2 * WIDTH), BF16)
    terms = jax.ShapeDtypeStruct((GROUP, WIDTH), BF16)
    return pl.pallas_call(
        kernel,
        out_shape=(tokens, tokens, terms, terms),
        in_specs=[hbm] * 5,
        out_specs=(hbm,) * 4,
        scratch_shapes=scratch,
        compiler_params=pltpu.CompilerParams(
            collective_id=0, has_side_effects=True, vmem_limit_bytes=56 * 1024 * 1024
        ),
    )(
        segment_ids.reshape(SEQ // WIDTH, WIDTH),
        queries,
        keys.reshape(2, 2, GROUP, WIDTH),
        values.reshape(2, 2, GROUP, WIDTH),
        out_grad,
    )


def solution(mesh):
    return jax.shard_map(
        on_device,
        mesh=mesh,
        in_specs=(P("ctx", None), P("ctx", None), P("ctx", None), P("ctx", None), P()),
        out_specs=(P("ctx", "dp"), P("ctx", "dp"), P(("dp", "ctx"), None), P(("dp", "ctx"), None)),
        check_vma=False,
    )
```

```python
import math

import jax
import jax.numpy as jnp
from jax import lax
from jax.experimental import pallas as pl
from jax.experimental.pallas import tpu as pltpu
from jax.sharding import PartitionSpec as P

F32 = jnp.float32
BF16 = jnp.bfloat16
MESH = pl.DeviceIdType.MESH

N = 4
CHIPS = N * N
ROWS = 256
PAIR = 2 * ROWS
WIDTH = 128
SEQ = PAIR * CHIPS
GROUP = 128
HOME = 64
PER = 2
TILE = PER * GROUP
TILES = 9
HEADS = 2
DEVS = 4
NEG = -1e30


def dot(a, b):
    return lax.dot_general(a, b, (((1,), (0,)), ((), ())), preferred_element_type=F32)


def kernel(
    seg_hbm, q_hbm, k_hbm, v_hbm, g_hbm,
    out_hbm, dq_hbm, dk_hbm, dv_hbm,
    seg_ref, kall, vall, qbuf, gbuf, s_buf, e_buf,
    qa, gt, gpa, gp, mx, tot, o_t, dq_t, core_x, xs, xr, st, rng, dkv,
    part, rs, acc, final, obuf, orecv,
    load_sem, kv_sem, ag_send, ag_recv, pair_send, pair_recv, own_send, own_recv, x_send, x_recv, rel_send, rel_recv,
    st_send, st_recv, core_send, core_recv, sum_send, sum_recv, out_send, out_recv, rs_send, rs_recv, store_sem,
):
    p = lax.axis_index("dp")
    c = lax.axis_index("ctx")
    core = c % 2
    chip = c // 2
    z = chip % N
    y = chip // N
    xp = p % 2
    me = 2 * xp + core
    neighbour = p + 1 - 2 * xp
    sibling = (p, 2 * chip + 1 - core)
    partner = (p, 2 * (CHIPS - 1 - chip) + core)
    upper = (chip >= CHIPS // 2).astype(jnp.int32)
    own = 1 - upper
    lo = jnp.minimum(chip, CHIPS - 1 - chip)
    hi = CHIPS - 1 - lo
    n_hi = hi // PER + 1
    n_lo = lo // PER + 1
    n_own = jnp.where(upper == 1, n_hi, n_lo)
    n_other = TILES - n_own

    def beside(core_):
        return (neighbour, 2 * chip + core_)

    def head_of(slot, parity):
        return 2 * (p - xp + slot) + parity

    def plane_chip(n):
        there = ((y + n // N) % N) * N + (z + n % N) % N
        return there, jnp.maximum(there, CHIPS - 1 - there)

    def cols(head):
        return pl.ds(pl.multiple_of(head * WIDTH, WIDTH), WIDTH)

    home_z = 2 * core + xp
    src_x, src_core = z % 2, z // 2
    keeps = home_z == z
    mine = N * p + y

    def is_me(dev):
        return (dev[0] == p) & (dev[1] == c)

    def home_of(block, half):
        return (block // N, ((block % N) * N + home_z) * 2 + half)

    def source(n):
        return (src_x + 2 * (n // CHIPS), 2 * (n % CHIPS) + src_core)

    barrier = pltpu.get_barrier_semaphore()

    def greet(there):
        pl.semaphore_signal(barrier, inc=1, device_id=there, device_id_type=MESH)

    def greet_plane(n, carry):
        greet((p, 2 * plane_chip(n)[0] + core))
        return carry

    def greet_source(n, carry):
        there = source(n)

        @pl.when(jnp.logical_not(is_me(there)))
        def _():
            greet(there)

        return carry

    lax.fori_loop(1, CHIPS, greet_plane, 0)
    greet(beside(core))
    greet(beside(1 - core))
    greet(sibling)
    lax.fori_loop(0, 2 * CHIPS, greet_source, 0)

    kv_loads = [
        pltpu.make_async_copy(src.at[pl.ds(pl.multiple_of(GROUP * xp, GROUP), GROUP)], dst.at[chip], kv_sem.at[i])
        for i, (src, dst) in enumerate(((k_hbm, kall), (v_hbm, vall)))
    ]
    arrays = ((q_hbm, qbuf), (g_hbm, gbuf))
    loads = [
        pltpu.make_async_copy(src.at[:, cols(head_of(i, upper))], buf.at[own, i, core], load_sem.at[a, i])
        for a, (src, buf) in enumerate(arrays)
        for i in range(HEADS)
    ]
    seg_load = pltpu.make_async_copy(seg_hbm, seg_ref, kv_sem.at[2])
    for copy in kv_loads + loads + [seg_load]:
        copy.start()
    started = []

    def remote(src, dst, send, recv, there):
        return pltpu.make_async_remote_copy(
            src_ref=src, dst_ref=dst, send_sem=send, recv_sem=recv, device_id=there, device_id_type=MESH
        )

    def go(copy):
        copy.start()
        started.append(copy)
        return copy

    def block_copy(which, n):
        there, need = plane_chip(n)
        spot = (kall, vall)[which].at[chip]
        copy = remote(spot, spot, ag_send.at[which, n], ag_recv.at[which, chip], (p, 2 * there + core))
        return copy, need >= chip

    def each_block(which, act):
        def one(n, carry):
            copy, needed = block_copy(which, n)
            pl.when(needed)(lambda: act(copy))
            return carry

        lax.fori_loop(1, CHIPS, one, 0)

    def arrived(which, j):
        @pl.when((j != chip) & (j <= hi))
        def _():
            spot = (kall, vall)[which].at[j]
            remote(spot, spot, ag_send.at[which, 0], ag_recv.at[which, j], sibling).wait_recv()

    def pair_copy(a):
        src, buf = arrays[a]
        src = src.at[:, cols(2 * p + 1 - upper)]
        return remote(src, buf.at[own, xp, core], pair_send.at[a], pair_recv.at[a], partner)

    def share_own(a):
        spot = arrays[a][1].at[own, :, core]
        for i in range(HEADS):
            loads[HEADS * a + i].wait()
        go(remote(spot, spot, own_send.at[a], own_recv.at[a], sibling))

    def to_sibling(a, slot):
        spot = arrays[a][1].at[1 - own, slot, core]
        go(remote(spot, spot, rel_send.at[a, slot], rel_recv.at[a, slot], sibling))

    def share_pair(a):
        spot = arrays[a][1].at[1 - own, xp, core]
        remote(spot, spot, pair_send.at[a], pair_recv.at[a], partner).wait_recv()
        go(remote(spot, spot, x_send.at[a], x_recv.at[a], beside(core)))
        to_sibling(a, xp)

    def pass_on(a):
        spot = arrays[a][1].at[1 - own, 1 - xp, core]
        remote(spot, spot, x_send.at[a], x_recv.at[a], sibling).wait_recv()
        to_sibling(a, 1 - xp)

    def from_sibling(a):
        for i in range(HEADS):
            spot = arrays[a][1].at[1 - own, i, 1 - core]
            remote(spot, spot, rel_send.at[a, 0], rel_recv.at[a, i], sibling).wait_recv()

    def own_from_sibling(a):
        spot = arrays[a][1].at[own, :, 1 - core]
        remote(spot, spot, own_send.at[a], own_recv.at[a], sibling).wait_recv()

    pl.semaphore_wait(barrier, CHIPS - 1 + 2 + 1 + 2 * CHIPS - keeps.astype(jnp.int32))
    go(pair_copy(0))
    kv_loads[0].wait()
    each_block(0, lambda copy: copy.start())
    share_own(0)
    go(pair_copy(1))
    kv_loads[1].wait()
    each_block(1, lambda copy: copy.start())
    share_own(1)

    scale = WIDTH**-0.5
    seg_load.wait()
    seg = seg_ref[...]
    starts = [jnp.sum((seg < doc).astype(jnp.int32), axis=(0, 1), keepdims=True) for doc in (1, 2, 3)]
    lane = lax.broadcasted_iota(jnp.int32, (1, WIDTH), 1)
    for g, block in ((0, hi), (1, lo)):
        for i in range(PAIR // WIDTH):
            ids = seg_ref[pl.ds(block * (PAIR // WIDTH) + i, 1), :]
            start = jnp.where(
                ids == 0, 0, jnp.where(ids == 1, starts[0], jnp.where(ids == 2, starts[1], starts[2]))
            )
            rng[g, 0, :, i * WIDTH : (i + 1) * WIDTH] = start
            rng[g, 1, :, i * WIDTH : (i + 1) * WIDTH] = block * PAIR + i * WIDTH + lane
    mx[...] = jnp.full_like(mx, NEG)
    tot[...] = jnp.zeros_like(tot)

    def clear(i, carry):
        for ref in (o_t, dq_t):
            ref[i] = jnp.zeros_like(ref[i])
        return carry

    lax.fori_loop(0, HEADS, clear, 0)

    def clear_block(j, carry):
        for which in (0, 1):
            dkv[which, j] = jnp.zeros((GROUP, WIDTH), F32)
        return carry

    lax.fori_loop(0, CHIPS, clear_block, 0)

    def unused_block(j, carry):
        for ref in (kall, vall):
            ref[j] = jnp.zeros((GROUP, WIDTH), BF16)
        return carry

    lax.fori_loop(hi + 1, CHIPS, unused_block, 0)

    def scale_rows(g):
        def one(i, carry):
            for r in (0, 1):
                at = slice(r * ROWS, (r + 1) * ROWS)
                scaled = qbuf[g, i, r].astype(F32).T * (scale * math.log2(math.e))
                high = scaled.astype(BF16)
                qa[g, i, :WIDTH, at] = high
                qa[g, i, WIDTH:, at] = (scaled - high.astype(F32)).astype(BF16)
            return carry

        lax.fori_loop(0, HEADS, one, 0)

    def turn_grads(g):
        def one(i, carry):
            for r in (0, 1):
                gt[g, i, :, r * ROWS : (r + 1) * ROWS] = gbuf[g, i, r].T
            return carry

        lax.fori_loop(0, HEADS, one, 0)

    row = lax.broadcasted_iota(jnp.int32, (TILE, PAIR), 0)
    token = PAIR * (row // GROUP) + row % GROUP + ROWS * core + GROUP * xp

    def tile_of(ref, b):
        return ref[pl.ds(PER * b, PER)].reshape(TILE, WIDTH)

    def fold(op, values):
        return op(values.reshape(TILE // 8, 8, PAIR), axis=0)

    def scores_step(g, b):
        k = tile_of(kall, b)
        k = jnp.concatenate([k, k], axis=1)
        key = token + b * (PER * PAIR)
        seen = (key >= rng[g, 0]) & (key <= rng[g, 1])

        def one(i, carry):
            s = jnp.where(seen, dot(k, qa[g, i]), NEG)
            s_buf[i, b + g * n_hi] = s
            mx[i, g] = jnp.maximum(mx[i, g], fold(jnp.max, s))
            return carry

        lax.fori_loop(0, HEADS, one, 0)

    share_pair(0)
    own_from_sibling(0)
    scale_rows(own)

    def scores_own(b, carry):
        for j in range(PER):
            arrived(0, PER * b + j)

        @pl.when(b < n_own)
        def _():
            scores_step(own, b)

        return carry

    lax.fori_loop(0, n_hi, scores_own, 0)
    share_pair(1)
    pass_on(0)
    own_from_sibling(1)
    turn_grads(own)
    from_sibling(0)
    scale_rows(1 - own)

    def scores_other(b, carry):
        scores_step(1 - own, b)
        return carry

    lax.fori_loop(0, n_other, scores_other, 0)
    pass_on(1)
    lax.fori_loop(0, CHIPS, lambda j, carry: (arrived(1, j), carry)[1], 0)

    def over_tiles(step):
        def one(t, carry):
            g = (t >= n_hi).astype(jnp.int32)
            step(t, g, t - g * n_hi)
            return carry

        lax.fori_loop(0, TILES, one, 0)

    def statistics(i):
        for g in (0, 1):
            at = 4 * g
            st[i, me, at : at + 1] = mx[i, g, 0:1]
            st[i, me, at + 1 : at + 2] = jnp.sum(tot[i, g], axis=0, keepdims=True)
            o = jnp.concatenate([o_t[i, g, 0], o_t[i, g, 1]], axis=1)
            st[i, me, at + 2 : at + 3] = jnp.sum(gt[g, i].astype(F32) * o, axis=0, keepdims=True)
            st[i, me, at + 3 : at + 4] = jnp.zeros((1, PAIR), F32)
        spot = st.at[i, me]
        for slot, there in enumerate((beside(core), beside(1 - core), sibling)):
            go(remote(spot, spot, st_send.at[i, slot], st_recv.at[i, me], there))

    for n, i in enumerate((xp, 1 - xp)):
        for g in (0, 1):
            mx[i, g] = jnp.broadcast_to(jnp.max(mx[i, g], axis=0, keepdims=True), (8, PAIR))

        def weights_step(t, g, b, i=i):
            e = jnp.exp2(s_buf[i, t] - mx[i, g, 0:1])
            tot[i, g] = tot[i, g] + fold(jnp.sum, e)
            e = e.astype(BF16)
            e_buf[i, t] = e
            o = dot(tile_of(vall, b).T, e)
            for r in (0, 1):
                o_t[i, g, r] = o_t[i, g, r] + o[:, r * ROWS : (r + 1) * ROWS]

        over_tiles(weights_step)
        if n == 0:
            from_sibling(1)
            turn_grads(1 - own)
        statistics(i)

    ones = jnp.ones((TILE, WIDTH), BF16)
    sub = lax.broadcasted_iota(jnp.int32, (WIDTH, PAIR), 0)

    def prepare(i):
        for other in (2 * (1 - xp), 2 * (1 - xp) + 1, 2 * xp + 1 - core):
            spot = st.at[i, other]
            remote(spot, spot, st_send.at[i, 0], st_recv.at[i, other], sibling).wait_recv()
        for g in (0, 1):
            at = 4 * g
            tops = [st[i, s, at : at + 1] for s in range(DEVS)]
            top = jnp.maximum(jnp.maximum(tops[0], tops[1]), jnp.maximum(tops[2], tops[3]))
            total = delta = jnp.zeros((1, PAIR), F32)
            for s in range(DEVS):
                by = jnp.exp2(tops[s] - top)
                total = total + by * st[i, s, at + 1 : at + 2]
                delta = delta + by * st[i, s, at + 2 : at + 3]
            inv = 1.0 / total
            factor = jnp.exp2(st[i, me, at : at + 1] - top) * inv
            delta = -delta * inv * factor
            for r in (0, 1):
                o_t[i, g, r] = o_t[i, g, r] * factor[:, r * ROWS : (r + 1) * ROWS]
            grad = (gt[g, i].astype(F32) * factor).astype(BF16)
            gpa[i, g, :WIDTH] = grad
            gp[i, g] = grad.T
            d1 = delta.astype(BF16).astype(F32)
            d2 = (delta - d1).astype(BF16).astype(F32)
            extra = jnp.where(sub == 0, d1, jnp.where(sub == 1, d2, jnp.where(sub == 2, delta - d1 - d2, 0.0)))
            gpa[i, g, WIDTH:] = extra.astype(BF16)

    parts_of = (o_t, dq_t)

    def to_core(kind, i, g):
        go(
            remote(
                parts_of[kind].at[i, g, 1 - core], core_x.at[kind, i, g],
                core_send.at[kind, i, g], core_recv.at[kind, i, g], sibling,
            )
        )

    def from_core(kind, i, g):
        spot = core_x.at[kind, i, g]
        remote(spot, spot, core_send.at[kind, i, g], core_recv.at[kind, i, g], sibling).wait_recv()
        return parts_of[kind][i, g, core] + core_x[kind, i, g]

    def to_beside(kind, g):
        xs[kind, g] = from_core(kind, 1 - xp, g).astype(BF16)
        go(remote(xs.at[kind, g], xr.at[kind, g], sum_send.at[kind, g], sum_recv.at[kind, g], beside(core)))

    stores = []

    def store(src, dst, i):
        stores.append(pltpu.make_async_copy(src, dst, store_sem.at[i]))
        stores[-1].start()

    def finish(kind, g):
        total = from_core(kind, xp, g)
        spot = xr.at[kind, g]
        remote(spot, spot, sum_send.at[kind, g], sum_recv.at[kind, g], sibling).wait_recv()
        total = total + xr[kind, g].astype(F32)
        if kind == 1:
            total = total * scale
        obuf[kind, g] = total.T.astype(BF16)

    def finish_own(kind):
        finish(kind, own)
        store(obuf.at[kind, own], (out_hbm, dq_hbm)[kind].at[:, cols(upper)], kind)

    def partner_copy(kind):
        return remote(obuf.at[kind, 1 - own], orecv.at[kind], out_send.at[kind], out_recv.at[kind], partner)

    def finish_other(kind):
        finish(kind, 1 - own)
        go(partner_copy(kind))

    def from_partner(kind):
        partner_copy(kind).wait_recv()
        store(orecv.at[kind], (out_hbm, dq_hbm)[kind].at[:, cols(1 - upper)], 2 + kind)

    def grad_copy(block, half):
        there = home_of(block, half)
        copy = remote(
            part.at[block, half], rs.at[me_source], rs_send.at[block, half], rs_recv.at[me_source], there
        )
        return copy, (block <= hi) & jnp.logical_not(is_me(there))

    me_source = (p // 2) * CHIPS + chip

    def each_half(block, act):
        for half in (0, 1):
            copy, needed = grad_copy(block, half)
            pl.when(needed)(lambda copy=copy: act(copy))

    def send_grads(b):
        for block in (PER * b, PER * b + 1):
            for half in (0, 1):
                at = slice(half * HOME, (half + 1) * HOME)
                part[block, half, 0] = (dkv[0, block, at] * scale).astype(BF16)
                part[block, half, 1] = dkv[1, block, at].astype(BF16)
            each_half(block, lambda copy: copy.start())

    def grads_pass(g, i, leave):
        n_tiles = jnp.where(g == 0, n_hi, n_lo)
        turn = (2 * p + y + 2 * z) % n_tiles

        def one(n, carry):
            b = (n + turn) % n_tiles
            e = e_buf[i, b + g * n_hi]
            k = tile_of(kall, b)
            dp = dot(jnp.concatenate([tile_of(vall, b), ones], axis=1), gpa[i, g])
            ds = (e.astype(F32) * dp).astype(BF16)
            at = pl.ds(PER * b, PER)
            dkv[0, at] = dkv[0, at] + dot(ds, qbuf[g, i].reshape(PAIR, WIDTH)).reshape(PER, GROUP, WIDTH)
            dkv[1, at] = dkv[1, at] + dot(e, gp[i, g]).reshape(PER, GROUP, WIDTH)
            dq = dot(k.T, ds)
            for r in (0, 1):
                dq_t[i, g, r] = dq_t[i, g, r] + dq[:, r * ROWS : (r + 1) * ROWS]
            if leave is not None:
                pl.when(leave(b))(lambda: send_grads(b))
            return carry

        lax.fori_loop(0, n_tiles, one, 0)
        to_core(1, i, g)

    prepare(1 - xp)
    for g in (0, 1):
        to_core(0, 1 - xp, g)
    grads_pass(1 - own, 1 - xp, None)
    prepare(xp)
    for g in (0, 1):
        to_core(0, xp, g)
    for g in (0, 1):
        to_beside(0, g)
    grads_pass(1 - own, xp, lambda b: b >= n_own)
    to_beside(1, 1 - own)
    finish_other(0)
    grads_pass(own, 1 - xp, None)
    finish_other(1)
    finish_own(0)
    grads_pass(own, xp, lambda b: b < n_own)
    to_beside(1, own)

    mine_half = core
    acc[...] = jnp.where(keeps & (mine <= hi), part[mine, mine_half].astype(F32), 0.0)

    def add_source(n, carry):
        slot = (me_source + n) % (2 * CHIPS)
        k = slot % CHIPS
        sends = jnp.maximum(k, CHIPS - 1 - k) >= mine

        @pl.when(sends & jnp.logical_not(is_me(source(slot))))
        def _():
            spot = rs.at[slot]
            remote(spot, spot, rs_send.at[0, 0], rs_recv.at[slot], sibling).wait_recv()
            acc[...] = acc[...] + rs[slot].astype(F32)

        return carry

    from_partner(0)
    finish_own(1)
    lax.fori_loop(0, 2 * CHIPS, add_source, 0)
    final[...] = acc[...].astype(BF16)
    store(final.at[0], dk_hbm, 4)
    store(final.at[1], dv_hbm, 5)
    from_partner(1)
    for which in (0, 1):
        each_block(which, lambda copy: copy.wait_send())

    def sent(block, carry):
        each_half(block, lambda copy: copy.wait_send())
        return carry

    lax.fori_loop(0, CHIPS, sent, 0)
    for copy in started:
        copy.wait_send()
    for copy in stores:
        copy.wait()


def on_device(queries, keys, values, out_grad, segment_ids):
    hbm = pl.BlockSpec(memory_space=pl.ANY)
    dma = pltpu.SemaphoreType.DMA
    vmem = pltpu.VMEM
    scratch = [
        vmem((SEQ // WIDTH, WIDTH), jnp.int32),
        vmem((CHIPS, GROUP, WIDTH), BF16),
        vmem((CHIPS, GROUP, WIDTH), BF16),
        vmem((2, HEADS, 2, ROWS, WIDTH), BF16),
        vmem((2, HEADS, 2, ROWS, WIDTH), BF16),
        vmem((HEADS, TILES, TILE, PAIR), F32),
        vmem((HEADS, TILES, TILE, PAIR), BF16),
        vmem((2, HEADS, 2 * WIDTH, PAIR), BF16),
        vmem((2, HEADS, WIDTH, PAIR), BF16),
        vmem((HEADS, 2, 2 * WIDTH, PAIR), BF16),
        vmem((HEADS, 2, PAIR, WIDTH), BF16),
        vmem((HEADS, 2, 8, PAIR), F32),
        vmem((HEADS, 2, 8, PAIR), F32),
        vmem((HEADS, 2, 2, WIDTH, ROWS), F32),
        vmem((HEADS, 2, 2, WIDTH, ROWS), F32),
        vmem((2, HEADS, 2, WIDTH, ROWS), F32),
        vmem((2, 2, WIDTH, ROWS), BF16),
        vmem((2, 2, WIDTH, ROWS), BF16),
        vmem((HEADS, DEVS, 8, PAIR), F32),
        vmem((2, 2, 1, PAIR), jnp.int32),
        vmem((2, CHIPS, GROUP, WIDTH), F32),
        vmem((CHIPS, 2, 2, HOME, WIDTH), BF16),
        vmem((2 * CHIPS, 2, HOME, WIDTH), BF16),
        vmem((2, HOME, WIDTH), F32),
        vmem((2, HOME, WIDTH), BF16),
        vmem((2, 2, ROWS, WIDTH), BF16),
        vmem((2, ROWS, WIDTH), BF16),
        dma((2, HEADS)),
        dma((3,)),
        dma((2, CHIPS)), dma((2, CHIPS)),
        dma((2,)), dma((2,)),
        dma((2,)), dma((2,)),
        dma((2,)), dma((2,)),
        dma((2, HEADS)), dma((2, HEADS)),
        dma((HEADS, 3)), dma((HEADS, DEVS)),
        dma((2, HEADS, 2)), dma((2, HEADS, 2)),
        dma((2, 2)), dma((2, 2)),
        dma((2,)), dma((2,)),
        dma((CHIPS, 2)), dma((2 * CHIPS,)),
        dma((6,)),
    ]
    tokens = jax.ShapeDtypeStruct((ROWS, 2 * WIDTH), BF16)
    terms = jax.ShapeDtypeStruct((HOME, WIDTH), BF16)
    return pl.pallas_call(
        kernel,
        out_shape=(tokens, tokens, terms, terms),
        in_specs=[hbm] * 5,
        out_specs=(hbm,) * 4,
        scratch_shapes=scratch,
        compiler_params=pltpu.CompilerParams(
            collective_id=0, has_side_effects=True, vmem_limit_bytes=56 * 1024 * 1024
        ),
    )(segment_ids.reshape(SEQ // WIDTH, WIDTH), queries, keys, values, out_grad)


def solution(mesh):
    return jax.shard_map(
        on_device,
        mesh=mesh,
        in_specs=(P("ctx", None), P("ctx", None), P("ctx", None), P("ctx", None), P()),
        out_specs=(P("ctx", "dp"), P("ctx", "dp"), P(("dp", "ctx"), None), P(("dp", "ctx"), None)),
        check_vma=False,
    )
```

```python
import math

import jax
import jax.numpy as jnp
from jax import lax
from jax.experimental import pallas as pl
from jax.experimental.pallas import tpu as pltpu
from jax.sharding import PartitionSpec as P

F32 = jnp.float32
BF16 = jnp.bfloat16
MESH = pl.DeviceIdType.MESH

N = 4
CHIPS = N * N
ROWS = 256
PAIR = 2 * ROWS
WIDTH = 128
SEQ = PAIR * CHIPS
GROUP = 128
HOME = 64
PER = 2
TILE = PER * GROUP
TILES = 9
HEADS = 2
DEVS = 4
NEG = -1e30


def dot(a, b):
    return lax.dot_general(a, b, (((1,), (0,)), ((), ())), preferred_element_type=F32)


def kernel(
    seg_hbm, q_hbm, k_hbm, v_hbm, g_hbm,
    out_hbm, dq_hbm, dk_hbm, dv_hbm,
    seg_ref, kall, vall, qbuf, gbuf, s_buf, e_buf,
    qa, gt, gpa, gp, mx, tot, o_t, dq_t, core_x, xs, xr, st, rng, dkv,
    part, r1, d2, r2, d3, r3, acc, sums, final, obuf, orecv,
    load_sem, kv_sem, ag_send, ag_recv, pair_send, pair_recv, own_send, own_recv, x_send, x_recv, rel_send, rel_recv,
    st_send, st_recv, core_send, core_recv, sum_send, sum_recv, out_send, out_recv, r1_send, r1_recv, r2_send, r2_recv, r3_send, r3_recv, store_sem,
):
    p = lax.axis_index("dp")
    c = lax.axis_index("ctx")
    core = c % 2
    chip = c // 2
    z = chip % N
    y = chip // N
    xp = p % 2
    me = 2 * xp + core
    neighbour = p + 1 - 2 * xp
    sibling = (p, 2 * chip + 1 - core)
    partner = (p, 2 * (CHIPS - 1 - chip) + core)
    upper = (chip >= CHIPS // 2).astype(jnp.int32)
    own = 1 - upper
    lo = jnp.minimum(chip, CHIPS - 1 - chip)
    hi = CHIPS - 1 - lo
    n_hi = hi // PER + 1
    n_lo = lo // PER + 1
    n_own = jnp.where(upper == 1, n_hi, n_lo)
    n_other = TILES - n_own

    def beside(core_):
        return (neighbour, 2 * chip + core_)

    def head_of(slot, parity):
        return 2 * (p - xp + slot) + parity

    def along(axis, d):
        there = dict(y=y, z=z)
        there[axis] = (there[axis] + d) % N
        return (p, (there["y"] * N + there["z"]) * 2 + core)

    def chip_at(dy, dz):
        return ((y + N - dy) % N) * N + (z + N - dz) % N

    def upper_of(k):
        return jnp.maximum(k, CHIPS - 1 - k)

    def cols(head):
        return pl.ds(pl.multiple_of(head * WIDTH, WIDTH), WIDTH)

    home_z = 2 * core + xp

    def home(half):
        return (z, (y * N + home_z) * 2 + half)

    def source(u):
        return (z % 2 + 2 * u, (y * N + p) * 2 + z // 2)

    def is_me(dev):
        return (dev[0] == p) & (dev[1] == c)

    keeps = (z == p) & (home_z == z)

    barrier = pltpu.get_barrier_semaphore()

    def greet(there):
        pl.semaphore_signal(barrier, inc=1, device_id=there, device_id_type=MESH)

    for d in range(1, N):
        for axis in "yz":
            greet(along(axis, d))
    for there in (partner, beside(core), beside(1 - core), sibling):
        greet(there)
    for u in (0, 1):
        pl.when(jnp.logical_not(is_me(source(u))))(lambda u=u: greet(source(u)))

    kv_loads = [
        pltpu.make_async_copy(src.at[xp], dst.at[chip], kv_sem.at[i])
        for i, (src, dst) in enumerate(((k_hbm, kall), (v_hbm, vall)))
    ]
    arrays = ((q_hbm, qbuf), (g_hbm, gbuf))
    loads = [
        pltpu.make_async_copy(src.at[:, cols(head_of(i, upper))], buf.at[own, i, core], load_sem.at[a, i])
        for a, (src, buf) in enumerate(arrays)
        for i in range(HEADS)
    ]
    seg_load = pltpu.make_async_copy(seg_hbm, seg_ref, kv_sem.at[2])
    for copy in kv_loads + loads + [seg_load]:
        copy.start()
    started = []

    def remote(src, dst, send, recv, there):
        return pltpu.make_async_remote_copy(
            src_ref=src, dst_ref=dst, send_sem=send, recv_sem=recv, device_id=there, device_id_type=MESH
        )

    def go(copy):
        copy.start()
        started.append(copy)
        return copy

    whole = (kall, vall)
    count = [0, 0]
    key_copies = []

    def push(which, block, half, there):
        spot = whole[which].at[block, half]
        copy = remote(spot, spot, ag_send.at[which, count[which]], ag_recv.at[which, block, half], there)
        count[which] += 1
        if which == 0:
            copy.start()
            key_copies.append(copy)
        else:
            go(copy)

    def arrived(which, block, half):
        spot = whole[which].at[block, half]
        remote(spot, spot, ag_send.at[which, 0], ag_recv.at[which, block, half], sibling).wait_recv()

    def push_mine(which):
        for axes in ("yz", "zy"):
            for d in (1, 3, 2):
                for half in (0, 1):
                    push(which, chip, half, along(axes[half], d))

    def relay(which):
        for d in (1, 3, 2):
            for half, block in ((0, chip_at(d, 0)), (1, chip_at(0, d))):
                arrived(which, block, half)
                for d2 in (1, 3, 2):
                    push(which, block, half, along("zy"[half], d2))

    def tile_in_order(n):
        turn = n // 2
        row_ = (y + jnp.where(turn == 2, 3, jnp.where(turn == 3, 2, turn))) % N
        return 2 * row_ + n % 2

    def tile_arrived(which, b):
        for j in (PER * b, PER * b + 1):
            pl.when(j % N != z)(lambda j=j: arrived(which, j, 0))
            pl.when(j // N != y)(lambda j=j: arrived(which, j, 1))

    def pair_copy(a):
        src, buf = arrays[a]
        src = src.at[:, cols(2 * p + 1 - upper)]
        return remote(src, buf.at[own, xp, core], pair_send.at[a], pair_recv.at[a], partner)

    def share_own(a):
        spot = arrays[a][1].at[own, :, core]
        for i in range(HEADS):
            loads[HEADS * a + i].wait()
        go(remote(spot, spot, own_send.at[a], own_recv.at[a], sibling))

    def to_sibling(a, slot):
        spot = arrays[a][1].at[1 - own, slot, core]
        go(remote(spot, spot, rel_send.at[a, slot], rel_recv.at[a, slot], sibling))

    def share_pair(a):
        spot = arrays[a][1].at[1 - own, xp, core]
        remote(spot, spot, pair_send.at[a], pair_recv.at[a], partner).wait_recv()
        go(remote(spot, spot, x_send.at[a], x_recv.at[a], beside(core)))
        to_sibling(a, xp)

    def pass_on(a):
        spot = arrays[a][1].at[1 - own, 1 - xp, core]
        remote(spot, spot, x_send.at[a], x_recv.at[a], sibling).wait_recv()
        to_sibling(a, 1 - xp)

    def from_sibling(a):
        for i in range(HEADS):
            spot = arrays[a][1].at[1 - own, i, 1 - core]
            remote(spot, spot, rel_send.at[a, 0], rel_recv.at[a, i], sibling).wait_recv()

    def own_from_sibling(a):
        spot = arrays[a][1].at[own, :, 1 - core]
        remote(spot, spot, own_send.at[a], own_recv.at[a], sibling).wait_recv()

    pl.semaphore_wait(barrier, 12 - keeps.astype(jnp.int32))
    go(pair_copy(0))
    kv_loads[0].wait()
    push_mine(0)
    share_own(0)
    go(pair_copy(1))
    relay(0)

    scale = WIDTH**-0.5
    seg_load.wait()
    seg = seg_ref[...]
    starts = [jnp.sum((seg < doc).astype(jnp.int32), axis=(0, 1), keepdims=True) for doc in (1, 2, 3)]
    lane = lax.broadcasted_iota(jnp.int32, (1, WIDTH), 1)
    for g, block in ((0, hi), (1, lo)):
        for i in range(PAIR // WIDTH):
            ids = seg_ref[pl.ds(block * (PAIR // WIDTH) + i, 1), :]
            start = jnp.where(
                ids == 0, 0, jnp.where(ids == 1, starts[0], jnp.where(ids == 2, starts[1], starts[2]))
            )
            rng[g, 0, :, i * WIDTH : (i + 1) * WIDTH] = start
            rng[g, 1, :, i * WIDTH : (i + 1) * WIDTH] = block * PAIR + i * WIDTH + lane
    mx[...] = jnp.full_like(mx, NEG)
    tot[...] = jnp.zeros_like(tot)

    def clear(i, carry):
        for ref in (o_t, dq_t):
            ref[i] = jnp.zeros_like(ref[i])
        return carry

    lax.fori_loop(0, HEADS, clear, 0)

    def clear_block(j, carry):
        for which in (0, 1):
            dkv[which, j] = jnp.zeros((GROUP, WIDTH), F32)
        return carry

    lax.fori_loop(0, CHIPS, clear_block, 0)

    def scale_rows(g):
        def one(i, carry):
            for r in (0, 1):
                at = slice(r * ROWS, (r + 1) * ROWS)
                scaled = qbuf[g, i, r].astype(F32).T * (scale * math.log2(math.e))
                high = scaled.astype(BF16)
                qa[g, i, :WIDTH, at] = high
                qa[g, i, WIDTH:, at] = (scaled - high.astype(F32)).astype(BF16)
            return carry

        lax.fori_loop(0, HEADS, one, 0)

    def turn_grads(g):
        def one(i, carry):
            for r in (0, 1):
                gt[g, i, :, r * ROWS : (r + 1) * ROWS] = gbuf[g, i, r].T
            return carry

        lax.fori_loop(0, HEADS, one, 0)

    row = lax.broadcasted_iota(jnp.int32, (TILE, PAIR), 0)
    token = PAIR * (row // GROUP) + row % GROUP + ROWS * core + GROUP * xp

    def tile_of(ref, b):
        return ref[pl.ds(PER * b, PER)].reshape(TILE, WIDTH)

    def fold(op, values):
        return op(values.reshape(TILE // 8, 8, PAIR), axis=0)

    def scores_step(g, b):
        k = tile_of(kall, b)
        k = jnp.concatenate([k, k], axis=1)
        key = token + b * (PER * PAIR)
        seen = (key >= rng[g, 0]) & (key <= rng[g, 1])

        def one(i, carry):
            s = jnp.where(seen, dot(k, qa[g, i]), NEG)
            s_buf[i, b + g * n_hi] = s
            mx[i, g] = jnp.maximum(mx[i, g], fold(jnp.max, s))
            return carry

        lax.fori_loop(0, HEADS, one, 0)

    share_pair(0)
    own_from_sibling(0)
    scale_rows(own)

    def scores_own(n, carry):
        b = tile_in_order(n)
        tile_arrived(0, b)

        @pl.when(b < n_own)
        def _():
            scores_step(own, b)

        return carry

    lax.fori_loop(0, 2, scores_own, 0)
    for copy in key_copies:
        copy.wait_send()
    kv_loads[1].wait()
    push_mine(1)
    share_own(1)
    pass_on(0)
    lax.fori_loop(2, CHIPS // PER, scores_own, 0)
    relay(1)
    share_pair(1)
    own_from_sibling(1)
    turn_grads(own)
    from_sibling(0)
    scale_rows(1 - own)

    def scores_other(b, carry):
        scores_step(1 - own, b)
        return carry

    lax.fori_loop(0, n_other, scores_other, 0)
    pass_on(1)
    lax.fori_loop(0, CHIPS // PER, lambda n, carry: (tile_arrived(1, tile_in_order(n)), carry)[1], 0)

    def over_tiles(step):
        def one(t, carry):
            g = (t >= n_hi).astype(jnp.int32)
            step(t, g, t - g * n_hi)
            return carry

        lax.fori_loop(0, TILES, one, 0)

    def statistics(i):
        for g in (0, 1):
            at = 4 * g
            st[i, me, at : at + 1] = mx[i, g, 0:1]
            st[i, me, at + 1 : at + 2] = jnp.sum(tot[i, g], axis=0, keepdims=True)
            o = jnp.concatenate([o_t[i, g, 0], o_t[i, g, 1]], axis=1)
            st[i, me, at + 2 : at + 3] = jnp.sum(gt[g, i].astype(F32) * o, axis=0, keepdims=True)
            st[i, me, at + 3 : at + 4] = jnp.zeros((1, PAIR), F32)
        spot = st.at[i, me]
        for slot, there in enumerate((beside(core), beside(1 - core), sibling)):
            go(remote(spot, spot, st_send.at[i, slot], st_recv.at[i, me], there))

    for n, i in enumerate((xp, 1 - xp)):
        for g in (0, 1):
            mx[i, g] = jnp.broadcast_to(jnp.max(mx[i, g], axis=0, keepdims=True), (8, PAIR))

        def weights_step(t, g, b, i=i):
            e = jnp.exp2(s_buf[i, t] - mx[i, g, 0:1])
            tot[i, g] = tot[i, g] + fold(jnp.sum, e)
            e = e.astype(BF16)
            e_buf[i, t] = e
            o = dot(tile_of(vall, b).T, e)
            for r in (0, 1):
                o_t[i, g, r] = o_t[i, g, r] + o[:, r * ROWS : (r + 1) * ROWS]

        over_tiles(weights_step)
        if n == 0:
            from_sibling(1)
            turn_grads(1 - own)
        statistics(i)

    ones = jnp.ones((TILE, WIDTH), BF16)
    sub = lax.broadcasted_iota(jnp.int32, (WIDTH, PAIR), 0)

    def prepare(i):
        for other in (2 * (1 - xp), 2 * (1 - xp) + 1, 2 * xp + 1 - core):
            spot = st.at[i, other]
            remote(spot, spot, st_send.at[i, 0], st_recv.at[i, other], sibling).wait_recv()
        for g in (0, 1):
            at = 4 * g
            tops = [st[i, s, at : at + 1] for s in range(DEVS)]
            top = jnp.maximum(jnp.maximum(tops[0], tops[1]), jnp.maximum(tops[2], tops[3]))
            total = delta = jnp.zeros((1, PAIR), F32)
            for s in range(DEVS):
                by = jnp.exp2(tops[s] - top)
                total = total + by * st[i, s, at + 1 : at + 2]
                delta = delta + by * st[i, s, at + 2 : at + 3]
            inv = 1.0 / total
            factor = jnp.exp2(st[i, me, at : at + 1] - top) * inv
            delta = -delta * inv * factor
            for r in (0, 1):
                o_t[i, g, r] = o_t[i, g, r] * factor[:, r * ROWS : (r + 1) * ROWS]
            grad = (gt[g, i].astype(F32) * factor).astype(BF16)
            gpa[i, g, :WIDTH] = grad
            gp[i, g] = grad.T
            d1 = delta.astype(BF16).astype(F32)
            d2 = (delta - d1).astype(BF16).astype(F32)
            extra = jnp.where(sub == 0, d1, jnp.where(sub == 1, d2, jnp.where(sub == 2, delta - d1 - d2, 0.0)))
            gpa[i, g, WIDTH:] = extra.astype(BF16)

    parts_of = (o_t, dq_t)

    def to_core(kind, i, g):
        go(
            remote(
                parts_of[kind].at[i, g, 1 - core], core_x.at[kind, i, g],
                core_send.at[kind, i, g], core_recv.at[kind, i, g], sibling,
            )
        )

    def from_core(kind, i, g):
        spot = core_x.at[kind, i, g]
        remote(spot, spot, core_send.at[kind, i, g], core_recv.at[kind, i, g], sibling).wait_recv()
        return parts_of[kind][i, g, core] + core_x[kind, i, g]

    def to_beside(kind, g):
        xs[kind, g] = from_core(kind, 1 - xp, g).astype(BF16)
        go(remote(xs.at[kind, g], xr.at[kind, g], sum_send.at[kind, g], sum_recv.at[kind, g], beside(core)))

    stores = []

    def store(src, dst, i):
        stores.append(pltpu.make_async_copy(src, dst, store_sem.at[i]))
        stores[-1].start()

    def finish(kind, g):
        total = from_core(kind, xp, g)
        spot = xr.at[kind, g]
        remote(spot, spot, sum_send.at[kind, g], sum_recv.at[kind, g], sibling).wait_recv()
        total = total + xr[kind, g].astype(F32)
        if kind == 1:
            total = total * scale
        obuf[kind, g] = total.T.astype(BF16)

    def finish_own(kind):
        finish(kind, own)
        store(obuf.at[kind, own], (out_hbm, dq_hbm)[kind].at[:, cols(upper)], kind)

    def partner_copy(kind):
        return remote(obuf.at[kind, 1 - own], orecv.at[kind], out_send.at[kind], out_recv.at[kind], partner)

    def finish_other(kind):
        finish(kind, 1 - own)
        go(partner_copy(kind))

    def from_partner(kind):
        partner_copy(kind).wait_recv()
        store(orecv.at[kind], (out_hbm, dq_hbm)[kind].at[:, cols(1 - upper)], 2 + kind)

    def touched(k, j):
        return j // PER <= upper_of(k) // PER

    def first_copy(which, j):
        axis = "yz"[which]
        d = (j % N + N - y) % N if which == 0 else (j // N + N - z) % N
        index = j // N if which == 0 else j % N
        copy = remote(
            part.at[which, j], r1.at[which, d - 1, index], r1_send.at[which, j], r1_recv.at[which, d - 1, index],
            along(axis, d),
        )
        return copy, d != 0

    def each_first(j, act):
        for which in (0, 1):
            copy, needed = first_copy(which, j)
            pl.when(needed)(lambda copy=copy: act(copy))

    def send_grads(b):
        for j in (PER * b, PER * b + 1):
            part[0, j] = (dkv[0, j] * scale).astype(BF16)
            part[1, j] = dkv[1, j].astype(BF16)
            each_first(j, lambda copy: copy.start())

    def grads_step(g, i, b):
        e = e_buf[i, b + g * n_hi]
        k = tile_of(kall, b)
        dp = dot(jnp.concatenate([tile_of(vall, b), ones], axis=1), gpa[i, g])
        ds = (e.astype(F32) * dp).astype(BF16)
        at = pl.ds(PER * b, PER)
        dkv[0, at] = dkv[0, at] + dot(ds, qbuf[g, i].reshape(PAIR, WIDTH)).reshape(PER, GROUP, WIDTH)
        dkv[1, at] = dkv[1, at] + dot(e, gp[i, g]).reshape(PER, GROUP, WIDTH)
        dq = dot(k.T, ds)
        for r in (0, 1):
            dq_t[i, g, r] = dq_t[i, g, r] + dq[:, r * ROWS : (r + 1) * ROWS]

    def grads_pass(i, leave):
        def one(n, carry):
            b = (2 * z + 2 + n) % (CHIPS // PER)
            pl.when(b < n_hi)(lambda: grads_step(0, i, b))
            pl.when(b < n_lo)(lambda: grads_step(1, i, b))
            if leave:
                pl.when(b < n_hi)(lambda: send_grads(b))
            return carry

        lax.fori_loop(0, CHIPS // PER, one, 0)
        for g in (0, 1):
            to_core(1, i, g)

    prepare(1 - xp)
    for g in (0, 1):
        to_core(0, 1 - xp, g)
    grads_pass(1 - xp, False)
    prepare(xp)
    for g in (0, 1):
        to_core(0, xp, g)
    for kind in (0, 1):
        for g in (0, 1):
            to_beside(kind, g)
    grads_pass(xp, True)

    def second_copy(which, i):
        d = (i + N - (z if which == 0 else y)) % N
        copy = remote(
            d2.at[which, i], r2.at[which, d - 1], r2_send.at[which, i], r2_recv.at[which, d - 1],
            along("zy"[which], d),
        )
        return copy, d != 0

    def first_sum(i, carry):
        for which in (0, 1):
            j = N * i + y if which == 0 else N * z + i
            acc[...] = jnp.where(touched(chip, j), part[which, j].astype(F32), 0.0)
            for s in range(N - 1):
                k = chip_at(s + 1, 0) if which == 0 else chip_at(0, s + 1)

                @pl.when(touched(k, j))
                def _(s=s):
                    spot = r1.at[which, s, i]
                    remote(spot, spot, r1_send.at[which, 0], r1_recv.at[which, s, i], sibling).wait_recv()
                    acc[...] = acc[...] + r1[which, s, i].astype(F32)

            d2[which, i] = acc[...].astype(BF16)
            copy, needed = second_copy(which, i)
            pl.when(needed)(lambda copy=copy: copy.start())
        return carry

    lax.fori_loop(0, N, first_sum, 0)
    finish_other(1)
    for which, i in ((0, z), (1, y)):
        total = d2[which, i].astype(F32)
        for s in range(N - 1):
            spot = r2.at[which, s]
            remote(spot, spot, r2_send.at[which, 0], r2_recv.at[which, s], sibling).wait_recv()
            total = total + r2[which, s].astype(F32)
        total = total.astype(BF16)
        for half in (0, 1):
            d3[half, which] = total[half * HOME : (half + 1) * HOME]

    def third_copy(half):
        there = home(half)
        copy = remote(d3.at[half], r3.at[p // 2], r3_send.at[half], r3_recv.at[p // 2], there)
        return copy, jnp.logical_not(is_me(there))

    for half in (0, 1):
        copy, needed = third_copy(half)
        pl.when(needed)(lambda copy=copy: copy.start())
    finish_own(1)
    finish_other(0)
    finish_own(0)
    total = jnp.where(keeps, d3[core].astype(F32), 0.0)
    sums[...] = total
    for u in (0, 1):

        @pl.when(jnp.logical_not(is_me(source(u))))
        def _(u=u):
            spot = r3.at[u]
            remote(spot, spot, r3_send.at[0], r3_recv.at[u], sibling).wait_recv()
            sums[...] = sums[...] + r3[u].astype(F32)

    final[...] = sums[...].astype(BF16)
    store(final.at[0], dk_hbm, 4)
    store(final.at[1], dv_hbm, 5)
    from_partner(0)
    from_partner(1)

    def sent(j, carry):
        @pl.when(j // PER < n_hi)
        def _():
            each_first(j, lambda copy: copy.wait_send())

        return carry

    lax.fori_loop(0, CHIPS, sent, 0)
    for which in (0, 1):
        for i in range(N):
            copy, needed = second_copy(which, i)
            pl.when(needed)(lambda copy=copy: copy.wait_send())
    for half in (0, 1):
        copy, needed = third_copy(half)
        pl.when(needed)(lambda copy=copy: copy.wait_send())
    for copy in started:
        copy.wait_send()
    for copy in stores:
        copy.wait()


def on_device(queries, keys, values, out_grad, segment_ids):
    hbm = pl.BlockSpec(memory_space=pl.ANY)
    dma = pltpu.SemaphoreType.DMA
    vmem = pltpu.VMEM
    scratch = [
        vmem((SEQ // WIDTH, WIDTH), jnp.int32),
        vmem((CHIPS, 2, HOME, WIDTH), BF16),
        vmem((CHIPS, 2, HOME, WIDTH), BF16),
        vmem((2, HEADS, 2, ROWS, WIDTH), BF16),
        vmem((2, HEADS, 2, ROWS, WIDTH), BF16),
        vmem((HEADS, TILES, TILE, PAIR), F32),
        vmem((HEADS, TILES, TILE, PAIR), BF16),
        vmem((2, HEADS, 2 * WIDTH, PAIR), BF16),
        vmem((2, HEADS, WIDTH, PAIR), BF16),
        vmem((HEADS, 2, 2 * WIDTH, PAIR), BF16),
        vmem((HEADS, 2, PAIR, WIDTH), BF16),
        vmem((HEADS, 2, 8, PAIR), F32),
        vmem((HEADS, 2, 8, PAIR), F32),
        vmem((HEADS, 2, 2, WIDTH, ROWS), F32),
        vmem((HEADS, 2, 2, WIDTH, ROWS), F32),
        vmem((2, HEADS, 2, WIDTH, ROWS), F32),
        vmem((2, 2, WIDTH, ROWS), BF16),
        vmem((2, 2, WIDTH, ROWS), BF16),
        vmem((HEADS, DEVS, 8, PAIR), F32),
        vmem((2, 2, 1, PAIR), jnp.int32),
        vmem((2, CHIPS, GROUP, WIDTH), F32),
        vmem((2, CHIPS, GROUP, WIDTH), BF16),
        vmem((2, N - 1, N, GROUP, WIDTH), BF16),
        vmem((2, N, GROUP, WIDTH), BF16),
        vmem((2, N - 1, GROUP, WIDTH), BF16),
        vmem((2, 2, HOME, WIDTH), BF16),
        vmem((2, 2, HOME, WIDTH), BF16),
        vmem((GROUP, WIDTH), F32),
        vmem((2, HOME, WIDTH), F32),
        vmem((2, HOME, WIDTH), BF16),
        vmem((2, 2, ROWS, WIDTH), BF16),
        vmem((2, ROWS, WIDTH), BF16),
        dma((2, HEADS)),
        dma((3,)),
        dma((2, 32)), dma((2, CHIPS, 2)),
        dma((2,)), dma((2,)),
        dma((2,)), dma((2,)),
        dma((2,)), dma((2,)),
        dma((2, HEADS)), dma((2, HEADS)),
        dma((HEADS, 3)), dma((HEADS, DEVS)),
        dma((2, HEADS, 2)), dma((2, HEADS, 2)),
        dma((2, 2)), dma((2, 2)),
        dma((2,)), dma((2,)),
        dma((2, CHIPS)), dma((2, N - 1, N)),
        dma((2, N)), dma((2, N - 1)),
        dma((2,)), dma((2,)),
        dma((6,)),
    ]
    tokens = jax.ShapeDtypeStruct((ROWS, 2 * WIDTH), BF16)
    terms = jax.ShapeDtypeStruct((HOME, WIDTH), BF16)
    return pl.pallas_call(
        kernel,
        out_shape=(tokens, tokens, terms, terms),
        in_specs=[hbm] * 5,
        out_specs=(hbm,) * 4,
        scratch_shapes=scratch,
        compiler_params=pltpu.CompilerParams(
            collective_id=0, has_side_effects=True, vmem_limit_bytes=56 * 1024 * 1024
        ),
    )(
        segment_ids.reshape(SEQ // WIDTH, WIDTH),
        queries,
        keys.reshape(2, 2, HOME, WIDTH),
        values.reshape(2, 2, HOME, WIDTH),
        out_grad,
    )


def solution(mesh):
    return jax.shard_map(
        on_device,
        mesh=mesh,
        in_specs=(P("ctx", None), P("ctx", None), P("ctx", None), P("ctx", None), P()),
        out_specs=(P("ctx", "dp"), P("ctx", "dp"), P(("dp", "ctx"), None), P(("dp", "ctx"), None)),
        check_vma=False,
    )
```

```python
import math

import jax
import jax.numpy as jnp
from jax import lax
from jax.experimental import pallas as pl
from jax.experimental.pallas import tpu as pltpu
from jax.sharding import PartitionSpec as P

F32 = jnp.float32
BF16 = jnp.bfloat16
MESH = pl.DeviceIdType.MESH

N = 4
CHIPS = N * N
ROWS = 256
PAIR = 2 * ROWS
WIDTH = 128
SEQ = PAIR * CHIPS
GROUP = 128
HOME = 64
PER = 4
TILE = PER * GROUP
TILES = 5
HEADS = 2
DEVS = 4
NEG = -1e30


def dot(a, b):
    return lax.dot_general(a, b, (((1,), (0,)), ((), ())), preferred_element_type=F32)


def kernel(
    seg_hbm, q_hbm, k_hbm, v_hbm, g_hbm,
    out_hbm, dq_hbm, dk_hbm, dv_hbm,
    seg_ref, kall, vall, qbuf, gbuf, s_buf, e_buf,
    qa, gt, gpa, gp, mx, tot, o_t, dq_t, core_x, xs, xr, st, rng, dkv,
    part, r1, d2, r2, d3, r3, acc, sums, final, obuf, orecv,
    load_sem, kv_sem, ag_send, ag_recv, pair_send, pair_recv, own_send, own_recv, x_send, x_recv, rel_send, rel_recv,
    st_send, st_recv, core_send, core_recv, sum_send, sum_recv, out_send, out_recv, r1_send, r1_recv, r2_send, r2_recv, r3_send, r3_recv, store_sem,
):
    p = lax.axis_index("dp")
    c = lax.axis_index("ctx")
    core = c % 2
    chip = c // 2
    z = chip % N
    y = chip // N
    xp = p % 2
    me = 2 * xp + core
    neighbour = p + 1 - 2 * xp
    sibling = (p, 2 * chip + 1 - core)
    partner = (p, 2 * (CHIPS - 1 - chip) + core)
    upper = (chip >= CHIPS // 2).astype(jnp.int32)
    own = 1 - upper
    lo = jnp.minimum(chip, CHIPS - 1 - chip)
    hi = CHIPS - 1 - lo
    n_hi = hi // PER + 1
    n_lo = lo // PER + 1
    n_own = jnp.where(upper == 1, n_hi, n_lo)
    n_other = TILES - n_own

    def beside(core_):
        return (neighbour, 2 * chip + core_)

    def head_of(slot, parity):
        return 2 * (p - xp + slot) + parity

    def along(axis, d):
        there = dict(y=y, z=z)
        there[axis] = (there[axis] + d) % N
        return (p, (there["y"] * N + there["z"]) * 2 + core)

    def chip_at(dy, dz):
        return ((y + N - dy) % N) * N + (z + N - dz) % N

    def upper_of(k):
        return jnp.maximum(k, CHIPS - 1 - k)

    def cols(head):
        return pl.ds(pl.multiple_of(head * WIDTH, WIDTH), WIDTH)

    home_z = 2 * core + xp

    def home(half):
        return (z, (y * N + home_z) * 2 + half)

    def source(u):
        return (z % 2 + 2 * u, (y * N + p) * 2 + z // 2)

    def is_me(dev):
        return (dev[0] == p) & (dev[1] == c)

    keeps = (z == p) & (home_z == z)

    barrier = pltpu.get_barrier_semaphore()

    def greet(there):
        pl.semaphore_signal(barrier, inc=1, device_id=there, device_id_type=MESH)

    for d in range(1, N):
        for axis in "yz":
            greet(along(axis, d))
    for there in (partner, beside(core), beside(1 - core), sibling):
        greet(there)
    for u in (0, 1):
        pl.when(jnp.logical_not(is_me(source(u))))(lambda u=u: greet(source(u)))

    kv_loads = [
        pltpu.make_async_copy(src.at[xp], dst.at[chip], kv_sem.at[i])
        for i, (src, dst) in enumerate(((k_hbm, kall), (v_hbm, vall)))
    ]
    arrays = ((q_hbm, qbuf), (g_hbm, gbuf))
    loads = [
        pltpu.make_async_copy(src.at[:, cols(head_of(i, upper))], buf.at[own, i, core], load_sem.at[a, i])
        for a, (src, buf) in enumerate(arrays)
        for i in range(HEADS)
    ]
    seg_load = pltpu.make_async_copy(seg_hbm, seg_ref, kv_sem.at[2])
    for copy in kv_loads + loads + [seg_load]:
        copy.start()
    started = []

    def remote(src, dst, send, recv, there):
        return pltpu.make_async_remote_copy(
            src_ref=src, dst_ref=dst, send_sem=send, recv_sem=recv, device_id=there, device_id_type=MESH
        )

    def go(copy):
        copy.start()
        started.append(copy)
        return copy

    whole = (kall, vall)
    count = [0, 0]
    key_copies = []

    def push(which, block, half, there):
        spot = whole[which].at[block, half]
        copy = remote(spot, spot, ag_send.at[which, count[which]], ag_recv.at[which, block, half], there)
        count[which] += 1
        if which == 0:
            copy.start()
            key_copies.append(copy)
        else:
            go(copy)

    def arrived(which, block, half):
        spot = whole[which].at[block, half]
        remote(spot, spot, ag_send.at[which, 0], ag_recv.at[which, block, half], sibling).wait_recv()

    def push_mine(which):
        for axes in ("yz", "zy"):
            for d in (1, 3, 2):
                for half in (0, 1):
                    push(which, chip, half, along(axes[half], d))

    def relay(which):
        for d in (1, 3, 2):
            for half, block in ((0, chip_at(d, 0)), (1, chip_at(0, d))):
                arrived(which, block, half)
                for d2 in (1, 3, 2):
                    push(which, block, half, along("zy"[half], d2))

    def tile_in_order(n):
        return (y + jnp.where(n == 2, 3, jnp.where(n == 3, 2, n))) % N

    def tile_arrived(which, b):
        for i in range(PER):
            j = PER * b + i
            pl.when(z != i)(lambda j=j: arrived(which, j, 0))
            pl.when(b != y)(lambda j=j: arrived(which, j, 1))

    def pair_copy(a):
        src, buf = arrays[a]
        src = src.at[:, cols(2 * p + 1 - upper)]
        return remote(src, buf.at[own, xp, core], pair_send.at[a], pair_recv.at[a], partner)

    def share_own(a):
        spot = arrays[a][1].at[own, :, core]
        for i in range(HEADS):
            loads[HEADS * a + i].wait()
        go(remote(spot, spot, own_send.at[a], own_recv.at[a], sibling))

    def to_sibling(a, slot):
        spot = arrays[a][1].at[1 - own, slot, core]
        go(remote(spot, spot, rel_send.at[a, slot], rel_recv.at[a, slot], sibling))

    def share_pair(a):
        spot = arrays[a][1].at[1 - own, xp, core]
        remote(spot, spot, pair_send.at[a], pair_recv.at[a], partner).wait_recv()
        go(remote(spot, spot, x_send.at[a], x_recv.at[a], beside(core)))
        to_sibling(a, xp)

    def pass_on(a):
        spot = arrays[a][1].at[1 - own, 1 - xp, core]
        remote(spot, spot, x_send.at[a], x_recv.at[a], sibling).wait_recv()
        to_sibling(a, 1 - xp)

    def from_sibling(a):
        for i in range(HEADS):
            spot = arrays[a][1].at[1 - own, i, 1 - core]
            remote(spot, spot, rel_send.at[a, 0], rel_recv.at[a, i], sibling).wait_recv()

    def own_from_sibling(a):
        spot = arrays[a][1].at[own, :, 1 - core]
        remote(spot, spot, own_send.at[a], own_recv.at[a], sibling).wait_recv()

    pl.semaphore_wait(barrier, 12 - keeps.astype(jnp.int32))
    go(pair_copy(0))
    kv_loads[0].wait()
    push_mine(0)
    share_own(0)
    go(pair_copy(1))
    relay(0)

    scale = WIDTH**-0.5
    seg_load.wait()
    seg = seg_ref[...]
    starts = [jnp.sum((seg < doc).astype(jnp.int32), axis=(0, 1), keepdims=True) for doc in (1, 2, 3)]
    lane = lax.broadcasted_iota(jnp.int32, (1, WIDTH), 1)
    for g, block in ((0, hi), (1, lo)):
        for i in range(PAIR // WIDTH):
            ids = seg_ref[pl.ds(block * (PAIR // WIDTH) + i, 1), :]
            start = jnp.where(
                ids == 0, 0, jnp.where(ids == 1, starts[0], jnp.where(ids == 2, starts[1], starts[2]))
            )
            rng[g, 0, :, i * WIDTH : (i + 1) * WIDTH] = start
            rng[g, 1, :, i * WIDTH : (i + 1) * WIDTH] = block * PAIR + i * WIDTH + lane
    mx[...] = jnp.full_like(mx, NEG)
    tot[...] = jnp.zeros_like(tot)

    def clear(i, carry):
        for ref in (o_t, dq_t):
            ref[i] = jnp.zeros_like(ref[i])
        return carry

    lax.fori_loop(0, HEADS, clear, 0)

    def clear_block(j, carry):
        for which in (0, 1):
            dkv[which, j] = jnp.zeros((GROUP, WIDTH), F32)
        return carry

    lax.fori_loop(0, CHIPS, clear_block, 0)

    def scale_rows(g):
        def one(i, carry):
            for r in (0, 1):
                at = slice(r * ROWS, (r + 1) * ROWS)
                scaled = qbuf[g, i, r].astype(F32).T * (scale * math.log2(math.e))
                high = scaled.astype(BF16)
                qa[g, i, :WIDTH, at] = high
                qa[g, i, WIDTH:, at] = (scaled - high.astype(F32)).astype(BF16)
            return carry

        lax.fori_loop(0, HEADS, one, 0)

    def turn_grads(g):
        def one(i, carry):
            for r in (0, 1):
                gt[g, i, :, r * ROWS : (r + 1) * ROWS] = gbuf[g, i, r].T
            return carry

        lax.fori_loop(0, HEADS, one, 0)

    row = lax.broadcasted_iota(jnp.int32, (TILE, PAIR), 0)
    token = PAIR * (row // GROUP) + row % GROUP + ROWS * core + GROUP * xp

    def tile_of(ref, b):
        return ref[pl.ds(PER * b, PER)].reshape(TILE, WIDTH)

    def fold(op, values):
        return op(values.reshape(TILE // 8, 8, PAIR), axis=0)

    def scores_step(g, b):
        k = tile_of(kall, b)
        k = jnp.concatenate([k, k], axis=1)
        key = token + b * (PER * PAIR)
        seen = (key >= rng[g, 0]) & (key <= rng[g, 1])

        def one(i, carry):
            s = jnp.where(seen, dot(k, qa[g, i]), NEG)
            s_buf[i, b + g * n_hi] = s
            mx[i, g] = jnp.maximum(mx[i, g], fold(jnp.max, s))
            return carry

        lax.fori_loop(0, HEADS, one, 0)

    share_pair(0)
    own_from_sibling(0)
    scale_rows(own)

    def scores_own(n, carry):
        b = tile_in_order(n)
        tile_arrived(0, b)

        @pl.when(b < n_own)
        def _():
            scores_step(own, b)

        return carry

    lax.fori_loop(0, 1, scores_own, 0)
    for copy in key_copies:
        copy.wait_send()
    kv_loads[1].wait()
    push_mine(1)
    share_own(1)
    pass_on(0)
    lax.fori_loop(1, CHIPS // PER, scores_own, 0)
    relay(1)
    share_pair(1)
    own_from_sibling(1)
    turn_grads(own)
    from_sibling(0)
    scale_rows(1 - own)

    def scores_other(b, carry):
        scores_step(1 - own, b)
        return carry

    lax.fori_loop(0, n_other, scores_other, 0)
    pass_on(1)

    def tile_place(t):
        g = (t >= n_hi).astype(jnp.int32)
        return g, t - g * n_hi

    def weights_step(i, g, b):
        t = b + g * n_hi
        e = jnp.exp2(s_buf[i, t] - mx[i, g, 0:1])
        tot[i, g] = tot[i, g] + fold(jnp.sum, e)
        e = e.astype(BF16)
        e_buf[i, t] = e
        o = dot(tile_of(vall, b).T, e)
        for r in (0, 1):
            o_t[i, g, r] = o_t[i, g, r] + o[:, r * ROWS : (r + 1) * ROWS]

    def weights_arriving(n, carry):
        b = tile_in_order(n)
        tile_arrived(1, b)
        pl.when(b < n_hi)(lambda: weights_step(xp, 0, b))
        pl.when(b < n_lo)(lambda: weights_step(xp, 1, b))
        return carry

    def weights_beside(n, carry):
        weights_step(1 - xp, *tile_place(n))
        return carry

    def statistics(i):
        for g in (0, 1):
            at = 4 * g
            st[i, me, at : at + 1] = mx[i, g, 0:1]
            st[i, me, at + 1 : at + 2] = jnp.sum(tot[i, g], axis=0, keepdims=True)
            o = jnp.concatenate([o_t[i, g, 0], o_t[i, g, 1]], axis=1)
            st[i, me, at + 2 : at + 3] = jnp.sum(gt[g, i].astype(F32) * o, axis=0, keepdims=True)
            st[i, me, at + 3 : at + 4] = jnp.zeros((1, PAIR), F32)
        spot = st.at[i, me]
        for slot, there in enumerate((beside(core), beside(1 - core), sibling)):
            go(remote(spot, spot, st_send.at[i, slot], st_recv.at[i, me], there))

    for i in (0, 1):
        for g in (0, 1):
            mx[i, g] = jnp.broadcast_to(jnp.max(mx[i, g], axis=0, keepdims=True), (8, PAIR))
    lax.fori_loop(0, CHIPS // PER, weights_arriving, 0)
    from_sibling(1)
    turn_grads(1 - own)
    statistics(xp)
    lax.fori_loop(0, TILES, weights_beside, 0)
    statistics(1 - xp)

    ones = jnp.ones((TILE, WIDTH), BF16)
    sub = lax.broadcasted_iota(jnp.int32, (WIDTH, PAIR), 0)

    def prepare(i):
        for other in (2 * (1 - xp), 2 * (1 - xp) + 1, 2 * xp + 1 - core):
            spot = st.at[i, other]
            remote(spot, spot, st_send.at[i, 0], st_recv.at[i, other], sibling).wait_recv()
        for g in (0, 1):
            at = 4 * g
            tops = [st[i, s, at : at + 1] for s in range(DEVS)]
            top = jnp.maximum(jnp.maximum(tops[0], tops[1]), jnp.maximum(tops[2], tops[3]))
            total = delta = jnp.zeros((1, PAIR), F32)
            for s in range(DEVS):
                by = jnp.exp2(tops[s] - top)
                total = total + by * st[i, s, at + 1 : at + 2]
                delta = delta + by * st[i, s, at + 2 : at + 3]
            inv = 1.0 / total
            factor = jnp.exp2(st[i, me, at : at + 1] - top) * inv
            delta = -delta * inv * factor
            for r in (0, 1):
                o_t[i, g, r] = o_t[i, g, r] * factor[:, r * ROWS : (r + 1) * ROWS]
            grad = (gt[g, i].astype(F32) * factor).astype(BF16)
            gpa[i, g, :WIDTH] = grad
            gp[i, g] = grad.T
            d1 = delta.astype(BF16).astype(F32)
            d2 = (delta - d1).astype(BF16).astype(F32)
            extra = jnp.where(sub == 0, d1, jnp.where(sub == 1, d2, jnp.where(sub == 2, delta - d1 - d2, 0.0)))
            gpa[i, g, WIDTH:] = extra.astype(BF16)

    parts_of = (o_t, dq_t)

    def to_core(kind, i, g):
        go(
            remote(
                parts_of[kind].at[i, g, 1 - core], core_x.at[kind, i, g],
                core_send.at[kind, i, g], core_recv.at[kind, i, g], sibling,
            )
        )

    def from_core(kind, i, g):
        spot = core_x.at[kind, i, g]
        remote(spot, spot, core_send.at[kind, i, g], core_recv.at[kind, i, g], sibling).wait_recv()
        return parts_of[kind][i, g, core] + core_x[kind, i, g]

    def to_beside(kind, g):
        xs[kind, g] = from_core(kind, 1 - xp, g).astype(BF16)
        go(remote(xs.at[kind, g], xr.at[kind, g], sum_send.at[kind, g], sum_recv.at[kind, g], beside(core)))

    stores = []

    def store(src, dst, i):
        stores.append(pltpu.make_async_copy(src, dst, store_sem.at[i]))
        stores[-1].start()

    def finish(kind, g):
        total = from_core(kind, xp, g)
        spot = xr.at[kind, g]
        remote(spot, spot, sum_send.at[kind, g], sum_recv.at[kind, g], sibling).wait_recv()
        total = total + xr[kind, g].astype(F32)
        if kind == 1:
            total = total * scale
        obuf[kind, g] = total.T.astype(BF16)

    def finish_own(kind):
        finish(kind, own)
        store(obuf.at[kind, own], (out_hbm, dq_hbm)[kind].at[:, cols(upper)], kind)

    def partner_copy(kind):
        return remote(obuf.at[kind, 1 - own], orecv.at[kind], out_send.at[kind], out_recv.at[kind], partner)

    def finish_other(kind):
        finish(kind, 1 - own)
        go(partner_copy(kind))

    def from_partner(kind):
        partner_copy(kind).wait_recv()
        store(orecv.at[kind], (out_hbm, dq_hbm)[kind].at[:, cols(1 - upper)], 2 + kind)

    def touched(k, j):
        return j // PER <= upper_of(k) // PER

    def first_copy(which, j):
        axis = "yz"[which]
        d = (j % N + N - y) % N if which == 0 else (j // N + N - z) % N
        index = j // N if which == 0 else j % N
        copy = remote(
            part.at[which, j], r1.at[which, d - 1, index], r1_send.at[which, j], r1_recv.at[which, d - 1, index],
            along(axis, d),
        )
        return copy, d != 0

    def each_first(j, act):
        for which in (0, 1):
            copy, needed = first_copy(which, j)
            pl.when(needed)(lambda copy=copy: act(copy))

    def send_grads(b):
        for j in [PER * b + k for k in range(PER)]:
            part[0, j] = (dkv[0, j] * scale).astype(BF16)
            part[1, j] = dkv[1, j].astype(BF16)
            each_first(j, lambda copy: copy.start())

    def grads_step(g, i, b):
        e = e_buf[i, b + g * n_hi]
        k = tile_of(kall, b)
        dp = dot(jnp.concatenate([tile_of(vall, b), ones], axis=1), gpa[i, g])
        ds = (e.astype(F32) * dp).astype(BF16)
        at = pl.ds(PER * b, PER)
        dkv[0, at] = dkv[0, at] + dot(ds, qbuf[g, i].reshape(PAIR, WIDTH)).reshape(PER, GROUP, WIDTH)
        dkv[1, at] = dkv[1, at] + dot(e, gp[i, g]).reshape(PER, GROUP, WIDTH)
        dq = dot(k.T, ds)
        for r in (0, 1):
            dq_t[i, g, r] = dq_t[i, g, r] + dq[:, r * ROWS : (r + 1) * ROWS]

    def grads_pass(i, leave):
        def one(t, carry):
            g = (t < n_lo).astype(jnp.int32)
            b = jnp.where(t < n_lo, t, (t - n_lo + z + 1) % n_hi)
            grads_step(g, i, b)
            if leave:
                pl.when(g == 0)(lambda: send_grads(b))
            return carry

        lax.fori_loop(0, TILES, one, 0)
        for g in (0, 1):
            to_core(1, i, g)

    prepare(1 - xp)
    for g in (0, 1):
        to_core(0, 1 - xp, g)
    grads_pass(1 - xp, False)
    prepare(xp)
    for g in (0, 1):
        to_core(0, xp, g)
    for kind in (0, 1):
        for g in (0, 1):
            to_beside(kind, g)
    grads_pass(xp, True)

    def second_copy(which, i):
        d = (i + N - (z if which == 0 else y)) % N
        copy = remote(
            d2.at[which, i], r2.at[which, d - 1], r2_send.at[which, i], r2_recv.at[which, d - 1],
            along("zy"[which], d),
        )
        return copy, d != 0

    def first_sum(i, carry):
        for which in (0, 1):
            j = N * i + y if which == 0 else N * z + i
            acc[...] = jnp.where(touched(chip, j), part[which, j].astype(F32), 0.0)
            for s in range(N - 1):
                k = chip_at(s + 1, 0) if which == 0 else chip_at(0, s + 1)

                @pl.when(touched(k, j))
                def _(s=s):
                    spot = r1.at[which, s, i]
                    remote(spot, spot, r1_send.at[which, 0], r1_recv.at[which, s, i], sibling).wait_recv()
                    acc[...] = acc[...] + r1[which, s, i].astype(F32)

            d2[which, i] = acc[...].astype(BF16)
            copy, needed = second_copy(which, i)
            pl.when(needed)(lambda copy=copy: copy.start())
        return carry

    lax.fori_loop(0, N, first_sum, 0)
    finish_other(1)
    for which, i in ((0, z), (1, y)):
        total = d2[which, i].astype(F32)
        for s in range(N - 1):
            spot = r2.at[which, s]
            remote(spot, spot, r2_send.at[which, 0], r2_recv.at[which, s], sibling).wait_recv()
            total = total + r2[which, s].astype(F32)
        total = total.astype(BF16)
        for half in (0, 1):
            d3[half, which] = total[half * HOME : (half + 1) * HOME]

    def third_copy(half):
        there = home(half)
        copy = remote(d3.at[half], r3.at[p // 2], r3_send.at[half], r3_recv.at[p // 2], there)
        return copy, jnp.logical_not(is_me(there))

    for half in (0, 1):
        copy, needed = third_copy(half)
        pl.when(needed)(lambda copy=copy: copy.start())
    finish_own(1)
    finish_other(0)
    finish_own(0)
    total = jnp.where(keeps, d3[core].astype(F32), 0.0)
    sums[...] = total
    for u in (0, 1):

        @pl.when(jnp.logical_not(is_me(source(u))))
        def _(u=u):
            spot = r3.at[u]
            remote(spot, spot, r3_send.at[0], r3_recv.at[u], sibling).wait_recv()
            sums[...] = sums[...] + r3[u].astype(F32)

    final[...] = sums[...].astype(BF16)
    store(final.at[0], dk_hbm, 4)
    store(final.at[1], dv_hbm, 5)
    from_partner(0)
    from_partner(1)

    def sent(j, carry):
        @pl.when(j // PER < n_hi)
        def _():
            each_first(j, lambda copy: copy.wait_send())

        return carry

    lax.fori_loop(0, CHIPS, sent, 0)
    for which in (0, 1):
        for i in range(N):
            copy, needed = second_copy(which, i)
            pl.when(needed)(lambda copy=copy: copy.wait_send())
    for half in (0, 1):
        copy, needed = third_copy(half)
        pl.when(needed)(lambda copy=copy: copy.wait_send())
    for copy in started:
        copy.wait_send()
    for copy in stores:
        copy.wait()


def hand_on(*refs):
    for i in range(4):
        refs[4 + i][...] = refs[i][...]


def on_device(queries, keys, values, out_grad, segment_ids):
    hbm = pl.BlockSpec(memory_space=pl.ANY)
    dma = pltpu.SemaphoreType.DMA
    vmem = pltpu.VMEM
    scratch = [
        vmem((SEQ // WIDTH, WIDTH), jnp.int32),
        vmem((CHIPS, 2, HOME, WIDTH), BF16),
        vmem((CHIPS, 2, HOME, WIDTH), BF16),
        vmem((2, HEADS, 2, ROWS, WIDTH), BF16),
        vmem((2, HEADS, 2, ROWS, WIDTH), BF16),
        vmem((HEADS, TILES, TILE, PAIR), F32),
        vmem((HEADS, TILES, TILE, PAIR), BF16),
        vmem((2, HEADS, 2 * WIDTH, PAIR), BF16),
        vmem((2, HEADS, WIDTH, PAIR), BF16),
        vmem((HEADS, 2, 2 * WIDTH, PAIR), BF16),
        vmem((HEADS, 2, PAIR, WIDTH), BF16),
        vmem((HEADS, 2, 8, PAIR), F32),
        vmem((HEADS, 2, 8, PAIR), F32),
        vmem((HEADS, 2, 2, WIDTH, ROWS), F32),
        vmem((HEADS, 2, 2, WIDTH, ROWS), F32),
        vmem((2, HEADS, 2, WIDTH, ROWS), F32),
        vmem((2, 2, WIDTH, ROWS), BF16),
        vmem((2, 2, WIDTH, ROWS), BF16),
        vmem((HEADS, DEVS, 8, PAIR), F32),
        vmem((2, 2, 1, PAIR), jnp.int32),
        vmem((2, CHIPS, GROUP, WIDTH), F32),
        vmem((2, CHIPS, GROUP, WIDTH), BF16),
        vmem((2, N - 1, N, GROUP, WIDTH), BF16),
        vmem((2, N, GROUP, WIDTH), BF16),
        vmem((2, N - 1, GROUP, WIDTH), BF16),
        vmem((2, 2, HOME, WIDTH), BF16),
        vmem((2, 2, HOME, WIDTH), BF16),
        vmem((GROUP, WIDTH), F32),
        vmem((2, HOME, WIDTH), F32),
        vmem((2, HOME, WIDTH), BF16),
        vmem((2, 2, ROWS, WIDTH), BF16),
        vmem((2, ROWS, WIDTH), BF16),
        dma((2, HEADS)),
        dma((3,)),
        dma((2, 32)), dma((2, CHIPS, 2)),
        dma((2,)), dma((2,)),
        dma((2,)), dma((2,)),
        dma((2,)), dma((2,)),
        dma((2, HEADS)), dma((2, HEADS)),
        dma((HEADS, 3)), dma((HEADS, DEVS)),
        dma((2, HEADS, 2)), dma((2, HEADS, 2)),
        dma((2, 2)), dma((2, 2)),
        dma((2,)), dma((2,)),
        dma((2, CHIPS)), dma((2, N - 1, N)),
        dma((2, N)), dma((2, N - 1)),
        dma((2,)), dma((2,)),
        dma((6,)),
    ]
    tokens = jax.ShapeDtypeStruct((ROWS, 2 * WIDTH), BF16)
    terms = jax.ShapeDtypeStruct((HOME, WIDTH), BF16)
    parts = pl.pallas_call(
        kernel,
        out_shape=(tokens, tokens, terms, terms),
        in_specs=[hbm] * 5,
        out_specs=(hbm,) * 4,
        scratch_shapes=scratch,
        compiler_params=pltpu.CompilerParams(
            collective_id=0, has_side_effects=True, vmem_limit_bytes=56 * 1024 * 1024
        ),
    )(
        segment_ids.reshape(SEQ // WIDTH, WIDTH),
        queries,
        keys.reshape(2, 2, HOME, WIDTH),
        values.reshape(2, 2, HOME, WIDTH),
        out_grad,
    )
    return pl.pallas_call(
        hand_on,
        out_shape=(tokens, tokens, terms, terms),
        in_specs=[pl.BlockSpec(memory_space=vmem)] * 4,
        out_specs=(pl.BlockSpec(memory_space=vmem),) * 4,
    )(*parts)


def solution(mesh):
    return jax.shard_map(
        on_device,
        mesh=mesh,
        in_specs=(P("ctx", None), P("ctx", None), P("ctx", None), P("ctx", None), P()),
        out_specs=(P("ctx", "dp"), P("ctx", "dp"), P(("dp", "ctx"), None), P(("dp", "ctx"), None)),
        check_vma=False,
    )
```

```python
import math

import jax
import jax.numpy as jnp
from jax import lax
from jax.experimental import pallas as pl
from jax.experimental.pallas import tpu as pltpu
from jax.sharding import PartitionSpec as P

F32 = jnp.float32
BF16 = jnp.bfloat16
MESH = pl.DeviceIdType.MESH

N = 4
CHIPS = N * N
ROWS = 256
PAIR = 2 * ROWS
WIDTH = 128
SEQ = PAIR * CHIPS
GROUP = 128
HOME = 64
PER = 4
TILE = PER * GROUP
TILES = 5
HEADS = 2
DEVS = 4
NEG = -1e30


def dot(a, b):
    return lax.dot_general(a, b, (((1,), (0,)), ((), ())), preferred_element_type=F32)


def kernel(
    seg_hbm, q_hbm, k_hbm, v_hbm, g_hbm,
    out_ref, dq_ref, dk_ref, dv_ref,
    seg_ref, kall, vall, qbuf, gbuf, s_buf, e_buf,
    qa, gt, gpa, gp, mx, tot, o_t, dq_t, core_x, xs, xr, st, rng, dkv,
    part, r1, d2, r2, d3, r3, acc, sums, obuf, orecv,
    load_sem, kv_sem, ag_send, ag_recv, pair_send, pair_recv, own_send, own_recv, x_send, x_recv, rel_send, rel_recv,
    st_send, st_recv, core_send, core_recv, sum_send, sum_recv, out_send, out_recv, r1_send, r1_recv, r2_send, r2_recv, r3_send, r3_recv,
):
    p = lax.axis_index("dp")
    c = lax.axis_index("ctx")
    core = c % 2
    chip = c // 2
    z = chip % N
    y = chip // N
    xp = p % 2
    me = 2 * xp + core
    neighbour = p + 1 - 2 * xp
    sibling = (p, 2 * chip + 1 - core)
    partner = (p, 2 * (CHIPS - 1 - chip) + core)
    upper = (chip >= CHIPS // 2).astype(jnp.int32)
    own = 1 - upper
    lo = jnp.minimum(chip, CHIPS - 1 - chip)
    hi = CHIPS - 1 - lo
    n_hi = hi // PER + 1
    n_lo = lo // PER + 1
    n_own = jnp.where(upper == 1, n_hi, n_lo)
    n_other = TILES - n_own

    def beside(core_):
        return (neighbour, 2 * chip + core_)

    def head_of(slot, parity):
        return 2 * (p - xp + slot) + parity

    def along(axis, d):
        there = dict(y=y, z=z)
        there[axis] = (there[axis] + d) % N
        return (p, (there["y"] * N + there["z"]) * 2 + core)

    def chip_at(dy, dz):
        return ((y + N - dy) % N) * N + (z + N - dz) % N

    def upper_of(k):
        return jnp.maximum(k, CHIPS - 1 - k)

    def cols(head):
        return pl.ds(pl.multiple_of(head * WIDTH, WIDTH), WIDTH)

    home_z = 2 * core + xp

    def home(half):
        return (z, (y * N + home_z) * 2 + half)

    def source(u):
        return (z % 2 + 2 * u, (y * N + p) * 2 + z // 2)

    def is_me(dev):
        return (dev[0] == p) & (dev[1] == c)

    keeps = (z == p) & (home_z == z)

    barrier = pltpu.get_barrier_semaphore()

    def greet(there):
        pl.semaphore_signal(barrier, inc=1, device_id=there, device_id_type=MESH)

    for d in range(1, N):
        for axis in "yz":
            greet(along(axis, d))
    for there in (partner, beside(core), beside(1 - core), sibling):
        greet(there)
    for u in (0, 1):
        pl.when(jnp.logical_not(is_me(source(u))))(lambda u=u: greet(source(u)))

    kv_loads = [
        pltpu.make_async_copy(src.at[xp], dst.at[chip], kv_sem.at[i])
        for i, (src, dst) in enumerate(((k_hbm, kall), (v_hbm, vall)))
    ]
    arrays = ((q_hbm, qbuf), (g_hbm, gbuf))
    loads = [
        pltpu.make_async_copy(src.at[:, cols(head_of(i, upper))], buf.at[own, i, core], load_sem.at[a, i])
        for a, (src, buf) in enumerate(arrays)
        for i in range(HEADS)
    ]
    seg_load = pltpu.make_async_copy(seg_hbm, seg_ref, kv_sem.at[2])
    for copy in kv_loads + loads + [seg_load]:
        copy.start()
    started = []

    def remote(src, dst, send, recv, there):
        return pltpu.make_async_remote_copy(
            src_ref=src, dst_ref=dst, send_sem=send, recv_sem=recv, device_id=there, device_id_type=MESH
        )

    def go(copy):
        copy.start()
        started.append(copy)
        return copy

    whole = (kall, vall)
    count = [0, 0]
    key_copies = []

    def push(which, block, half, there):
        spot = whole[which].at[block, half]
        copy = remote(spot, spot, ag_send.at[which, count[which]], ag_recv.at[which, block, half], there)
        count[which] += 1
        if which == 0:
            copy.start()
            key_copies.append(copy)
        else:
            go(copy)

    def arrived(which, block, half):
        spot = whole[which].at[block, half]
        remote(spot, spot, ag_send.at[which, 0], ag_recv.at[which, block, half], sibling).wait_recv()

    def push_mine(which):
        for axes in ("yz", "zy"):
            for d in (1, 3, 2):
                for half in (0, 1):
                    push(which, chip, half, along(axes[half], d))

    def relay(which):
        for d in (1, 3, 2):
            for half, block in ((0, chip_at(d, 0)), (1, chip_at(0, d))):
                arrived(which, block, half)
                for d2 in (1, 3, 2):
                    push(which, block, half, along("zy"[half], d2))

    def tile_in_order(n):
        return (y + jnp.where(n == 2, 3, jnp.where(n == 3, 2, n))) % N

    def tile_arrived(which, b):
        for i in range(PER):
            j = PER * b + i
            pl.when(z != i)(lambda j=j: arrived(which, j, 0))
            pl.when(b != y)(lambda j=j: arrived(which, j, 1))

    def pair_copy(a):
        src, buf = arrays[a]
        src = src.at[:, cols(2 * p + 1 - upper)]
        return remote(src, buf.at[own, xp, core], pair_send.at[a], pair_recv.at[a], partner)

    def share_own(a):
        spot = arrays[a][1].at[own, :, core]
        for i in range(HEADS):
            loads[HEADS * a + i].wait()
        go(remote(spot, spot, own_send.at[a], own_recv.at[a], sibling))

    def to_sibling(a, slot):
        spot = arrays[a][1].at[1 - own, slot, core]
        go(remote(spot, spot, rel_send.at[a, slot], rel_recv.at[a, slot], sibling))

    def share_pair(a):
        spot = arrays[a][1].at[1 - own, xp, core]
        remote(spot, spot, pair_send.at[a], pair_recv.at[a], partner).wait_recv()
        go(remote(spot, spot, x_send.at[a], x_recv.at[a], beside(core)))
        to_sibling(a, xp)

    def pass_on(a):
        spot = arrays[a][1].at[1 - own, 1 - xp, core]
        remote(spot, spot, x_send.at[a], x_recv.at[a], sibling).wait_recv()
        to_sibling(a, 1 - xp)

    def from_sibling(a):
        for i in range(HEADS):
            spot = arrays[a][1].at[1 - own, i, 1 - core]
            remote(spot, spot, rel_send.at[a, 0], rel_recv.at[a, i], sibling).wait_recv()

    def own_from_sibling(a):
        spot = arrays[a][1].at[own, :, 1 - core]
        remote(spot, spot, own_send.at[a], own_recv.at[a], sibling).wait_recv()

    pl.semaphore_wait(barrier, 12 - keeps.astype(jnp.int32))
    go(pair_copy(0))
    kv_loads[0].wait()
    push_mine(0)
    share_own(0)
    go(pair_copy(1))
    relay(0)
    kv_loads[1].wait()
    push_mine(1)

    scale = WIDTH**-0.5
    seg_load.wait()
    seg = seg_ref[...]
    starts = [jnp.sum((seg < doc).astype(jnp.int32), axis=(0, 1), keepdims=True) for doc in (1, 2, 3)]
    lane = lax.broadcasted_iota(jnp.int32, (1, WIDTH), 1)
    for g, block in ((0, hi), (1, lo)):
        for i in range(PAIR // WIDTH):
            ids = seg_ref[pl.ds(block * (PAIR // WIDTH) + i, 1), :]
            start = jnp.where(
                ids == 0, 0, jnp.where(ids == 1, starts[0], jnp.where(ids == 2, starts[1], starts[2]))
            )
            rng[g, 0, :, i * WIDTH : (i + 1) * WIDTH] = start
            rng[g, 1, :, i * WIDTH : (i + 1) * WIDTH] = block * PAIR + i * WIDTH + lane
    mx[...] = jnp.full_like(mx, NEG)
    tot[...] = jnp.zeros_like(tot)

    def clear(i, carry):
        for ref in (o_t, dq_t):
            ref[i] = jnp.zeros_like(ref[i])
        return carry

    lax.fori_loop(0, HEADS, clear, 0)

    def clear_block(j, carry):
        for which in (0, 1):
            dkv[which, j] = jnp.zeros((GROUP, WIDTH), F32)
        return carry

    lax.fori_loop(0, CHIPS, clear_block, 0)

    def scale_rows(g):
        def one(i, carry):
            for r in (0, 1):
                at = slice(r * ROWS, (r + 1) * ROWS)
                scaled = qbuf[g, i, r].astype(F32).T * (scale * math.log2(math.e))
                high = scaled.astype(BF16)
                qa[g, i, :WIDTH, at] = high
                qa[g, i, WIDTH:, at] = (scaled - high.astype(F32)).astype(BF16)
            return carry

        lax.fori_loop(0, HEADS, one, 0)

    def turn_grads(g):
        def one(i, carry):
            for r in (0, 1):
                gt[g, i, :, r * ROWS : (r + 1) * ROWS] = gbuf[g, i, r].T
            return carry

        lax.fori_loop(0, HEADS, one, 0)

    row = lax.broadcasted_iota(jnp.int32, (TILE, PAIR), 0)
    token = PAIR * (row // GROUP) + row % GROUP + ROWS * core + GROUP * xp

    def tile_of(ref, b):
        return ref[pl.ds(PER * b, PER)].reshape(TILE, WIDTH)

    def fold(op, values):
        return op(values.reshape(TILE // 8, 8, PAIR), axis=0)

    def scores_step(g, b):
        k = tile_of(kall, b)
        k = jnp.concatenate([k, k], axis=1)
        key = token + b * (PER * PAIR)
        seen = (key >= rng[g, 0]) & (key <= rng[g, 1])

        def one(i, carry):
            s = jnp.where(seen, dot(k, qa[g, i]), NEG)
            s_buf[i, b + g * n_hi] = s
            mx[i, g] = jnp.maximum(mx[i, g], fold(jnp.max, s))
            return carry

        lax.fori_loop(0, HEADS, one, 0)

    share_pair(0)
    own_from_sibling(0)
    scale_rows(own)

    def scores_own(n, carry):
        b = tile_in_order(n)
        tile_arrived(0, b)

        @pl.when(b < n_own)
        def _():
            scores_step(own, b)

        return carry

    lax.fori_loop(0, 1, scores_own, 0)
    for copy in key_copies:
        copy.wait_send()
    share_own(1)
    share_pair(1)
    pass_on(0)
    relay(1)
    lax.fori_loop(1, CHIPS // PER, scores_own, 0)
    own_from_sibling(1)
    turn_grads(own)
    from_sibling(0)
    scale_rows(1 - own)

    def scores_other(b, carry):
        scores_step(1 - own, b)
        return carry

    lax.fori_loop(0, n_other, scores_other, 0)
    pass_on(1)

    def tile_place(t):
        g = (t >= n_hi).astype(jnp.int32)
        return g, t - g * n_hi

    def weights_step(i, g, b):
        t = b + g * n_hi
        e = jnp.exp2(s_buf[i, t] - mx[i, g, 0:1])
        tot[i, g] = tot[i, g] + fold(jnp.sum, e)
        e = e.astype(BF16)
        e_buf[i, t] = e
        o = dot(tile_of(vall, b).T, e)
        for r in (0, 1):
            o_t[i, g, r] = o_t[i, g, r] + o[:, r * ROWS : (r + 1) * ROWS]

    def weights_arriving(n, carry):
        b = tile_in_order(n)
        tile_arrived(1, b)
        pl.when(b < n_hi)(lambda: weights_step(xp, 0, b))
        pl.when(b < n_lo)(lambda: weights_step(xp, 1, b))
        return carry

    def weights_beside(n, carry):
        weights_step(1 - xp, *tile_place(n))
        return carry

    def statistics(i):
        for g in (0, 1):
            at = 4 * g
            st[i, me, at : at + 1] = mx[i, g, 0:1]
            st[i, me, at + 1 : at + 2] = jnp.sum(tot[i, g], axis=0, keepdims=True)
            o = jnp.concatenate([o_t[i, g, 0], o_t[i, g, 1]], axis=1)
            st[i, me, at + 2 : at + 3] = jnp.sum(gt[g, i].astype(F32) * o, axis=0, keepdims=True)
            st[i, me, at + 3 : at + 4] = jnp.zeros((1, PAIR), F32)
        spot = st.at[i, me]
        for slot, there in enumerate((beside(core), beside(1 - core), sibling)):
            go(remote(spot, spot, st_send.at[i, slot], st_recv.at[i, me], there))

    for i in (0, 1):
        for g in (0, 1):
            mx[i, g] = jnp.broadcast_to(jnp.max(mx[i, g], axis=0, keepdims=True), (8, PAIR))
    lax.fori_loop(0, CHIPS // PER, weights_arriving, 0)
    from_sibling(1)
    turn_grads(1 - own)
    statistics(xp)
    lax.fori_loop(0, TILES, weights_beside, 0)
    statistics(1 - xp)

    ones = jnp.ones((TILE, WIDTH), BF16)
    sub = lax.broadcasted_iota(jnp.int32, (WIDTH, PAIR), 0)

    def prepare(i):
        for other in (2 * (1 - xp), 2 * (1 - xp) + 1, 2 * xp + 1 - core):
            spot = st.at[i, other]
            remote(spot, spot, st_send.at[i, 0], st_recv.at[i, other], sibling).wait_recv()
        for g in (0, 1):
            at = 4 * g
            tops = [st[i, s, at : at + 1] for s in range(DEVS)]
            top = jnp.maximum(jnp.maximum(tops[0], tops[1]), jnp.maximum(tops[2], tops[3]))
            total = delta = jnp.zeros((1, PAIR), F32)
            for s in range(DEVS):
                by = jnp.exp2(tops[s] - top)
                total = total + by * st[i, s, at + 1 : at + 2]
                delta = delta + by * st[i, s, at + 2 : at + 3]
            inv = 1.0 / total
            factor = jnp.exp2(st[i, me, at : at + 1] - top) * inv
            delta = -delta * inv * factor
            for r in (0, 1):
                o_t[i, g, r] = o_t[i, g, r] * factor[:, r * ROWS : (r + 1) * ROWS]
            grad = (gt[g, i].astype(F32) * factor).astype(BF16)
            gpa[i, g, :WIDTH] = grad
            gp[i, g] = grad.T
            d1 = delta.astype(BF16).astype(F32)
            d2 = (delta - d1).astype(BF16).astype(F32)
            extra = jnp.where(sub == 0, d1, jnp.where(sub == 1, d2, jnp.where(sub == 2, delta - d1 - d2, 0.0)))
            gpa[i, g, WIDTH:] = extra.astype(BF16)

    parts_of = (o_t, dq_t)

    def to_core(kind, i, g):
        go(
            remote(
                parts_of[kind].at[i, g, 1 - core], core_x.at[kind, i, g],
                core_send.at[kind, i, g], core_recv.at[kind, i, g], sibling,
            )
        )

    def from_core(kind, i, g):
        spot = core_x.at[kind, i, g]
        remote(spot, spot, core_send.at[kind, i, g], core_recv.at[kind, i, g], sibling).wait_recv()
        return parts_of[kind][i, g, core] + core_x[kind, i, g]

    def to_beside(kind, g):
        xs[kind, g] = from_core(kind, 1 - xp, g).astype(BF16)
        go(remote(xs.at[kind, g], xr.at[kind, g], sum_send.at[kind, g], sum_recv.at[kind, g], beside(core)))

    def finish(kind, g):
        total = from_core(kind, xp, g)
        spot = xr.at[kind, g]
        remote(spot, spot, sum_send.at[kind, g], sum_recv.at[kind, g], sibling).wait_recv()
        total = total + xr[kind, g].astype(F32)
        if kind == 1:
            total = total * scale
        obuf[kind, g] = total.T.astype(BF16)

    def finish_own(kind):
        finish(kind, own)
        (out_ref, dq_ref)[kind][:, cols(upper)] = obuf[kind, own]

    def partner_copy(kind):
        return remote(obuf.at[kind, 1 - own], orecv.at[kind], out_send.at[kind], out_recv.at[kind], partner)

    def finish_other(kind):
        finish(kind, 1 - own)
        go(partner_copy(kind))

    def from_partner(kind):
        partner_copy(kind).wait_recv()
        (out_ref, dq_ref)[kind][:, cols(1 - upper)] = orecv[kind]

    def touched(k, j):
        return j // PER <= upper_of(k) // PER

    def first_copy(which, j):
        axis = "yz"[which]
        d = (j % N + N - y) % N if which == 0 else (j // N + N - z) % N
        index = j // N if which == 0 else j % N
        copy = remote(
            part.at[which, j], r1.at[which, d - 1, index], r1_send.at[which, j], r1_recv.at[which, d - 1, index],
            along(axis, d),
        )
        return copy, d != 0

    def each_first(j, act):
        for which in (0, 1):
            copy, needed = first_copy(which, j)
            pl.when(needed)(lambda copy=copy: act(copy))

    def send_grads(b):
        for j in [PER * b + k for k in range(PER)]:
            part[0, j] = (dkv[0, j] * scale).astype(BF16)
            part[1, j] = dkv[1, j].astype(BF16)
            each_first(j, lambda copy: copy.start())

    def grads_step(g, i, b):
        e = e_buf[i, b + g * n_hi]
        k = tile_of(kall, b)
        dp = dot(jnp.concatenate([tile_of(vall, b), ones], axis=1), gpa[i, g])
        ds = (e.astype(F32) * dp).astype(BF16)
        at = pl.ds(PER * b, PER)
        dkv[0, at] = dkv[0, at] + dot(ds, qbuf[g, i].reshape(PAIR, WIDTH)).reshape(PER, GROUP, WIDTH)
        dkv[1, at] = dkv[1, at] + dot(e, gp[i, g]).reshape(PER, GROUP, WIDTH)
        dq = dot(k.T, ds)
        for r in (0, 1):
            dq_t[i, g, r] = dq_t[i, g, r] + dq[:, r * ROWS : (r + 1) * ROWS]

    def grads_pass(i, leave):
        def lower(b, carry):
            grads_step(1, i, b)
            return carry

        def upper_tile(n, carry):
            b = (z + 1 + n) % N

            @pl.when(b < n_hi)
            def _():
                grads_step(0, i, b)
                if leave:
                    send_grads(b)

            return carry

        lax.fori_loop(0, n_lo, lower, 0)
        lax.fori_loop(0, N, upper_tile, 0)
        for g in (0, 1):
            to_core(1, i, g)

    prepare(1 - xp)
    for g in (0, 1):
        to_core(0, 1 - xp, g)
    grads_pass(1 - xp, False)
    prepare(xp)
    for g in (0, 1):
        to_core(0, xp, g)
    for kind in (0, 1):
        for g in (0, 1):
            to_beside(kind, g)
    grads_pass(xp, True)

    def second_copy(which, i):
        d = (i + N - (z if which == 0 else y)) % N
        copy = remote(
            d2.at[which, i], r2.at[which, d - 1], r2_send.at[which, i], r2_recv.at[which, d - 1],
            along("zy"[which], d),
        )
        return copy, d != 0

    def first_sum(i, carry):
        for which in (0, 1):
            j = N * i + y if which == 0 else N * z + i
            acc[...] = jnp.where(touched(chip, j), part[which, j].astype(F32), 0.0)
            for s in range(N - 1):
                k = chip_at(s + 1, 0) if which == 0 else chip_at(0, s + 1)

                @pl.when(touched(k, j))
                def _(s=s):
                    spot = r1.at[which, s, i]
                    remote(spot, spot, r1_send.at[which, 0], r1_recv.at[which, s, i], sibling).wait_recv()
                    acc[...] = acc[...] + r1[which, s, i].astype(F32)

            d2[which, i] = acc[...].astype(BF16)
            copy, needed = second_copy(which, i)
            pl.when(needed)(lambda copy=copy: copy.start())
        return carry

    lax.fori_loop(0, N, first_sum, 0)
    finish_other(1)
    for which, i in ((0, z), (1, y)):
        total = d2[which, i].astype(F32)
        for s in range(N - 1):
            spot = r2.at[which, s]
            remote(spot, spot, r2_send.at[which, 0], r2_recv.at[which, s], sibling).wait_recv()
            total = total + r2[which, s].astype(F32)
        total = total.astype(BF16)
        for half in (0, 1):
            d3[half, which] = total[half * HOME : (half + 1) * HOME]

    def third_copy(half):
        there = home(half)
        copy = remote(d3.at[half], r3.at[p // 2], r3_send.at[half], r3_recv.at[p // 2], there)
        return copy, jnp.logical_not(is_me(there))

    for half in (0, 1):
        copy, needed = third_copy(half)
        pl.when(needed)(lambda copy=copy: copy.start())
    finish_own(1)
    finish_other(0)
    finish_own(0)
    total = jnp.where(keeps, d3[core].astype(F32), 0.0)
    sums[...] = total
    for u in (0, 1):

        @pl.when(jnp.logical_not(is_me(source(u))))
        def _(u=u):
            spot = r3.at[u]
            remote(spot, spot, r3_send.at[0], r3_recv.at[u], sibling).wait_recv()
            sums[...] = sums[...] + r3[u].astype(F32)

    for which, ref in enumerate((dk_ref, dv_ref)):
        ref[...] = sums[which].astype(BF16)
    from_partner(0)
    from_partner(1)

    def sent(j, carry):
        @pl.when(j // PER < n_hi)
        def _():
            each_first(j, lambda copy: copy.wait_send())

        return carry

    lax.fori_loop(0, CHIPS, sent, 0)
    for which in (0, 1):
        for i in range(N):
            copy, needed = second_copy(which, i)
            pl.when(needed)(lambda copy=copy: copy.wait_send())
    for half in (0, 1):
        copy, needed = third_copy(half)
        pl.when(needed)(lambda copy=copy: copy.wait_send())
    for copy in started:
        copy.wait_send()


def hand_on(*refs):
    for i in range(4):
        refs[4 + i][...] = refs[i][...]


def on_device(queries, keys, values, out_grad, segment_ids):
    hbm = pl.BlockSpec(memory_space=pl.ANY)
    dma = pltpu.SemaphoreType.DMA
    vmem = pltpu.VMEM
    scratch = [
        vmem((SEQ // WIDTH, WIDTH), jnp.int32),
        vmem((CHIPS, 2, HOME, WIDTH), BF16),
        vmem((CHIPS, 2, HOME, WIDTH), BF16),
        vmem((2, HEADS, 2, ROWS, WIDTH), BF16),
        vmem((2, HEADS, 2, ROWS, WIDTH), BF16),
        vmem((HEADS, TILES, TILE, PAIR), F32),
        vmem((HEADS, TILES, TILE, PAIR), BF16),
        vmem((2, HEADS, 2 * WIDTH, PAIR), BF16),
        vmem((2, HEADS, WIDTH, PAIR), BF16),
        vmem((HEADS, 2, 2 * WIDTH, PAIR), BF16),
        vmem((HEADS, 2, PAIR, WIDTH), BF16),
        vmem((HEADS, 2, 8, PAIR), F32),
        vmem((HEADS, 2, 8, PAIR), F32),
        vmem((HEADS, 2, 2, WIDTH, ROWS), F32),
        vmem((HEADS, 2, 2, WIDTH, ROWS), F32),
        vmem((2, HEADS, 2, WIDTH, ROWS), F32),
        vmem((2, 2, WIDTH, ROWS), BF16),
        vmem((2, 2, WIDTH, ROWS), BF16),
        vmem((HEADS, DEVS, 8, PAIR), F32),
        vmem((2, 2, 1, PAIR), jnp.int32),
        vmem((2, CHIPS, GROUP, WIDTH), F32),
        vmem((2, CHIPS, GROUP, WIDTH), BF16),
        vmem((2, N - 1, N, GROUP, WIDTH), BF16),
        vmem((2, N, GROUP, WIDTH), BF16),
        vmem((2, N - 1, GROUP, WIDTH), BF16),
        vmem((2, 2, HOME, WIDTH), BF16),
        vmem((2, 2, HOME, WIDTH), BF16),
        vmem((GROUP, WIDTH), F32),
        vmem((2, HOME, WIDTH), F32),
        vmem((2, 2, ROWS, WIDTH), BF16),
        vmem((2, ROWS, WIDTH), BF16),
        dma((2, HEADS)),
        dma((3,)),
        dma((2, 32)), dma((2, CHIPS, 2)),
        dma((2,)), dma((2,)),
        dma((2,)), dma((2,)),
        dma((2,)), dma((2,)),
        dma((2, HEADS)), dma((2, HEADS)),
        dma((HEADS, 3)), dma((HEADS, DEVS)),
        dma((2, HEADS, 2)), dma((2, HEADS, 2)),
        dma((2, 2)), dma((2, 2)),
        dma((2,)), dma((2,)),
        dma((2, CHIPS)), dma((2, N - 1, N)),
        dma((2, N)), dma((2, N - 1)),
        dma((2,)), dma((2,)),
    ]
    tokens = jax.ShapeDtypeStruct((ROWS, 2 * WIDTH), BF16)
    terms = jax.ShapeDtypeStruct((HOME, WIDTH), BF16)
    results = (tokens, tokens, terms, terms)
    parts = pl.pallas_call(
        kernel,
        out_shape=[vmem(like.shape, like.dtype) for like in results],
        in_specs=[hbm] * 5,
        out_specs=[pl.BlockSpec(memory_space=vmem)] * 4,
        scratch_shapes=scratch,
        compiler_params=pltpu.CompilerParams(
            collective_id=0, has_side_effects=True, vmem_limit_bytes=56 * 1024 * 1024
        ),
    )(
        segment_ids.reshape(SEQ // WIDTH, WIDTH),
        queries,
        keys.reshape(2, 2, HOME, WIDTH),
        values.reshape(2, 2, HOME, WIDTH),
        out_grad,
    )
    return pl.pallas_call(
        hand_on,
        out_shape=results,
        in_specs=[pl.BlockSpec(memory_space=vmem)] * 4,
        out_specs=(pl.BlockSpec(memory_space=vmem),) * 4,
    )(*[pltpu.with_memory_space_constraint(part, vmem) for part in parts])


def solution(mesh):
    return jax.shard_map(
        on_device,
        mesh=mesh,
        in_specs=(P("ctx", None), P("ctx", None), P("ctx", None), P("ctx", None), P()),
        out_specs=(P("ctx", "dp"), P("ctx", "dp"), P(("dp", "ctx"), None), P(("dp", "ctx"), None)),
        check_vma=False,
    )
```

```python
import math

import jax
import jax.numpy as jnp
from jax import lax
from jax.experimental import pallas as pl
from jax.experimental.pallas import tpu as pltpu
from jax.sharding import PartitionSpec as P

F32 = jnp.float32
BF16 = jnp.bfloat16
MESH = pl.DeviceIdType.MESH

N = 4
CHIPS = N * N
ROWS = 256
PAIR = 2 * ROWS
WIDTH = 128
SEQ = PAIR * CHIPS
GROUP = 128
HOME = 64
PER = 4
TILE = PER * GROUP
TILES = 5
HEADS = 2
DEVS = 4
NEG = -1e30


def dot(a, b):
    return lax.dot_general(a, b, (((1,), (0,)), ((), ())), preferred_element_type=F32)


def kernel(
    seg_hbm, q_hbm, k_hbm, v_hbm, g_hbm,
    out_ref, dq_ref, dk_ref, dv_ref,
    seg_ref, kall, vall, qbuf, gbuf, s_buf, e_buf,
    qa, gt, gpa, gp, mx, tot, o_t, dq_t, core_x, xs, xr, st, rng, dkv,
    part, r1, d2, r2, d3, r3, acc, sums, obuf, orecv,
    load_sem, kv_sem, ag_send, ag_recv, pair_send, pair_recv, own_send, own_recv, x_send, x_recv, rel_send, rel_recv,
    st_send, st_recv, core_send, core_recv, sum_send, sum_recv, out_send, out_recv, r1_send, r1_recv, r2_send, r2_recv, r3_send, r3_recv,
):
    p = lax.axis_index("dp")
    c = lax.axis_index("ctx")
    core = c % 2
    chip = c // 2
    z = chip % N
    y = chip // N
    xp = p % 2
    me = 2 * xp + core
    neighbour = p + 1 - 2 * xp
    sibling = (p, 2 * chip + 1 - core)
    partner = (p, 2 * (CHIPS - 1 - chip) + core)
    upper = (chip >= CHIPS // 2).astype(jnp.int32)
    own = 1 - upper
    lo = jnp.minimum(chip, CHIPS - 1 - chip)
    hi = CHIPS - 1 - lo
    n_hi = hi // PER + 1
    n_lo = lo // PER + 1
    n_own = jnp.where(upper == 1, n_hi, n_lo)
    n_other = TILES - n_own

    def beside(core_):
        return (neighbour, 2 * chip + core_)

    def head_of(slot, parity):
        return 2 * (p - xp + slot) + parity

    def along(axis, d):
        there = dict(y=y, z=z)
        there[axis] = (there[axis] + d) % N
        return (p, (there["y"] * N + there["z"]) * 2 + core)

    def chip_at(dy, dz):
        return ((y + N - dy) % N) * N + (z + N - dz) % N

    def upper_of(k):
        return jnp.maximum(k, CHIPS - 1 - k)

    def cols(head):
        return pl.ds(pl.multiple_of(head * WIDTH, WIDTH), WIDTH)

    home_z = 2 * core + xp

    def home(half):
        return (z, (y * N + home_z) * 2 + half)

    def source(u):
        return (z % 2 + 2 * u, (y * N + p) * 2 + z // 2)

    def is_me(dev):
        return (dev[0] == p) & (dev[1] == c)

    keeps = (z == p) & (home_z == z)

    barrier = pltpu.get_barrier_semaphore()

    def greet(there):
        pl.semaphore_signal(barrier, inc=1, device_id=there, device_id_type=MESH)

    for d in range(1, N):
        for axis in "yz":
            greet(along(axis, d))
    for there in (partner, beside(core), beside(1 - core), sibling):
        greet(there)
    for u in (0, 1):
        pl.when(jnp.logical_not(is_me(source(u))))(lambda u=u: greet(source(u)))

    kv_loads = [
        pltpu.make_async_copy(src.at[xp], dst.at[chip], kv_sem.at[i])
        for i, (src, dst) in enumerate(((k_hbm, kall), (v_hbm, vall)))
    ]
    arrays = ((q_hbm, qbuf), (g_hbm, gbuf))
    loads = [
        pltpu.make_async_copy(src.at[:, cols(head_of(i, upper))], buf.at[own, i, core], load_sem.at[a, i])
        for a, (src, buf) in enumerate(arrays)
        for i in range(HEADS)
    ]
    seg_load = pltpu.make_async_copy(seg_hbm, seg_ref, kv_sem.at[2])
    for copy in kv_loads + loads + [seg_load]:
        copy.start()
    started = []

    def remote(src, dst, send, recv, there):
        return pltpu.make_async_remote_copy(
            src_ref=src, dst_ref=dst, send_sem=send, recv_sem=recv, device_id=there, device_id_type=MESH
        )

    def go(copy):
        copy.start()
        started.append(copy)
        return copy

    whole = (kall, vall)
    count = [0, 0]
    key_copies = []

    def push(which, block, half, there):
        spot = whole[which].at[block, half]
        copy = remote(spot, spot, ag_send.at[which, count[which]], ag_recv.at[which, block, half], there)
        count[which] += 1
        if which == 0:
            copy.start()
            key_copies.append(copy)
        else:
            go(copy)

    def arrived(which, block, half):
        spot = whole[which].at[block, half]
        remote(spot, spot, ag_send.at[which, 0], ag_recv.at[which, block, half], sibling).wait_recv()

    def push_mine(which):
        for axes in ("yz", "zy"):
            for d in (1, 3, 2):
                for half in (0, 1):
                    push(which, chip, half, along(axes[half], d))

    def relay(which):
        for d in (1, 3, 2):
            for half, block in ((0, chip_at(d, 0)), (1, chip_at(0, d))):
                arrived(which, block, half)
                for d2 in (1, 3, 2):
                    push(which, block, half, along("zy"[half], d2))

    def tile_in_order(n):
        return (y + jnp.where(n == 2, 3, jnp.where(n == 3, 2, n))) % N

    def tile_arrived(which, b):
        for i in range(PER):
            j = PER * b + i
            pl.when(z != i)(lambda j=j: arrived(which, j, 0))
            pl.when(b != y)(lambda j=j: arrived(which, j, 1))

    def pair_copy(a):
        src, buf = arrays[a]
        src = src.at[:, cols(2 * p + 1 - upper)]
        return remote(src, buf.at[own, xp, core], pair_send.at[a], pair_recv.at[a], partner)

    def share_own(a):
        spot = arrays[a][1].at[own, :, core]
        for i in range(HEADS):
            loads[HEADS * a + i].wait()
        go(remote(spot, spot, own_send.at[a], own_recv.at[a], sibling))

    def to_sibling(a, slot):
        spot = arrays[a][1].at[1 - own, slot, core]
        go(remote(spot, spot, rel_send.at[a, slot], rel_recv.at[a, slot], sibling))

    def share_pair(a):
        spot = arrays[a][1].at[1 - own, xp, core]
        remote(spot, spot, pair_send.at[a], pair_recv.at[a], partner).wait_recv()
        go(remote(spot, spot, x_send.at[a], x_recv.at[a], beside(core)))
        to_sibling(a, xp)

    def pass_on(a):
        spot = arrays[a][1].at[1 - own, 1 - xp, core]
        remote(spot, spot, x_send.at[a], x_recv.at[a], sibling).wait_recv()
        to_sibling(a, 1 - xp)

    def from_sibling(a):
        for i in range(HEADS):
            spot = arrays[a][1].at[1 - own, i, 1 - core]
            remote(spot, spot, rel_send.at[a, 0], rel_recv.at[a, i], sibling).wait_recv()

    def own_from_sibling(a):
        spot = arrays[a][1].at[own, :, 1 - core]
        remote(spot, spot, own_send.at[a], own_recv.at[a], sibling).wait_recv()

    pl.semaphore_wait(barrier, 12 - keeps.astype(jnp.int32))
    go(pair_copy(0))
    kv_loads[0].wait()
    push_mine(0)
    share_own(0)
    go(pair_copy(1))
    relay(0)
    kv_loads[1].wait()
    push_mine(1)

    scale = WIDTH**-0.5
    seg_load.wait()
    seg = seg_ref[...]
    starts = [jnp.sum((seg < doc).astype(jnp.int32), axis=(0, 1), keepdims=True) for doc in (1, 2, 3)]
    lane = lax.broadcasted_iota(jnp.int32, (1, WIDTH), 1)
    for g, block in ((0, hi), (1, lo)):
        for i in range(PAIR // WIDTH):
            ids = seg_ref[pl.ds(block * (PAIR // WIDTH) + i, 1), :]
            start = jnp.where(
                ids == 0, 0, jnp.where(ids == 1, starts[0], jnp.where(ids == 2, starts[1], starts[2]))
            )
            rng[g, 0, :, i * WIDTH : (i + 1) * WIDTH] = start
            rng[g, 1, :, i * WIDTH : (i + 1) * WIDTH] = block * PAIR + i * WIDTH + lane
    mx[...] = jnp.full_like(mx, NEG)
    tot[...] = jnp.zeros_like(tot)

    def clear(i, carry):
        for ref in (o_t, dq_t):
            ref[i] = jnp.zeros_like(ref[i])
        return carry

    lax.fori_loop(0, HEADS, clear, 0)

    def clear_block(j, carry):
        for which in (0, 1):
            dkv[which, j] = jnp.zeros((GROUP, WIDTH), F32)
        return carry

    lax.fori_loop(0, CHIPS, clear_block, 0)

    def scale_rows(g):
        def one(i, carry):
            for r in (0, 1):
                at = slice(r * ROWS, (r + 1) * ROWS)
                scaled = qbuf[g, i, r].astype(F32).T * (scale * math.log2(math.e))
                high = scaled.astype(BF16)
                qa[g, i, :WIDTH, at] = high
                qa[g, i, WIDTH:, at] = (scaled - high.astype(F32)).astype(BF16)
            return carry

        lax.fori_loop(0, HEADS, one, 0)

    def turn_grads(g):
        def one(i, carry):
            for r in (0, 1):
                gt[g, i, :, r * ROWS : (r + 1) * ROWS] = gbuf[g, i, r].T
            return carry

        lax.fori_loop(0, HEADS, one, 0)

    row = lax.broadcasted_iota(jnp.int32, (TILE, PAIR), 0)
    token = PAIR * (row // GROUP) + row % GROUP + ROWS * core + GROUP * xp

    def tile_of(ref, b):
        return ref[pl.ds(PER * b, PER)].reshape(TILE, WIDTH)

    def fold(op, values):
        return op(values.reshape(TILE // 8, 8, PAIR), axis=0)

    def scores_step(g, b):
        k = tile_of(kall, b)
        k = jnp.concatenate([k, k], axis=1)
        key = token + b * (PER * PAIR)
        seen = (key >= rng[g, 0]) & (key <= rng[g, 1])

        def one(i, carry):
            s = jnp.where(seen, dot(k, qa[g, i]), NEG)
            s_buf[i, b + g * n_hi] = s
            mx[i, g] = jnp.maximum(mx[i, g], fold(jnp.max, s))
            return carry

        lax.fori_loop(0, HEADS, one, 0)

    share_pair(0)
    own_from_sibling(0)
    scale_rows(own)

    def scores_own(n, carry):
        b = tile_in_order(n)
        tile_arrived(0, b)

        @pl.when(b < n_own)
        def _():
            scores_step(own, b)

        return carry

    lax.fori_loop(0, 1, scores_own, 0)
    for copy in key_copies:
        copy.wait_send()
    share_own(1)
    share_pair(1)
    pass_on(0)
    relay(1)
    lax.fori_loop(1, CHIPS // PER, scores_own, 0)
    own_from_sibling(1)
    turn_grads(own)
    from_sibling(0)
    scale_rows(1 - own)

    def scores_other(b, carry):
        scores_step(1 - own, b)
        return carry

    lax.fori_loop(0, n_other, scores_other, 0)
    pass_on(1)

    def tile_place(t):
        g = (t >= n_hi).astype(jnp.int32)
        return g, t - g * n_hi

    def weights_step(i, g, b):
        t = b + g * n_hi
        e = jnp.exp2(s_buf[i, t] - mx[i, g, 0:1])
        tot[i, g] = tot[i, g] + fold(jnp.sum, e)
        e = e.astype(BF16)
        e_buf[i, t] = e
        o = dot(tile_of(vall, b).T, e)
        for r in (0, 1):
            o_t[i, g, r] = o_t[i, g, r] + o[:, r * ROWS : (r + 1) * ROWS]

    def weights_arriving(n, carry):
        b = tile_in_order(n)
        tile_arrived(1, b)
        pl.when(b < n_hi)(lambda: weights_step(xp, 0, b))
        pl.when(b < n_lo)(lambda: weights_step(xp, 1, b))
        return carry

    def weights_beside(n, carry):
        weights_step(1 - xp, *tile_place(n))
        return carry

    def statistics(i):
        for g in (0, 1):
            at = 4 * g
            st[i, me, at : at + 1] = mx[i, g, 0:1]
            st[i, me, at + 1 : at + 2] = jnp.sum(tot[i, g], axis=0, keepdims=True)
            o = jnp.concatenate([o_t[i, g, 0], o_t[i, g, 1]], axis=1)
            st[i, me, at + 2 : at + 3] = jnp.sum(gt[g, i].astype(F32) * o, axis=0, keepdims=True)
            st[i, me, at + 3 : at + 4] = jnp.zeros((1, PAIR), F32)
        spot = st.at[i, me]
        for slot, there in enumerate((beside(core), beside(1 - core), sibling)):
            go(remote(spot, spot, st_send.at[i, slot], st_recv.at[i, me], there))

    for i in (0, 1):
        for g in (0, 1):
            mx[i, g] = jnp.broadcast_to(jnp.max(mx[i, g], axis=0, keepdims=True), (8, PAIR))
    lax.fori_loop(0, CHIPS // PER, weights_arriving, 0)
    from_sibling(1)
    turn_grads(1 - own)
    statistics(xp)
    lax.fori_loop(0, TILES, weights_beside, 0)
    statistics(1 - xp)

    ones = jnp.ones((TILE, WIDTH), BF16)
    sub = lax.broadcasted_iota(jnp.int32, (WIDTH, PAIR), 0)

    def prepare(i):
        for other in (2 * (1 - xp), 2 * (1 - xp) + 1, 2 * xp + 1 - core):
            spot = st.at[i, other]
            remote(spot, spot, st_send.at[i, 0], st_recv.at[i, other], sibling).wait_recv()
        for g in (0, 1):
            at = 4 * g
            tops = [st[i, s, at : at + 1] for s in range(DEVS)]
            top = jnp.maximum(jnp.maximum(tops[0], tops[1]), jnp.maximum(tops[2], tops[3]))
            total = delta = jnp.zeros((1, PAIR), F32)
            for s in range(DEVS):
                by = jnp.exp2(tops[s] - top)
                total = total + by * st[i, s, at + 1 : at + 2]
                delta = delta + by * st[i, s, at + 2 : at + 3]
            inv = 1.0 / total
            factor = jnp.exp2(st[i, me, at : at + 1] - top) * inv
            delta = -delta * inv * factor
            for r in (0, 1):
                o_t[i, g, r] = o_t[i, g, r] * factor[:, r * ROWS : (r + 1) * ROWS]
            grad = (gt[g, i].astype(F32) * factor).astype(BF16)
            gpa[i, g, :WIDTH] = grad
            gp[i, g] = grad.T
            d1 = delta.astype(BF16).astype(F32)
            d2 = (delta - d1).astype(BF16).astype(F32)
            extra = jnp.where(sub == 0, d1, jnp.where(sub == 1, d2, jnp.where(sub == 2, delta - d1 - d2, 0.0)))
            gpa[i, g, WIDTH:] = extra.astype(BF16)

    parts_of = (o_t, dq_t)

    def to_core(kind, i, g):
        go(
            remote(
                parts_of[kind].at[i, g, 1 - core], core_x.at[kind, i, g],
                core_send.at[kind, i, g], core_recv.at[kind, i, g], sibling,
            )
        )

    def from_core(kind, i, g):
        spot = core_x.at[kind, i, g]
        remote(spot, spot, core_send.at[kind, i, g], core_recv.at[kind, i, g], sibling).wait_recv()
        return parts_of[kind][i, g, core] + core_x[kind, i, g]

    def to_beside(kind, g):
        xs[kind, g] = from_core(kind, 1 - xp, g).astype(BF16)
        go(remote(xs.at[kind, g], xr.at[kind, g], sum_send.at[kind, g], sum_recv.at[kind, g], beside(core)))

    def finish(kind, g):
        total = from_core(kind, xp, g)
        spot = xr.at[kind, g]
        remote(spot, spot, sum_send.at[kind, g], sum_recv.at[kind, g], sibling).wait_recv()
        total = total + xr[kind, g].astype(F32)
        if kind == 1:
            total = total * scale
        obuf[kind, g] = total.T.astype(BF16)

    def finish_own(kind):
        finish(kind, own)
        (out_ref, dq_ref)[kind][:, cols(upper)] = obuf[kind, own]

    def partner_copy(kind):
        return remote(obuf.at[kind, 1 - own], orecv.at[kind], out_send.at[kind], out_recv.at[kind], partner)

    def finish_other(kind):
        finish(kind, 1 - own)
        go(partner_copy(kind))

    def from_partner(kind):
        partner_copy(kind).wait_recv()
        (out_ref, dq_ref)[kind][:, cols(1 - upper)] = orecv[kind]

    def touched(k, j):
        return j // PER <= upper_of(k) // PER

    def first_copy(which, j):
        axis = "yz"[which]
        d = (j % N + N - y) % N if which == 0 else (j // N + N - z) % N
        index = j // N if which == 0 else j % N
        copy = remote(
            part.at[which, j], r1.at[which, d - 1, index], r1_send.at[which, j], r1_recv.at[which, d - 1, index],
            along(axis, d),
        )
        return copy, d != 0

    def each_first(j, act):
        for which in (0, 1):
            copy, needed = first_copy(which, j)
            pl.when(needed)(lambda copy=copy: act(copy))

    def send_grads(b):
        for j in [PER * b + k for k in range(PER)]:
            part[0, j] = (dkv[0, j] * scale).astype(BF16)
            part[1, j] = dkv[1, j].astype(BF16)
            each_first(j, lambda copy: copy.start())

    def grads_step(g, i, b):
        e = e_buf[i, b + g * n_hi]
        k = tile_of(kall, b)
        dp = dot(jnp.concatenate([tile_of(vall, b), ones], axis=1), gpa[i, g])
        ds = (e.astype(F32) * dp).astype(BF16)
        at = pl.ds(PER * b, PER)
        dkv[0, at] = dkv[0, at] + dot(ds, qbuf[g, i].reshape(PAIR, WIDTH)).reshape(PER, GROUP, WIDTH)
        dkv[1, at] = dkv[1, at] + dot(e, gp[i, g]).reshape(PER, GROUP, WIDTH)
        dq = dot(k.T, ds)
        for r in (0, 1):
            dq_t[i, g, r] = dq_t[i, g, r] + dq[:, r * ROWS : (r + 1) * ROWS]

    def grads_pass(i, leave):
        def lower(b, carry):
            grads_step(1, i, b)
            return carry

        def upper_tile(n, carry):
            b = (z + 1 + n) % N

            @pl.when(b < n_hi)
            def _():
                grads_step(0, i, b)
                if leave:
                    send_grads(b)

            return carry

        lax.fori_loop(0, n_lo, lower, 0)
        if leave:
            for g in (0, 1):
                to_beside(1, g)
        lax.fori_loop(0, N, upper_tile, 0)
        for g in (0, 1):
            to_core(1, i, g)

    prepare(1 - xp)
    for g in (0, 1):
        to_core(0, 1 - xp, g)
    grads_pass(1 - xp, False)
    prepare(xp)
    for g in (0, 1):
        to_core(0, xp, g)
    for g in (0, 1):
        to_beside(0, g)
    grads_pass(xp, True)

    def second_copy(which, i):
        d = (i + N - (z if which == 0 else y)) % N
        copy = remote(
            d2.at[which, i], r2.at[which, d - 1], r2_send.at[which, i], r2_recv.at[which, d - 1],
            along("zy"[which], d),
        )
        return copy, d != 0

    def first_sum(i, carry):
        for which in (0, 1):
            j = N * i + y if which == 0 else N * z + i
            acc[...] = jnp.where(touched(chip, j), part[which, j].astype(F32), 0.0)
            for s in range(N - 1):
                k = chip_at(s + 1, 0) if which == 0 else chip_at(0, s + 1)

                @pl.when(touched(k, j))
                def _(s=s):
                    spot = r1.at[which, s, i]
                    remote(spot, spot, r1_send.at[which, 0], r1_recv.at[which, s, i], sibling).wait_recv()
                    acc[...] = acc[...] + r1[which, s, i].astype(F32)

            d2[which, i] = acc[...].astype(BF16)
            copy, needed = second_copy(which, i)
            pl.when(needed)(lambda copy=copy: copy.start())
        return carry

    lax.fori_loop(0, N, first_sum, 0)
    finish_other(1)
    finish_other(0)
    for which, i in ((0, z), (1, y)):
        total = d2[which, i].astype(F32)
        for s in range(N - 1):
            spot = r2.at[which, s]
            remote(spot, spot, r2_send.at[which, 0], r2_recv.at[which, s], sibling).wait_recv()
            total = total + r2[which, s].astype(F32)
        total = total.astype(BF16)
        for half in (0, 1):
            d3[half, which] = total[half * HOME : (half + 1) * HOME]

    def third_copy(half):
        there = home(half)
        copy = remote(d3.at[half], r3.at[p // 2], r3_send.at[half], r3_recv.at[p // 2], there)
        return copy, jnp.logical_not(is_me(there))

    for half in (0, 1):
        copy, needed = third_copy(half)
        pl.when(needed)(lambda copy=copy: copy.start())
    finish_own(1)
    finish_own(0)
    total = jnp.where(keeps, d3[core].astype(F32), 0.0)
    sums[...] = total
    for u in (0, 1):

        @pl.when(jnp.logical_not(is_me(source(u))))
        def _(u=u):
            spot = r3.at[u]
            remote(spot, spot, r3_send.at[0], r3_recv.at[u], sibling).wait_recv()
            sums[...] = sums[...] + r3[u].astype(F32)

    for which, ref in enumerate((dk_ref, dv_ref)):
        ref[...] = sums[which].astype(BF16)
    from_partner(0)
    from_partner(1)

    def sent(j, carry):
        @pl.when(j // PER < n_hi)
        def _():
            each_first(j, lambda copy: copy.wait_send())

        return carry

    lax.fori_loop(0, CHIPS, sent, 0)
    for which in (0, 1):
        for i in range(N):
            copy, needed = second_copy(which, i)
            pl.when(needed)(lambda copy=copy: copy.wait_send())
    for half in (0, 1):
        copy, needed = third_copy(half)
        pl.when(needed)(lambda copy=copy: copy.wait_send())
    for copy in started:
        copy.wait_send()


def hand_on(*refs):
    for i in range(4):
        refs[4 + i][...] = refs[i][...]


def on_device(queries, keys, values, out_grad, segment_ids):
    hbm = pl.BlockSpec(memory_space=pl.ANY)
    dma = pltpu.SemaphoreType.DMA
    vmem = pltpu.VMEM
    scratch = [
        vmem((SEQ // WIDTH, WIDTH), jnp.int32),
        vmem((CHIPS, 2, HOME, WIDTH), BF16),
        vmem((CHIPS, 2, HOME, WIDTH), BF16),
        vmem((2, HEADS, 2, ROWS, WIDTH), BF16),
        vmem((2, HEADS, 2, ROWS, WIDTH), BF16),
        vmem((HEADS, TILES, TILE, PAIR), F32),
        vmem((HEADS, TILES, TILE, PAIR), BF16),
        vmem((2, HEADS, 2 * WIDTH, PAIR), BF16),
        vmem((2, HEADS, WIDTH, PAIR), BF16),
        vmem((HEADS, 2, 2 * WIDTH, PAIR), BF16),
        vmem((HEADS, 2, PAIR, WIDTH), BF16),
        vmem((HEADS, 2, 8, PAIR), F32),
        vmem((HEADS, 2, 8, PAIR), F32),
        vmem((HEADS, 2, 2, WIDTH, ROWS), F32),
        vmem((HEADS, 2, 2, WIDTH, ROWS), F32),
        vmem((2, HEADS, 2, WIDTH, ROWS), F32),
        vmem((2, 2, WIDTH, ROWS), BF16),
        vmem((2, 2, WIDTH, ROWS), BF16),
        vmem((HEADS, DEVS, 8, PAIR), F32),
        vmem((2, 2, 1, PAIR), jnp.int32),
        vmem((2, CHIPS, GROUP, WIDTH), F32),
        vmem((2, CHIPS, GROUP, WIDTH), BF16),
        vmem((2, N - 1, N, GROUP, WIDTH), BF16),
        vmem((2, N, GROUP, WIDTH), BF16),
        vmem((2, N - 1, GROUP, WIDTH), BF16),
        vmem((2, 2, HOME, WIDTH), BF16),
        vmem((2, 2, HOME, WIDTH), BF16),
        vmem((GROUP, WIDTH), F32),
        vmem((2, HOME, WIDTH), F32),
        vmem((2, 2, ROWS, WIDTH), BF16),
        vmem((2, ROWS, WIDTH), BF16),
        dma((2, HEADS)),
        dma((3,)),
        dma((2, 32)), dma((2, CHIPS, 2)),
        dma((2,)), dma((2,)),
        dma((2,)), dma((2,)),
        dma((2,)), dma((2,)),
        dma((2, HEADS)), dma((2, HEADS)),
        dma((HEADS, 3)), dma((HEADS, DEVS)),
        dma((2, HEADS, 2)), dma((2, HEADS, 2)),
        dma((2, 2)), dma((2, 2)),
        dma((2,)), dma((2,)),
        dma((2, CHIPS)), dma((2, N - 1, N)),
        dma((2, N)), dma((2, N - 1)),
        dma((2,)), dma((2,)),
    ]
    tokens = jax.ShapeDtypeStruct((ROWS, 2 * WIDTH), BF16)
    terms = jax.ShapeDtypeStruct((HOME, WIDTH), BF16)
    results = (tokens, tokens, terms, terms)
    parts = pl.pallas_call(
        kernel,
        out_shape=[vmem(like.shape, like.dtype) for like in results],
        in_specs=[hbm] * 5,
        out_specs=[pl.BlockSpec(memory_space=vmem)] * 4,
        scratch_shapes=scratch,
        compiler_params=pltpu.CompilerParams(
            collective_id=0, has_side_effects=True, vmem_limit_bytes=56 * 1024 * 1024
        ),
    )(
        segment_ids.reshape(SEQ // WIDTH, WIDTH),
        queries,
        keys.reshape(2, 2, HOME, WIDTH),
        values.reshape(2, 2, HOME, WIDTH),
        out_grad,
    )
    return pl.pallas_call(
        hand_on,
        out_shape=results,
        in_specs=[pl.BlockSpec(memory_space=vmem)] * 4,
        out_specs=(pl.BlockSpec(memory_space=vmem),) * 4,
    )(*[pltpu.with_memory_space_constraint(part, vmem) for part in parts])


def solution(mesh):
    return jax.shard_map(
        on_device,
        mesh=mesh,
        in_specs=(P("ctx", None), P("ctx", None), P("ctx", None), P("ctx", None), P()),
        out_specs=(P("ctx", "dp"), P("ctx", "dp"), P(("dp", "ctx"), None), P(("dp", "ctx"), None)),
        check_vma=False,
    )
```

```python
import math

import jax
import jax.numpy as jnp
from jax import lax
from jax.experimental import pallas as pl
from jax.experimental.pallas import tpu as pltpu
from jax.sharding import PartitionSpec as P

F32 = jnp.float32
BF16 = jnp.bfloat16
MESH = pl.DeviceIdType.MESH

N = 4
CHIPS = N * N
ROWS = 256
PAIR = 2 * ROWS
WIDTH = 128
SEQ = PAIR * CHIPS
GROUP = 128
HOME = 64
PER = 4
TILE = PER * GROUP
TILES = 5
HEADS = 2
DEVS = 4
NEG = -1e30


def dot(a, b):
    return lax.dot_general(a, b, (((1,), (0,)), ((), ())), preferred_element_type=F32)


def kernel(
    seg_hbm, q_hbm, k_hbm, v_hbm, g_hbm,
    out_ref, dq_ref, dk_ref, dv_ref,
    seg_ref, kall, vall, qbuf, gbuf, s_buf, e_buf,
    qa, gt, gpa, gp, mx, tot, o_t, dq_t, core_x, xs, xr, st, rng, dkv,
    part, r1, d2, r2, d3, r3, acc, sums, obuf, orecv,
    load_sem, kv_sem, ag_send, ag_recv, pair_send, pair_recv, own_send, own_recv, x_send, x_recv, rel_send, rel_recv,
    st_send, st_recv, core_send, core_recv, sum_send, sum_recv, out_send, out_recv, r1_send, r1_recv, r2_send, r2_recv, r3_send, r3_recv,
):
    p = lax.axis_index("dp")
    c = lax.axis_index("ctx")
    core = c % 2
    chip = c // 2
    z = chip % N
    y = chip // N
    xp = p % 2
    me = 2 * xp + core
    neighbour = p + 1 - 2 * xp
    sibling = (p, 2 * chip + 1 - core)
    partner = (p, 2 * (CHIPS - 1 - chip) + core)
    upper = (chip >= CHIPS // 2).astype(jnp.int32)
    own = 1 - upper
    lo = jnp.minimum(chip, CHIPS - 1 - chip)
    hi = CHIPS - 1 - lo
    n_hi = hi // PER + 1
    n_lo = lo // PER + 1
    n_own = jnp.where(upper == 1, n_hi, n_lo)
    n_other = TILES - n_own

    def beside(core_):
        return (neighbour, 2 * chip + core_)

    def head_of(slot, parity):
        return 2 * (p - xp + slot) + parity

    def along(axis, d):
        there = dict(y=y, z=z)
        there[axis] = (there[axis] + d) % N
        return (p, (there["y"] * N + there["z"]) * 2 + core)

    def chip_at(dy, dz):
        return ((y + N - dy) % N) * N + (z + N - dz) % N

    def upper_of(k):
        return jnp.maximum(k, CHIPS - 1 - k)

    def cols(head):
        return pl.ds(pl.multiple_of(head * WIDTH, WIDTH), WIDTH)

    home_z = 2 * core + xp

    def home(half):
        return (z, (y * N + home_z) * 2 + half)

    def source(u):
        return (z % 2 + 2 * u, (y * N + p) * 2 + z // 2)

    def is_me(dev):
        return (dev[0] == p) & (dev[1] == c)

    keeps = (z == p) & (home_z == z)

    barrier = pltpu.get_barrier_semaphore()

    def greet(there):
        pl.semaphore_signal(barrier, inc=1, device_id=there, device_id_type=MESH)

    for d in range(1, N):
        for axis in "yz":
            greet(along(axis, d))
    for there in (partner, beside(core), beside(1 - core), sibling):
        greet(there)
    for u in (0, 1):
        pl.when(jnp.logical_not(is_me(source(u))))(lambda u=u: greet(source(u)))

    kv_loads = [
        pltpu.make_async_copy(src.at[xp], dst.at[chip], kv_sem.at[i])
        for i, (src, dst) in enumerate(((k_hbm, kall), (v_hbm, vall)))
    ]
    arrays = ((q_hbm, qbuf), (g_hbm, gbuf))
    loads = [
        pltpu.make_async_copy(src.at[:, cols(head_of(i, upper))], buf.at[own, i, core], load_sem.at[a, i])
        for a, (src, buf) in enumerate(arrays)
        for i in range(HEADS)
    ]
    seg_load = pltpu.make_async_copy(seg_hbm, seg_ref, kv_sem.at[2])
    for copy in kv_loads + loads + [seg_load]:
        copy.start()
    started = []

    def remote(src, dst, send, recv, there):
        return pltpu.make_async_remote_copy(
            src_ref=src, dst_ref=dst, send_sem=send, recv_sem=recv, device_id=there, device_id_type=MESH
        )

    def go(copy):
        copy.start()
        started.append(copy)
        return copy

    whole = (kall, vall)
    count = [0, 0]
    key_copies = []

    def push(which, block, half, there):
        spot = whole[which].at[block, half]
        copy = remote(spot, spot, ag_send.at[which, count[which]], ag_recv.at[which, block, half], there)
        count[which] += 1
        if which == 0:
            copy.start()
            key_copies.append(copy)
        else:
            go(copy)

    def arrived(which, block, half):
        spot = whole[which].at[block, half]
        remote(spot, spot, ag_send.at[which, 0], ag_recv.at[which, block, half], sibling).wait_recv()

    def push_mine(which):
        for axes in ("yz", "zy"):
            for d in (1, 3, 2):
                for half in (0, 1):
                    push(which, chip, half, along(axes[half], d))

    def relay(which):
        for d in (1, 3, 2):
            for half, block in ((0, chip_at(d, 0)), (1, chip_at(0, d))):
                arrived(which, block, half)
                for d2 in (1, 3, 2):
                    push(which, block, half, along("zy"[half], d2))

    def tile_in_order(n):
        return (y + jnp.where(n == 2, 3, jnp.where(n == 3, 2, n))) % N

    def tile_arrived(which, b):
        for i in range(PER):
            j = PER * b + i
            pl.when(z != i)(lambda j=j: arrived(which, j, 0))
            pl.when(b != y)(lambda j=j: arrived(which, j, 1))

    def pair_copy(a):
        src, buf = arrays[a]
        src = src.at[:, cols(2 * p + 1 - upper)]
        return remote(src, buf.at[own, xp, core], pair_send.at[a], pair_recv.at[a], partner)

    def share_own(a):
        spot = arrays[a][1].at[own, :, core]
        for i in range(HEADS):
            loads[HEADS * a + i].wait()
        go(remote(spot, spot, own_send.at[a], own_recv.at[a], sibling))

    def to_sibling(a, slot):
        spot = arrays[a][1].at[1 - own, slot, core]
        go(remote(spot, spot, rel_send.at[a, slot], rel_recv.at[a, slot], sibling))

    def share_pair(a):
        spot = arrays[a][1].at[1 - own, xp, core]
        remote(spot, spot, pair_send.at[a], pair_recv.at[a], partner).wait_recv()
        go(remote(spot, spot, x_send.at[a], x_recv.at[a], beside(core)))
        to_sibling(a, xp)

    def pass_on(a):
        spot = arrays[a][1].at[1 - own, 1 - xp, core]
        remote(spot, spot, x_send.at[a], x_recv.at[a], sibling).wait_recv()
        to_sibling(a, 1 - xp)

    def from_sibling(a):
        for i in range(HEADS):
            spot = arrays[a][1].at[1 - own, i, 1 - core]
            remote(spot, spot, rel_send.at[a, 0], rel_recv.at[a, i], sibling).wait_recv()

    def own_from_sibling(a):
        spot = arrays[a][1].at[own, :, 1 - core]
        remote(spot, spot, own_send.at[a], own_recv.at[a], sibling).wait_recv()

    pl.semaphore_wait(barrier, 12 - keeps.astype(jnp.int32))
    go(pair_copy(0))
    kv_loads[0].wait()
    push_mine(0)
    share_own(0)
    go(pair_copy(1))
    relay(0)
    kv_loads[1].wait()
    push_mine(1)

    scale = WIDTH**-0.5
    seg_load.wait()
    seg = seg_ref[...]
    starts = [jnp.sum((seg < doc).astype(jnp.int32), axis=(0, 1), keepdims=True) for doc in (1, 2, 3)]
    lane = lax.broadcasted_iota(jnp.int32, (1, WIDTH), 1)
    for g, block in ((0, hi), (1, lo)):
        for i in range(PAIR // WIDTH):
            ids = seg_ref[pl.ds(block * (PAIR // WIDTH) + i, 1), :]
            start = jnp.where(
                ids == 0, 0, jnp.where(ids == 1, starts[0], jnp.where(ids == 2, starts[1], starts[2]))
            )
            rng[g, 0, :, i * WIDTH : (i + 1) * WIDTH] = start
            rng[g, 1, :, i * WIDTH : (i + 1) * WIDTH] = block * PAIR + i * WIDTH + lane
    mx[...] = jnp.full_like(mx, NEG)
    tot[...] = jnp.zeros_like(tot)

    def clear(i, carry):
        for ref in (o_t, dq_t):
            ref[i] = jnp.zeros_like(ref[i])
        return carry

    lax.fori_loop(0, HEADS, clear, 0)

    def clear_block(j, carry):
        for which in (0, 1):
            dkv[which, j] = jnp.zeros((GROUP, WIDTH), F32)
        return carry

    lax.fori_loop(0, CHIPS, clear_block, 0)

    def scale_rows(g):
        def one(i, carry):
            for r in (0, 1):
                at = slice(r * ROWS, (r + 1) * ROWS)
                scaled = qbuf[g, i, r].astype(F32).T * (scale * math.log2(math.e))
                high = scaled.astype(BF16)
                qa[g, i, :WIDTH, at] = high
                qa[g, i, WIDTH:, at] = (scaled - high.astype(F32)).astype(BF16)
            return carry

        lax.fori_loop(0, HEADS, one, 0)

    def turn_grads(g):
        def one(i, carry):
            for r in (0, 1):
                gt[g, i, :, r * ROWS : (r + 1) * ROWS] = gbuf[g, i, r].T
            return carry

        lax.fori_loop(0, HEADS, one, 0)

    row = lax.broadcasted_iota(jnp.int32, (TILE, PAIR), 0)
    token = PAIR * (row // GROUP) + row % GROUP + ROWS * core + GROUP * xp

    def tile_of(ref, b):
        return ref[pl.ds(PER * b, PER)].reshape(TILE, WIDTH)

    def fold(op, values):
        return op(values.reshape(TILE // 8, 8, PAIR), axis=0)

    def scores_step(g, b):
        k = tile_of(kall, b)
        k = jnp.concatenate([k, k], axis=1)
        key = token + b * (PER * PAIR)
        seen = (key >= rng[g, 0]) & (key <= rng[g, 1])

        def one(i, carry):
            s = jnp.where(seen, dot(k, qa[g, i]), NEG)
            s_buf[i, b + g * n_hi] = s
            mx[i, g] = jnp.maximum(mx[i, g], fold(jnp.max, s))
            return carry

        lax.fori_loop(0, HEADS, one, 0)

    share_pair(0)
    own_from_sibling(0)
    scale_rows(own)

    def scores_own(n, carry):
        b = tile_in_order(n)
        tile_arrived(0, b)

        @pl.when(b < n_own)
        def _():
            scores_step(own, b)

        return carry

    lax.fori_loop(0, 1, scores_own, 0)
    for copy in key_copies:
        copy.wait_send()
    share_own(1)
    share_pair(1)
    pass_on(0)
    relay(1)
    lax.fori_loop(1, CHIPS // PER, scores_own, 0)
    own_from_sibling(1)
    turn_grads(own)
    from_sibling(0)
    scale_rows(1 - own)

    def scores_other(b, carry):
        scores_step(1 - own, b)
        return carry

    lax.fori_loop(0, n_other, scores_other, 0)
    pass_on(1)

    def tile_place(t):
        g = (t >= n_hi).astype(jnp.int32)
        return g, t - g * n_hi

    def weights_step(i, g, b):
        t = b + g * n_hi
        e = jnp.exp2(s_buf[i, t] - mx[i, g, 0:1])
        tot[i, g] = tot[i, g] + fold(jnp.sum, e)
        e = e.astype(BF16)
        e_buf[i, t] = e
        o = dot(tile_of(vall, b).T, e)
        for r in (0, 1):
            o_t[i, g, r] = o_t[i, g, r] + o[:, r * ROWS : (r + 1) * ROWS]

    def weights_arriving(n, carry):
        b = tile_in_order(n)
        tile_arrived(1, b)
        pl.when(b < n_hi)(lambda: weights_step(xp, 0, b))
        pl.when(b < n_lo)(lambda: weights_step(xp, 1, b))
        return carry

    def weights_beside(n, carry):
        weights_step(1 - xp, *tile_place(n))
        return carry

    def statistics(i):
        for g in (0, 1):
            at = 4 * g
            st[i, me, at : at + 1] = mx[i, g, 0:1]
            st[i, me, at + 1 : at + 2] = jnp.sum(tot[i, g], axis=0, keepdims=True)
            o = jnp.concatenate([o_t[i, g, 0], o_t[i, g, 1]], axis=1)
            st[i, me, at + 2 : at + 3] = jnp.sum(gt[g, i].astype(F32) * o, axis=0, keepdims=True)
            st[i, me, at + 3 : at + 4] = jnp.zeros((1, PAIR), F32)
        spot = st.at[i, me]
        for slot, there in enumerate((beside(core), beside(1 - core), sibling)):
            go(remote(spot, spot, st_send.at[i, slot], st_recv.at[i, me], there))

    for i in (0, 1):
        for g in (0, 1):
            mx[i, g] = jnp.broadcast_to(jnp.max(mx[i, g], axis=0, keepdims=True), (8, PAIR))
    lax.fori_loop(0, CHIPS // PER, weights_arriving, 0)
    from_sibling(1)
    turn_grads(1 - own)
    statistics(xp)
    lax.fori_loop(0, TILES, weights_beside, 0)
    statistics(1 - xp)

    ones = jnp.ones((TILE, WIDTH), BF16)
    sub = lax.broadcasted_iota(jnp.int32, (WIDTH, PAIR), 0)

    def prepare(i):
        for other in (2 * (1 - xp), 2 * (1 - xp) + 1, 2 * xp + 1 - core):
            spot = st.at[i, other]
            remote(spot, spot, st_send.at[i, 0], st_recv.at[i, other], sibling).wait_recv()
        for g in (0, 1):
            at = 4 * g
            tops = [st[i, s, at : at + 1] for s in range(DEVS)]
            top = jnp.maximum(jnp.maximum(tops[0], tops[1]), jnp.maximum(tops[2], tops[3]))
            total = delta = jnp.zeros((1, PAIR), F32)
            for s in range(DEVS):
                by = jnp.exp2(tops[s] - top)
                total = total + by * st[i, s, at + 1 : at + 2]
                delta = delta + by * st[i, s, at + 2 : at + 3]
            inv = 1.0 / total
            factor = jnp.exp2(st[i, me, at : at + 1] - top) * inv
            delta = -delta * inv * factor
            for r in (0, 1):
                o_t[i, g, r] = o_t[i, g, r] * factor[:, r * ROWS : (r + 1) * ROWS]
            grad = (gt[g, i].astype(F32) * factor).astype(BF16)
            gpa[i, g, :WIDTH] = grad
            gp[i, g] = grad.T
            d1 = delta.astype(BF16).astype(F32)
            d2 = (delta - d1).astype(BF16).astype(F32)
            extra = jnp.where(sub == 0, d1, jnp.where(sub == 1, d2, jnp.where(sub == 2, delta - d1 - d2, 0.0)))
            gpa[i, g, WIDTH:] = extra.astype(BF16)

    parts_of = (o_t, dq_t)

    def to_core(kind, i, g):
        go(
            remote(
                parts_of[kind].at[i, g, 1 - core], core_x.at[kind, i, g],
                core_send.at[kind, i, g], core_recv.at[kind, i, g], sibling,
            )
        )

    def from_core(kind, i, g):
        spot = core_x.at[kind, i, g]
        remote(spot, spot, core_send.at[kind, i, g], core_recv.at[kind, i, g], sibling).wait_recv()
        return parts_of[kind][i, g, core] + core_x[kind, i, g]

    def to_beside(kind, g):
        xs[kind, g] = from_core(kind, 1 - xp, g).astype(BF16)
        go(remote(xs.at[kind, g], xr.at[kind, g], sum_send.at[kind, g], sum_recv.at[kind, g], beside(core)))

    def finish(kind, g):
        total = from_core(kind, xp, g)
        spot = xr.at[kind, g]
        remote(spot, spot, sum_send.at[kind, g], sum_recv.at[kind, g], sibling).wait_recv()
        total = total + xr[kind, g].astype(F32)
        if kind == 1:
            total = total * scale
        obuf[kind, g] = total.T.astype(BF16)

    def finish_own(kind):
        finish(kind, own)
        (out_ref, dq_ref)[kind][:, cols(upper)] = obuf[kind, own]

    def partner_copy(kind):
        return remote(obuf.at[kind, 1 - own], orecv.at[kind], out_send.at[kind], out_recv.at[kind], partner)

    def finish_other(kind):
        finish(kind, 1 - own)
        go(partner_copy(kind))

    def from_partner(kind):
        partner_copy(kind).wait_recv()
        (out_ref, dq_ref)[kind][:, cols(1 - upper)] = orecv[kind]

    def touched(k, j):
        return j // PER <= upper_of(k) // PER

    def first_copy(which, j):
        axis = "yz"[which]
        d = (j % N + N - y) % N if which == 0 else (j // N + N - z) % N
        index = j // N if which == 0 else j % N
        slot = jnp.maximum(d - 1, 0)
        copy = remote(
            part.at[which, j], r1.at[which, slot, index], r1_send.at[which, j], r1_recv.at[which, slot, index],
            along(axis, d),
        )
        return copy, d != 0

    def each_first(j, act):
        for which in (0, 1):
            copy, needed = first_copy(which, j)
            pl.when(needed)(lambda copy=copy: act(copy))

    def send_grads(b):
        for j in [PER * b + k for k in range(PER)]:
            part[0, j] = (dkv[0, j] * scale).astype(BF16)
            part[1, j] = dkv[1, j].astype(BF16)
            each_first(j, lambda copy: copy.start())

    def grads_step(g, i, b):
        e = e_buf[i, b + g * n_hi]
        k = tile_of(kall, b)
        dp = dot(jnp.concatenate([tile_of(vall, b), ones], axis=1), gpa[i, g])
        ds = (e.astype(F32) * dp).astype(BF16)
        at = pl.ds(PER * b, PER)
        dkv[0, at] = dkv[0, at] + dot(ds, qbuf[g, i].reshape(PAIR, WIDTH)).reshape(PER, GROUP, WIDTH)
        dkv[1, at] = dkv[1, at] + dot(e, gp[i, g]).reshape(PER, GROUP, WIDTH)
        dq = dot(k.T, ds)
        for r in (0, 1):
            dq_t[i, g, r] = dq_t[i, g, r] + dq[:, r * ROWS : (r + 1) * ROWS]

    def grads_pass(i, leave):
        def lower(b, carry):
            grads_step(1, i, b)
            return carry

        def upper_tile(n, carry):
            b = (z + 1 + n) % N

            @pl.when(b < n_hi)
            def _():
                grads_step(0, i, b)
                if leave:
                    send_grads(b)

            return carry

        lax.fori_loop(0, n_lo, lower, 0)
        if leave:
            for g in (0, 1):
                to_beside(1, g)
        lax.fori_loop(0, N, upper_tile, 0)
        for g in (0, 1):
            to_core(1, i, g)

    prepare(1 - xp)
    for g in (0, 1):
        to_core(0, 1 - xp, g)
    grads_pass(1 - xp, False)
    prepare(xp)
    for g in (0, 1):
        to_core(0, xp, g)
    for g in (0, 1):
        to_beside(0, g)
    grads_pass(xp, True)

    def second_copy(which, i):
        d = (i + N - (z if which == 0 else y)) % N
        slot = jnp.maximum(d - 1, 0)
        copy = remote(
            d2.at[which, i], r2.at[which, slot], r2_send.at[which, i], r2_recv.at[which, slot],
            along("zy"[which], d),
        )
        return copy, d != 0

    def first_sum(i, carry):
        for which in (0, 1):
            j = N * i + y if which == 0 else N * z + i
            acc[...] = jnp.where(touched(chip, j), part[which, j].astype(F32), 0.0)
            for s in range(N - 1):
                k = chip_at(s + 1, 0) if which == 0 else chip_at(0, s + 1)

                @pl.when(touched(k, j))
                def _(s=s):
                    spot = r1.at[which, s, i]
                    remote(spot, spot, r1_send.at[which, 0], r1_recv.at[which, s, i], sibling).wait_recv()
                    acc[...] = acc[...] + r1[which, s, i].astype(F32)

            d2[which, i] = acc[...].astype(BF16)
            copy, needed = second_copy(which, i)
            pl.when(needed)(lambda copy=copy: copy.start())
        return carry

    lax.fori_loop(0, N, first_sum, 0)
    finish_other(1)
    finish_other(0)
    for which, i in ((0, z), (1, y)):
        total = d2[which, i].astype(F32)
        for s in range(N - 1):
            spot = r2.at[which, s]
            remote(spot, spot, r2_send.at[which, 0], r2_recv.at[which, s], sibling).wait_recv()
            total = total + r2[which, s].astype(F32)
        total = total.astype(BF16)
        for half in (0, 1):
            d3[half, which] = total[half * HOME : (half + 1) * HOME]

    def third_copy(half):
        there = home(half)
        copy = remote(d3.at[half], r3.at[p // 2], r3_send.at[half], r3_recv.at[p // 2], there)
        return copy, jnp.logical_not(is_me(there))

    for half in (0, 1):
        copy, needed = third_copy(half)
        pl.when(needed)(lambda copy=copy: copy.start())
    finish_own(1)
    finish_own(0)
    total = jnp.where(keeps, d3[core].astype(F32), 0.0)
    sums[...] = total
    for u in (0, 1):

        @pl.when(jnp.logical_not(is_me(source(u))))
        def _(u=u):
            spot = r3.at[u]
            remote(spot, spot, r3_send.at[0], r3_recv.at[u], sibling).wait_recv()
            sums[...] = sums[...] + r3[u].astype(F32)

    for which, ref in enumerate((dk_ref, dv_ref)):
        ref[...] = sums[which].astype(BF16)
    from_partner(0)
    from_partner(1)

    def sent(j, carry):
        @pl.when(j // PER < n_hi)
        def _():
            each_first(j, lambda copy: copy.wait_send())

        return carry

    lax.fori_loop(0, CHIPS, sent, 0)
    for which in (0, 1):
        for i in range(N):
            copy, needed = second_copy(which, i)
            pl.when(needed)(lambda copy=copy: copy.wait_send())
    for half in (0, 1):
        copy, needed = third_copy(half)
        pl.when(needed)(lambda copy=copy: copy.wait_send())
    for copy in started:
        copy.wait_send()


def hand_on(*refs):
    for i in range(4):
        refs[4 + i][...] = refs[i][...]


def on_device(queries, keys, values, out_grad, segment_ids):
    hbm = pl.BlockSpec(memory_space=pl.ANY)
    dma = pltpu.SemaphoreType.DMA
    vmem = pltpu.VMEM
    scratch = [
        vmem((SEQ // WIDTH, WIDTH), jnp.int32),
        vmem((CHIPS, 2, HOME, WIDTH), BF16),
        vmem((CHIPS, 2, HOME, WIDTH), BF16),
        vmem((2, HEADS, 2, ROWS, WIDTH), BF16),
        vmem((2, HEADS, 2, ROWS, WIDTH), BF16),
        vmem((HEADS, TILES, TILE, PAIR), F32),
        vmem((HEADS, TILES, TILE, PAIR), BF16),
        vmem((2, HEADS, 2 * WIDTH, PAIR), BF16),
        vmem((2, HEADS, WIDTH, PAIR), BF16),
        vmem((HEADS, 2, 2 * WIDTH, PAIR), BF16),
        vmem((HEADS, 2, PAIR, WIDTH), BF16),
        vmem((HEADS, 2, 8, PAIR), F32),
        vmem((HEADS, 2, 8, PAIR), F32),
        vmem((HEADS, 2, 2, WIDTH, ROWS), F32),
        vmem((HEADS, 2, 2, WIDTH, ROWS), F32),
        vmem((2, HEADS, 2, WIDTH, ROWS), F32),
        vmem((2, 2, WIDTH, ROWS), BF16),
        vmem((2, 2, WIDTH, ROWS), BF16),
        vmem((HEADS, DEVS, 8, PAIR), F32),
        vmem((2, 2, 1, PAIR), jnp.int32),
        vmem((2, CHIPS, GROUP, WIDTH), F32),
        vmem((2, CHIPS, GROUP, WIDTH), BF16),
        vmem((2, N - 1, N, GROUP, WIDTH), BF16),
        vmem((2, N, GROUP, WIDTH), BF16),
        vmem((2, N - 1, GROUP, WIDTH), BF16),
        vmem((2, 2, HOME, WIDTH), BF16),
        vmem((2, 2, HOME, WIDTH), BF16),
        vmem((GROUP, WIDTH), F32),
        vmem((2, HOME, WIDTH), F32),
        vmem((2, 2, ROWS, WIDTH), BF16),
        vmem((2, ROWS, WIDTH), BF16),
        dma((2, HEADS)),
        dma((3,)),
        dma((2, 32)), dma((2, CHIPS, 2)),
        dma((2,)), dma((2,)),
        dma((2,)), dma((2,)),
        dma((2,)), dma((2,)),
        dma((2, HEADS)), dma((2, HEADS)),
        dma((HEADS, 3)), dma((HEADS, DEVS)),
        dma((2, HEADS, 2)), dma((2, HEADS, 2)),
        dma((2, 2)), dma((2, 2)),
        dma((2,)), dma((2,)),
        dma((2, CHIPS)), dma((2, N - 1, N)),
        dma((2, N)), dma((2, N - 1)),
        dma((2,)), dma((2,)),
    ]
    tokens = jax.ShapeDtypeStruct((ROWS, 2 * WIDTH), BF16)
    terms = jax.ShapeDtypeStruct((HOME, WIDTH), BF16)
    results = (tokens, tokens, terms, terms)
    parts = pl.pallas_call(
        kernel,
        out_shape=[vmem(like.shape, like.dtype) for like in results],
        in_specs=[hbm] * 5,
        out_specs=[pl.BlockSpec(memory_space=vmem)] * 4,
        scratch_shapes=scratch,
        compiler_params=pltpu.CompilerParams(
            collective_id=0, has_side_effects=True, vmem_limit_bytes=56 * 1024 * 1024
        ),
    )(
        segment_ids.reshape(SEQ // WIDTH, WIDTH),
        queries,
        keys.reshape(2, 2, HOME, WIDTH),
        values.reshape(2, 2, HOME, WIDTH),
        out_grad,
    )
    return pl.pallas_call(
        hand_on,
        out_shape=results,
        in_specs=[pl.BlockSpec(memory_space=vmem)] * 4,
        out_specs=(pl.BlockSpec(memory_space=vmem),) * 4,
    )(*[pltpu.with_memory_space_constraint(part, vmem) for part in parts])


def solution(mesh):
    return jax.shard_map(
        on_device,
        mesh=mesh,
        in_specs=(P("ctx", None), P("ctx", None), P("ctx", None), P("ctx", None), P()),
        out_specs=(P("ctx", "dp"), P("ctx", "dp"), P(("dp", "ctx"), None), P(("dp", "ctx"), None)),
        check_vma=False,
    )
```

```python
import math

import jax
import jax.numpy as jnp
from jax import lax
from jax.experimental import pallas as pl
from jax.experimental.pallas import tpu as pltpu
from jax.sharding import PartitionSpec as P

F32 = jnp.float32
BF16 = jnp.bfloat16
MESH = pl.DeviceIdType.MESH

N = 4
CHIPS = N * N
ROWS = 256
PAIR = 2 * ROWS
WIDTH = 128
SEQ = PAIR * CHIPS
GROUP = 128
HOME = 64
PER = 4
TILE = PER * GROUP
TILES = 5
HEADS = 2
DEVS = 4
NEG = -1e30


def dot(a, b):
    return lax.dot_general(a, b, (((1,), (0,)), ((), ())), preferred_element_type=F32)


def kernel(
    seg_hbm, q_hbm, k_hbm, v_hbm, g_hbm,
    out_ref, dq_ref, dk_ref, dv_ref,
    seg_ref, kall, vall, qbuf, gbuf, s_buf, e_buf,
    qa, gt, gpa, gp, mx, tot, o_t, dq_t, core_x, xs, xr, st, rng, dkv,
    part, r1, d2, r2, d3, r3, acc, sums, obuf, orecv,
    load_sem, kv_sem, ag_send, ag_recv, pair_send, pair_recv, own_send, own_recv, x_send, x_recv, rel_send, rel_recv,
    st_send, st_recv, core_send, core_recv, sum_send, sum_recv, out_send, out_recv, r1_send, r1_recv, r2_send, r2_recv, r3_send, r3_recv,
):
    p = lax.axis_index("dp")
    c = lax.axis_index("ctx")
    core = c % 2
    chip = c // 2
    z = chip % N
    y = chip // N
    xp = p % 2
    me = 2 * xp + core
    neighbour = p + 1 - 2 * xp
    sibling = (p, 2 * chip + 1 - core)
    partner = (p, 2 * (CHIPS - 1 - chip) + core)
    upper = (chip >= CHIPS // 2).astype(jnp.int32)
    own = 1 - upper
    lo = jnp.minimum(chip, CHIPS - 1 - chip)
    hi = CHIPS - 1 - lo
    n_hi = hi // PER + 1
    n_lo = lo // PER + 1
    n_own = jnp.where(upper == 1, n_hi, n_lo)
    n_other = TILES - n_own

    def beside(core_):
        return (neighbour, 2 * chip + core_)

    def head_of(slot, parity):
        return 2 * (p - xp + slot) + parity

    def along(axis, d):
        there = dict(y=y, z=z)
        there[axis] = (there[axis] + d) % N
        return (p, (there["y"] * N + there["z"]) * 2 + core)

    def chip_at(dy, dz):
        return ((y + N - dy) % N) * N + (z + N - dz) % N

    def upper_of(k):
        return jnp.maximum(k, CHIPS - 1 - k)

    def cols(head):
        return pl.ds(pl.multiple_of(head * WIDTH, WIDTH), WIDTH)

    home_z = 2 * core + xp

    def home(half):
        return (z, (y * N + home_z) * 2 + half)

    def source(u):
        return (z % 2 + 2 * u, (y * N + p) * 2 + z // 2)

    def is_me(dev):
        return (dev[0] == p) & (dev[1] == c)

    keeps = (z == p) & (home_z == z)

    barrier = pltpu.get_barrier_semaphore()

    def greet(there):
        pl.semaphore_signal(barrier, inc=1, device_id=there, device_id_type=MESH)

    for d in range(1, N):
        for axis in "yz":
            greet(along(axis, d))
    for there in (partner, beside(core), beside(1 - core), sibling):
        greet(there)
    for u in (0, 1):
        pl.when(jnp.logical_not(is_me(source(u))))(lambda u=u: greet(source(u)))

    kv_loads = [
        pltpu.make_async_copy(src.at[xp], dst.at[chip], kv_sem.at[i])
        for i, (src, dst) in enumerate(((k_hbm, kall), (v_hbm, vall)))
    ]
    arrays = ((q_hbm, qbuf), (g_hbm, gbuf))
    loads = [
        pltpu.make_async_copy(src.at[:, cols(head_of(i, upper))], buf.at[own, i, core], load_sem.at[a, i])
        for a, (src, buf) in enumerate(arrays)
        for i in range(HEADS)
    ]
    seg_load = pltpu.make_async_copy(seg_hbm, seg_ref, kv_sem.at[2])
    for copy in kv_loads + loads + [seg_load]:
        copy.start()
    started = []

    def remote(src, dst, send, recv, there):
        return pltpu.make_async_remote_copy(
            src_ref=src, dst_ref=dst, send_sem=send, recv_sem=recv, device_id=there, device_id_type=MESH
        )

    def go(copy):
        copy.start()
        started.append(copy)
        return copy

    whole = (kall, vall)
    count = [0, 0]
    key_copies = []

    def push(which, block, half, there):
        spot = whole[which].at[block, half]
        copy = remote(spot, spot, ag_send.at[which, count[which]], ag_recv.at[which, block, half], there)
        count[which] += 1
        if which == 0:
            copy.start()
            key_copies.append(copy)
        else:
            go(copy)

    def arrived(which, block, half):
        spot = whole[which].at[block, half]
        remote(spot, spot, ag_send.at[which, 0], ag_recv.at[which, block, half], sibling).wait_recv()

    def push_mine(which):
        for axes in ("yz", "zy"):
            for d in (1, 3, 2):
                for half in (0, 1):
                    push(which, chip, half, along(axes[half], d))

    def relay(which):
        for d in (1, 3, 2):
            for half, block in ((0, chip_at(d, 0)), (1, chip_at(0, d))):
                arrived(which, block, half)
                for d2 in (1, 3, 2):
                    push(which, block, half, along("zy"[half], d2))

    def tile_in_order(n):
        return (y + jnp.where(n == 2, 3, jnp.where(n == 3, 2, n))) % N

    def tile_arrived(which, b):
        for i in range(PER):
            j = PER * b + i
            pl.when(z != i)(lambda j=j: arrived(which, j, 0))
            pl.when(b != y)(lambda j=j: arrived(which, j, 1))

    def pair_copy(a):
        src, buf = arrays[a]
        src = src.at[:, cols(2 * p + 1 - upper)]
        return remote(src, buf.at[own, xp, core], pair_send.at[a], pair_recv.at[a], partner)

    def share_own(a):
        spot = arrays[a][1].at[own, :, core]
        for i in range(HEADS):
            loads[HEADS * a + i].wait()
        go(remote(spot, spot, own_send.at[a], own_recv.at[a], sibling))

    def to_sibling(a, slot):
        spot = arrays[a][1].at[1 - own, slot, core]
        go(remote(spot, spot, rel_send.at[a, slot], rel_recv.at[a, slot], sibling))

    def share_pair(a):
        spot = arrays[a][1].at[1 - own, xp, core]
        remote(spot, spot, pair_send.at[a], pair_recv.at[a], partner).wait_recv()
        go(remote(spot, spot, x_send.at[a], x_recv.at[a], beside(core)))
        to_sibling(a, xp)

    def pass_on(a):
        spot = arrays[a][1].at[1 - own, 1 - xp, core]
        remote(spot, spot, x_send.at[a], x_recv.at[a], sibling).wait_recv()
        to_sibling(a, 1 - xp)

    def from_sibling(a):
        for i in range(HEADS):
            spot = arrays[a][1].at[1 - own, i, 1 - core]
            remote(spot, spot, rel_send.at[a, 0], rel_recv.at[a, i], sibling).wait_recv()

    def own_from_sibling(a):
        spot = arrays[a][1].at[own, :, 1 - core]
        remote(spot, spot, own_send.at[a], own_recv.at[a], sibling).wait_recv()

    pl.semaphore_wait(barrier, 12 - keeps.astype(jnp.int32))
    go(pair_copy(0))
    kv_loads[0].wait()
    push_mine(0)
    share_own(0)
    go(pair_copy(1))
    relay(0)
    kv_loads[1].wait()
    push_mine(1)

    scale = WIDTH**-0.5
    seg_load.wait()
    seg = seg_ref[...]
    starts = [jnp.sum((seg < doc).astype(jnp.int32), axis=(0, 1), keepdims=True) for doc in (1, 2, 3)]
    lane = lax.broadcasted_iota(jnp.int32, (1, WIDTH), 1)
    for g, block in ((0, hi), (1, lo)):
        for i in range(PAIR // WIDTH):
            ids = seg_ref[pl.ds(block * (PAIR // WIDTH) + i, 1), :]
            start = jnp.where(
                ids == 0, 0, jnp.where(ids == 1, starts[0], jnp.where(ids == 2, starts[1], starts[2]))
            )
            rng[g, 0, :, i * WIDTH : (i + 1) * WIDTH] = start
            rng[g, 1, :, i * WIDTH : (i + 1) * WIDTH] = block * PAIR + i * WIDTH + lane
    mx[...] = jnp.full_like(mx, NEG)
    tot[...] = jnp.zeros_like(tot)

    def clear(i, carry):
        for ref in (o_t, dq_t):
            ref[i] = jnp.zeros_like(ref[i])
        return carry

    lax.fori_loop(0, HEADS, clear, 0)

    def clear_block(j, carry):
        for which in (0, 1):
            dkv[which, j] = jnp.zeros((GROUP, WIDTH), F32)
        return carry

    lax.fori_loop(0, CHIPS, clear_block, 0)

    def scale_rows(g):
        def one(i, carry):
            for r in (0, 1):
                at = slice(r * ROWS, (r + 1) * ROWS)
                scaled = qbuf[g, i, r].astype(F32).T * (scale * math.log2(math.e))
                high = scaled.astype(BF16)
                qa[g, i, :WIDTH, at] = high
                qa[g, i, WIDTH:, at] = (scaled - high.astype(F32)).astype(BF16)
            return carry

        lax.fori_loop(0, HEADS, one, 0)

    def turn_grads(g):
        def one(i, carry):
            for r in (0, 1):
                gt[g, i, :, r * ROWS : (r + 1) * ROWS] = gbuf[g, i, r].T
            return carry

        lax.fori_loop(0, HEADS, one, 0)

    row = lax.broadcasted_iota(jnp.int32, (TILE, PAIR), 0)
    token = PAIR * (row // GROUP) + row % GROUP + ROWS * core + GROUP * xp

    def tile_of(ref, b):
        return ref[pl.ds(PER * b, PER)].reshape(TILE, WIDTH)

    def fold(op, values):
        return op(values.reshape(TILE // 8, 8, PAIR), axis=0)

    def scores_step(g, b):
        k = tile_of(kall, b)
        k = jnp.concatenate([k, k], axis=1)
        key = token + b * (PER * PAIR)
        seen = (key >= rng[g, 0]) & (key <= rng[g, 1])

        def one(i, carry):
            s = jnp.where(seen, dot(k, qa[g, i]), NEG)
            s_buf[i, b + g * n_hi] = s
            mx[i, g] = jnp.maximum(mx[i, g], fold(jnp.max, s))
            return carry

        lax.fori_loop(0, HEADS, one, 0)

    share_pair(0)
    own_from_sibling(0)
    scale_rows(own)

    def scores_own(n, carry):
        b = tile_in_order(n)
        tile_arrived(0, b)

        @pl.when(b < n_own)
        def _():
            scores_step(own, b)

        return carry

    lax.fori_loop(0, 1, scores_own, 0)
    for copy in key_copies:
        copy.wait_send()
    share_own(1)
    share_pair(1)
    pass_on(0)
    relay(1)
    lax.fori_loop(1, CHIPS // PER, scores_own, 0)
    own_from_sibling(1)
    turn_grads(own)
    from_sibling(0)
    scale_rows(1 - own)

    def scores_other(b, carry):
        scores_step(1 - own, b)
        return carry

    lax.fori_loop(0, n_other, scores_other, 0)
    pass_on(1)

    def tile_place(t):
        g = (t >= n_hi).astype(jnp.int32)
        return g, t - g * n_hi

    def weights_step(i, g, b):
        t = b + g * n_hi
        e = jnp.exp2(s_buf[i, t] - mx[i, g, 0:1])
        tot[i, g] = tot[i, g] + fold(jnp.sum, e)
        e = e.astype(BF16)
        e_buf[i, t] = e
        o = dot(tile_of(vall, b).T, e)
        for r in (0, 1):
            o_t[i, g, r] = o_t[i, g, r] + o[:, r * ROWS : (r + 1) * ROWS]

    def weights_arriving(n, carry):
        b = tile_in_order(n)
        tile_arrived(1, b)
        pl.when(b < n_hi)(lambda: weights_step(xp, 0, b))
        pl.when(b < n_lo)(lambda: weights_step(xp, 1, b))
        return carry

    def weights_beside(n, carry):
        weights_step(1 - xp, *tile_place(n))
        return carry

    def statistics(i):
        for g in (0, 1):
            at = 4 * g
            st[i, me, at : at + 1] = mx[i, g, 0:1]
            st[i, me, at + 1 : at + 2] = jnp.sum(tot[i, g], axis=0, keepdims=True)
            o = jnp.concatenate([o_t[i, g, 0], o_t[i, g, 1]], axis=1)
            st[i, me, at + 2 : at + 3] = jnp.sum(gt[g, i].astype(F32) * o, axis=0, keepdims=True)
            st[i, me, at + 3 : at + 4] = jnp.zeros((1, PAIR), F32)
        spot = st.at[i, me]
        for slot, there in enumerate((beside(core), beside(1 - core), sibling)):
            go(remote(spot, spot, st_send.at[i, slot], st_recv.at[i, me], there))

    for i in (0, 1):
        for g in (0, 1):
            mx[i, g] = jnp.broadcast_to(jnp.max(mx[i, g], axis=0, keepdims=True), (8, PAIR))
    lax.fori_loop(0, CHIPS // PER, weights_arriving, 0)
    from_sibling(1)
    turn_grads(1 - own)
    statistics(xp)
    lax.fori_loop(0, TILES, weights_beside, 0)
    statistics(1 - xp)

    ones = jnp.ones((TILE, WIDTH), BF16)
    sub = lax.broadcasted_iota(jnp.int32, (WIDTH, PAIR), 0)

    def prepare(i):
        for other in (2 * (1 - xp), 2 * (1 - xp) + 1, 2 * xp + 1 - core):
            spot = st.at[i, other]
            remote(spot, spot, st_send.at[i, 0], st_recv.at[i, other], sibling).wait_recv()
        for g in (0, 1):
            at = 4 * g
            tops = [st[i, s, at : at + 1] for s in range(DEVS)]
            top = jnp.maximum(jnp.maximum(tops[0], tops[1]), jnp.maximum(tops[2], tops[3]))
            total = delta = jnp.zeros((1, PAIR), F32)
            for s in range(DEVS):
                by = jnp.exp2(tops[s] - top)
                total = total + by * st[i, s, at + 1 : at + 2]
                delta = delta + by * st[i, s, at + 2 : at + 3]
            inv = 1.0 / total
            factor = jnp.exp2(st[i, me, at : at + 1] - top) * inv
            delta = -delta * inv * factor
            for r in (0, 1):
                o_t[i, g, r] = o_t[i, g, r] * factor[:, r * ROWS : (r + 1) * ROWS]
            grad = (gt[g, i].astype(F32) * factor).astype(BF16)
            gpa[i, g, :WIDTH] = grad
            gp[i, g] = grad.T
            d1 = delta.astype(BF16).astype(F32)
            d2 = (delta - d1).astype(BF16).astype(F32)
            extra = jnp.where(sub == 0, d1, jnp.where(sub == 1, d2, jnp.where(sub == 2, delta - d1 - d2, 0.0)))
            gpa[i, g, WIDTH:] = extra.astype(BF16)

    parts_of = (o_t, dq_t)

    def to_core(kind, i, g):
        go(
            remote(
                parts_of[kind].at[i, g, 1 - core], core_x.at[kind, i, g],
                core_send.at[kind, i, g], core_recv.at[kind, i, g], sibling,
            )
        )

    def from_core(kind, i, g):
        spot = core_x.at[kind, i, g]
        remote(spot, spot, core_send.at[kind, i, g], core_recv.at[kind, i, g], sibling).wait_recv()
        return parts_of[kind][i, g, core] + core_x[kind, i, g]

    def to_beside(kind, g):
        xs[kind, g] = from_core(kind, 1 - xp, g).astype(BF16)
        go(remote(xs.at[kind, g], xr.at[kind, g], sum_send.at[kind, g], sum_recv.at[kind, g], beside(core)))

    def finish(kind, g):
        total = from_core(kind, xp, g)
        spot = xr.at[kind, g]
        remote(spot, spot, sum_send.at[kind, g], sum_recv.at[kind, g], sibling).wait_recv()
        total = total + xr[kind, g].astype(F32)
        if kind == 1:
            total = total * scale
        obuf[kind, g] = total.T.astype(BF16)

    def finish_own(kind):
        finish(kind, own)
        (out_ref, dq_ref)[kind][:, cols(upper)] = obuf[kind, own]

    def partner_copy(kind):
        return remote(obuf.at[kind, 1 - own], orecv.at[kind], out_send.at[kind], out_recv.at[kind], partner)

    def finish_other(kind):
        finish(kind, 1 - own)
        go(partner_copy(kind))

    def from_partner(kind):
        partner_copy(kind).wait_recv()
        (out_ref, dq_ref)[kind][:, cols(1 - upper)] = orecv[kind]

    def touched(k, j):
        return j // PER <= upper_of(k) // PER

    def first_copy(which, j):
        axis = "yz"[which]
        d = (j % N + N - y) % N if which == 0 else (j // N + N - z) % N
        index = j // N if which == 0 else j % N
        slot = jnp.maximum(d - 1, 0)
        copy = remote(
            part.at[which, j], r1.at[which, slot, index], r1_send.at[which, j], r1_recv.at[which, slot, index],
            along(axis, d),
        )
        return copy, d != 0

    def each_first(j, act):
        for which in (0, 1):
            copy, needed = first_copy(which, j)
            pl.when(needed)(lambda copy=copy: act(copy))

    def send_grads(b):
        for j in [PER * b + k for k in range(PER)]:
            part[0, j] = (dkv[0, j] * scale).astype(BF16)
            part[1, j] = dkv[1, j].astype(BF16)
            each_first(j, lambda copy: copy.start())

    def grads_step(g, i, b):
        e = e_buf[i, b + g * n_hi]
        k = tile_of(kall, b)
        dp = dot(jnp.concatenate([tile_of(vall, b), ones], axis=1), gpa[i, g])
        ds = (e.astype(F32) * dp).astype(BF16)
        at = pl.ds(PER * b, PER)
        dkv[0, at] = dkv[0, at] + dot(ds, qbuf[g, i].reshape(PAIR, WIDTH)).reshape(PER, GROUP, WIDTH)
        dkv[1, at] = dkv[1, at] + dot(e, gp[i, g]).reshape(PER, GROUP, WIDTH)
        dq = dot(k.T, ds)
        for r in (0, 1):
            dq_t[i, g, r] = dq_t[i, g, r] + dq[:, r * ROWS : (r + 1) * ROWS]

    def grads_pass(i, leave):
        def lower(b, carry):
            grads_step(1, i, b)
            return carry

        def upper_tile(n, carry):
            b = (z + 1 + n) % N

            @pl.when(b < n_hi)
            def _():
                grads_step(0, i, b)
                if leave:
                    send_grads(b)

            return carry

        lax.fori_loop(0, n_lo, lower, 0)
        to_core(1, i, 1)
        if leave:
            for g in (0, 1):
                to_beside(1, g)
        lax.fori_loop(0, N, upper_tile, 0)
        to_core(1, i, 0)

    prepare(1 - xp)
    for g in (0, 1):
        to_core(0, 1 - xp, g)
    grads_pass(1 - xp, False)
    prepare(xp)
    for g in (0, 1):
        to_core(0, xp, g)
    for g in (0, 1):
        to_beside(0, g)
    grads_pass(xp, True)

    def second_copy(which, i):
        d = (i + N - (z if which == 0 else y)) % N
        slot = jnp.maximum(d - 1, 0)
        copy = remote(
            d2.at[which, i], r2.at[which, slot], r2_send.at[which, i], r2_recv.at[which, slot],
            along("zy"[which], d),
        )
        return copy, d != 0

    def first_sum(i, carry):
        for which in (0, 1):
            j = N * i + y if which == 0 else N * z + i
            acc[...] = jnp.where(touched(chip, j), part[which, j].astype(F32), 0.0)
            for s in range(N - 1):
                k = chip_at(s + 1, 0) if which == 0 else chip_at(0, s + 1)

                @pl.when(touched(k, j))
                def _(s=s):
                    spot = r1.at[which, s, i]
                    remote(spot, spot, r1_send.at[which, 0], r1_recv.at[which, s, i], sibling).wait_recv()
                    acc[...] = acc[...] + r1[which, s, i].astype(F32)

            d2[which, i] = acc[...].astype(BF16)
            copy, needed = second_copy(which, i)
            pl.when(needed)(lambda copy=copy: copy.start())
        return carry

    lax.fori_loop(0, N, first_sum, 0)
    finish_other(1)
    finish_other(0)
    for which, i in ((0, z), (1, y)):
        total = d2[which, i].astype(F32)
        for s in range(N - 1):
            spot = r2.at[which, s]
            remote(spot, spot, r2_send.at[which, 0], r2_recv.at[which, s], sibling).wait_recv()
            total = total + r2[which, s].astype(F32)
        total = total.astype(BF16)
        for half in (0, 1):
            d3[half, which] = total[half * HOME : (half + 1) * HOME]

    def third_copy(half):
        there = home(half)
        copy = remote(d3.at[half], r3.at[p // 2], r3_send.at[half], r3_recv.at[p // 2], there)
        return copy, jnp.logical_not(is_me(there))

    for half in (0, 1):
        copy, needed = third_copy(half)
        pl.when(needed)(lambda copy=copy: copy.start())
    finish_own(1)
    finish_own(0)
    total = jnp.where(keeps, d3[core].astype(F32), 0.0)
    sums[...] = total
    for u in (0, 1):

        @pl.when(jnp.logical_not(is_me(source(u))))
        def _(u=u):
            spot = r3.at[u]
            remote(spot, spot, r3_send.at[0], r3_recv.at[u], sibling).wait_recv()
            sums[...] = sums[...] + r3[u].astype(F32)

    for which, ref in enumerate((dk_ref, dv_ref)):
        ref[...] = sums[which].astype(BF16)
    from_partner(0)
    from_partner(1)

    def sent(j, carry):
        @pl.when(j // PER < n_hi)
        def _():
            each_first(j, lambda copy: copy.wait_send())

        return carry

    lax.fori_loop(0, CHIPS, sent, 0)
    for which in (0, 1):
        for i in range(N):
            copy, needed = second_copy(which, i)
            pl.when(needed)(lambda copy=copy: copy.wait_send())
    for half in (0, 1):
        copy, needed = third_copy(half)
        pl.when(needed)(lambda copy=copy: copy.wait_send())
    for copy in started:
        copy.wait_send()


def hand_on(*refs):
    for i in range(4):
        refs[4 + i][...] = refs[i][...]


def on_device(queries, keys, values, out_grad, segment_ids):
    hbm = pl.BlockSpec(memory_space=pl.ANY)
    dma = pltpu.SemaphoreType.DMA
    vmem = pltpu.VMEM
    scratch = [
        vmem((SEQ // WIDTH, WIDTH), jnp.int32),
        vmem((CHIPS, 2, HOME, WIDTH), BF16),
        vmem((CHIPS, 2, HOME, WIDTH), BF16),
        vmem((2, HEADS, 2, ROWS, WIDTH), BF16),
        vmem((2, HEADS, 2, ROWS, WIDTH), BF16),
        vmem((HEADS, TILES, TILE, PAIR), F32),
        vmem((HEADS, TILES, TILE, PAIR), BF16),
        vmem((2, HEADS, 2 * WIDTH, PAIR), BF16),
        vmem((2, HEADS, WIDTH, PAIR), BF16),
        vmem((HEADS, 2, 2 * WIDTH, PAIR), BF16),
        vmem((HEADS, 2, PAIR, WIDTH), BF16),
        vmem((HEADS, 2, 8, PAIR), F32),
        vmem((HEADS, 2, 8, PAIR), F32),
        vmem((HEADS, 2, 2, WIDTH, ROWS), F32),
        vmem((HEADS, 2, 2, WIDTH, ROWS), F32),
        vmem((2, HEADS, 2, WIDTH, ROWS), F32),
        vmem((2, 2, WIDTH, ROWS), BF16),
        vmem((2, 2, WIDTH, ROWS), BF16),
        vmem((HEADS, DEVS, 8, PAIR), F32),
        vmem((2, 2, 1, PAIR), jnp.int32),
        vmem((2, CHIPS, GROUP, WIDTH), F32),
        vmem((2, CHIPS, GROUP, WIDTH), BF16),
        vmem((2, N - 1, N, GROUP, WIDTH), BF16),
        vmem((2, N, GROUP, WIDTH), BF16),
        vmem((2, N - 1, GROUP, WIDTH), BF16),
        vmem((2, 2, HOME, WIDTH), BF16),
        vmem((2, 2, HOME, WIDTH), BF16),
        vmem((GROUP, WIDTH), F32),
        vmem((2, HOME, WIDTH), F32),
        vmem((2, 2, ROWS, WIDTH), BF16),
        vmem((2, ROWS, WIDTH), BF16),
        dma((2, HEADS)),
        dma((3,)),
        dma((2, 32)), dma((2, CHIPS, 2)),
        dma((2,)), dma((2,)),
        dma((2,)), dma((2,)),
        dma((2,)), dma((2,)),
        dma((2, HEADS)), dma((2, HEADS)),
        dma((HEADS, 3)), dma((HEADS, DEVS)),
        dma((2, HEADS, 2)), dma((2, HEADS, 2)),
        dma((2, 2)), dma((2, 2)),
        dma((2,)), dma((2,)),
        dma((2, CHIPS)), dma((2, N - 1, N)),
        dma((2, N)), dma((2, N - 1)),
        dma((2,)), dma((2,)),
    ]
    tokens = jax.ShapeDtypeStruct((ROWS, 2 * WIDTH), BF16)
    terms = jax.ShapeDtypeStruct((HOME, WIDTH), BF16)
    results = (tokens, tokens, terms, terms)
    parts = pl.pallas_call(
        kernel,
        out_shape=[vmem(like.shape, like.dtype) for like in results],
        in_specs=[hbm] * 5,
        out_specs=[pl.BlockSpec(memory_space=vmem)] * 4,
        scratch_shapes=scratch,
        compiler_params=pltpu.CompilerParams(
            collective_id=0, has_side_effects=True, vmem_limit_bytes=56 * 1024 * 1024
        ),
    )(
        segment_ids.reshape(SEQ // WIDTH, WIDTH),
        queries,
        keys.reshape(2, 2, HOME, WIDTH),
        values.reshape(2, 2, HOME, WIDTH),
        out_grad,
    )
    return pl.pallas_call(
        hand_on,
        out_shape=results,
        in_specs=[pl.BlockSpec(memory_space=vmem)] * 4,
        out_specs=(pl.BlockSpec(memory_space=vmem),) * 4,
    )(*[pltpu.with_memory_space_constraint(part, vmem) for part in parts])


def solution(mesh):
    return jax.shard_map(
        on_device,
        mesh=mesh,
        in_specs=(P("ctx", None), P("ctx", None), P("ctx", None), P("ctx", None), P()),
        out_specs=(P("ctx", "dp"), P("ctx", "dp"), P(("dp", "ctx"), None), P(("dp", "ctx"), None)),
        check_vma=False,
    )
```
